128 devices in a mesh: enc: 4 (over y), clu: 32 (over x, z, core).
Axes of the slice: x: 4, y: 4, z: 4, core: 2. Of those that a mesh axis runs over, the one named last changes fastest.
Arguments:
- states: bfloat16 [1024, 32, 1024], P(('enc', 'clu')), may hold values from -6 to 6
- lengths: int32 [1024], P(('enc', 'clu')), may hold values from 8 to 32
- w_in: bfloat16 [1024, 2048], P('clu'), may hold values from -0.1875 to 0.1875
- w_out: bfloat16 [2048, 1024], P('clu'), may hold values from -0.125 to 0.125
- norm_gain: float32 [1024], replicated, may hold values from 0.5 to 1.5
- label_tiles: float32 [8192, 1024], P('clu'), may hold values from -0.6 to 0.6
- tile_mean: float32 [8192, 1024], P('clu'), may hold values from -0.06 to 0.06
- tile_var: float32 [8192, 1024], P('clu'), may hold values from 1e-05 to 0.001
- shortlist: int32 [1024, 400], P('enc'), may hold values from 0 to 2047, as said below
- positives: int32 [1024, 4], P('enc'), may hold values from 0 to 8191, as said below
- owner_map: int32 [2048], replicated, may hold values from 0 to 2047, each once
Outputs:
- loss: float32 [1024], P(('enc', 'clu'))
- new_tiles: float32 [8192, 1024], P('clu')
- new_mean: float32 [8192, 1024], P('clu')
- new_var: float32 [8192, 1024], P('clu')
- grad_in: float32 [1024, 2048], P('clu')
- grad_out: float32 [2048, 1024], P('clu')
The draws below stay inside these ranges and needn't reach their ends.
Inputs may be any that keep to these rules, and one draw needn't show every extreme that they name: `shortlist`: each row names 400 different clusters; some clusters are named by many more rows than others. `positives`: each row names 4 different labels, each in a cluster named in the same row of shortlist.
All inputs are finite; a program needn't handle non-finite values.
Results may differ from the reference program's by a relative error of at most 0.0045.
Values may be sent and summed in bfloat16 or wider, within the bound.
No kernel may reach another device: no remote copies, remote signals or barrier semaphores. Data moves between devices by JAX's collectives and lax.ppermute only.
A program may use at most 128 MiB of HBM per device.

```python
import math
import jax
import jax.numpy as jnp
from jax import lax

D = 1024
FF = 2048
LEN = 32
DOC_DEV = 8
LPC = 4
SHORT = 400
POS = 4
DOCS = 1024
CATEGORY_GROUPS = 2048
LABELS = 8192
N_ENC = 4
N_CLU = 32


def pick_lists(key):
    key_hot, noise_key, key_slot, key_offset = jax.random.split(key, 4)
    frequent_categories = jax.random.randint(key_hot, (CATEGORY_GROUPS,), 0, 4096)
    logit_increment = frequent_categories * frequent_categories // 256
    gumbel_perturbation = jax.random.randint(noise_key, (DOCS, CATEGORY_GROUPS), 0, 65536)
    category_order = (gumbel_perturbation + logit_increment[None, :]) * CATEGORY_GROUPS + jnp.arange(CATEGORY_GROUPS, dtype=jnp.int32)[None, :]
    unused, chosen = lax.top_k(category_order, SHORT)
    chosen = chosen.astype(jnp.int32)
    slot_rank = jax.random.randint(key_slot, (DOCS, SHORT), 0, 65536) * SHORT + jnp.arange(SHORT, dtype=jnp.int32)[None, :]
    unused_two, slot_pick = lax.top_k(slot_rank, POS)
    picked_clusters = jnp.take_along_axis(chosen, slot_pick.astype(jnp.int32), axis=1)
    shift_amounts = jax.random.randint(key_offset, (DOCS, POS), 0, LPC)
    return (chosen, (picked_clusters * LPC + shift_amounts).astype(jnp.int32))


def draw_shortlist(key, part):
    chosen, labels = pick_lists(key)
    return chosen


def draw_positives(key, part):
    chosen, labels = pick_lists(key)
    return labels


def set_ends(drawn, key, low, largest):
    shape = drawn.shape
    spot = [jax.random.randint(jax.random.fold_in(key, axis), (), 0, shape[axis]) for axis in range(len(shape))]
    drawn = drawn.at[tuple(spot)].set(low)
    longest = shape.index(max(shape))
    spot[longest] = (spot[longest] + 1) % shape[longest]
    return drawn.at[tuple(spot)].set(largest)


def levels(own_key, dims, cuts, smallest, largest):
    factor_of, own = 1.0, jax.random.fold_in(own_key, 6)
    for dim, blocks in cuts:
        heights = jnp.exp(jax.random.uniform(jax.random.fold_in(own, dim), (blocks,), jnp.float32, smallest / len(cuts), largest / len(cuts)))
        factor_of = factor_of * jnp.repeat(heights, dims[dim] // blocks).reshape([-1 if axis == dim else 1 for axis in range(len(dims))])
    return factor_of


def bell_draw(own_key, shape, width, limit, shards=(), kind=jnp.bfloat16):
    result = width * jax.random.normal(own_key, shape, jnp.float32)
    if shards:
        result = result * levels(own_key, shape, shards, -0.22, 0.18)
    return jnp.clip(result, -limit, limit).astype(kind)


def setup_inputs(seed: int = 0) -> dict:
    key_of = jax.random.split(jax.random.key(seed), 12)
    return {
        "states": bell_draw(key_of[0], (DOCS, LEN, D), 1.0, 6.0, ((0, 128),)),
        "lengths": set_ends(jax.random.randint(key_of[1], (DOCS,), LEN // 4, LEN + 1), jax.random.fold_in(key_of[1], 1), LEN // 4, LEN).astype(jnp.int32),
        "w_in": bell_draw(key_of[2], (D, FF), D ** -0.5, 0.1875, ((0, 32),)),
        "w_out": bell_draw(key_of[3], (FF, D), FF ** -0.5, 0.125, ((0, 32),)),
        "norm_gain": jnp.clip(1.0 + 0.1 * jax.random.normal(key_of[4], (D,), jnp.float32), 0.5, 1.5),
        "label_tiles": bell_draw(key_of[5], (LABELS, D), 0.1, 0.6, ((0, 32),), jnp.float32),
        "tile_mean": bell_draw(key_of[6], (LABELS, D), 0.01, 0.06, ((0, 32),), jnp.float32),
        "tile_var": jnp.clip(jnp.exp(math.log(0.001) - 4.6051703 * jax.random.uniform(key_of[7], (LABELS, D), jnp.float32) ** levels(key_of[7], (LABELS, D), ((0, 32),), -0.2, 0.2)), 9.999999747378752e-06, 0.001),
        "shortlist": draw_shortlist(jax.random.fold_in(key_of[11], 71), 0),
        "positives": draw_positives(jax.random.fold_in(key_of[11], 71), 0),
        "owner_map": jax.random.permutation(key_of[10], CATEGORY_GROUPS).astype(jnp.int32),
    }


NORM_EPS = 1e-05
INV_ROOT_TWO = 0.7071067811865476
INV_ROOT_TWO_PI = 0.3989422804014327
CORR_ONE = 1.000026562104397
CORR_TWO = 10.50333528

def encode_block(block_states, w_in, w_out, norm_gain, doc_lengths):
    doc_count = block_states.shape[0]
    token_rows = block_states.reshape(-1, block_states.shape[2])
    pre_act = jnp.dot(token_rows, w_in, preferred_element_type=jnp.float32)
    normal_cdf = 0.5 * (1.0 + lax.erf(pre_act * INV_ROOT_TWO))
    hidden = (pre_act * normal_cdf).astype(jnp.bfloat16)
    summed = token_rows.astype(jnp.float32) + jnp.dot(hidden, w_out, preferred_element_type=jnp.float32)
    row_mean = lax.optimization_barrier(jnp.mean(summed, axis=-1, keepdims=True))
    centred = summed - row_mean
    inv_scale = lax.rsqrt(lax.optimization_barrier(jnp.mean(centred * centred, axis=-1, keepdims=True)) + NORM_EPS)
    normed = centred * inv_scale
    block_out = normed * norm_gain
    positions = jnp.arange(block_states.shape[1], dtype=jnp.int32)
    live_mask = (positions[None, :] < doc_lengths[:, None]).astype(jnp.float32)
    live_share = live_mask / doc_lengths[:, None].astype(jnp.float32)
    pooled = lax.optimization_barrier(jnp.sum(block_out.reshape(doc_count, block_states.shape[1], -1) * live_share[:, :, None], axis=1))
    embedded_tokens = pooled.astype(jnp.bfloat16)
    return (pre_act, normal_cdf, hidden, normed, inv_scale, live_share, embedded_tokens)

def backward_block(block_states, parts, emb_grad, w_out, norm_gain):
    pre_act, normal_cdf, hidden, normed, inv_scale, live_share, embedded_tokens = parts
    token_rows = block_states.reshape(-1, block_states.shape[2])
    pooled_grad = (emb_grad[:, None, :] * live_share[:, :, None]).reshape(token_rows.shape[0], -1)
    scaled = pooled_grad * norm_gain
    sum_grad = (scaled - lax.optimization_barrier(jnp.mean(scaled, axis=-1, keepdims=True)) - normed * lax.optimization_barrier(jnp.mean(scaled * normed, axis=-1, keepdims=True))) * inv_scale
    sum_grad = sum_grad.astype(jnp.bfloat16)
    grad_out = jnp.dot(hidden.T, sum_grad, preferred_element_type=jnp.float32)
    back_hidden = lax.dot_general(sum_grad, w_out, (((1,), (1,)), ((), ())), preferred_element_type=jnp.float32)
    slope = normal_cdf + pre_act * jnp.exp(-0.5 * pre_act * pre_act) * INV_ROOT_TWO_PI
    act_grad = (back_hidden * slope).astype(jnp.bfloat16)
    grad_in = jnp.dot(token_rows.T, act_grad, preferred_element_type=jnp.float32)
    return (grad_in, grad_out)

def reference(states, lengths, w_in, w_out, norm_gain, label_tiles, tile_mean, tile_var, shortlist, positives, owner_map):
    blocks = N_ENC * N_CLU
    state_blocks = states.reshape(blocks, DOC_DEV, LEN, D)
    length_blocks = lengths.reshape(blocks, DOC_DEV)

    def forward_embed(inputs):
        return encode_block(inputs[0], w_in, w_out, norm_gain, inputs[1])[6]
    embedded_tokens = lax.map(forward_embed, (state_blocks, length_blocks)).reshape(DOCS, D)
    doc_vectors = embedded_tokens.astype(jnp.float32)
    scores = jnp.dot(doc_vectors, label_tiles.T, precision=lax.Precision.HIGHEST)
    doc_index = jnp.arange(DOCS, dtype=jnp.int32)[:, None]
    slot_ids = jnp.take(owner_map, shortlist).astype(jnp.int32)
    cluster_live = jnp.zeros((DOCS, CATEGORY_GROUPS), jnp.float32).at[doc_index, slot_ids].set(1.0)
    live = jnp.repeat(cluster_live, LPC, axis=1)
    weighted = live * jnp.exp(scores)
    expsum = lax.optimization_barrier(jnp.sum(weighted, axis=1))
    posrow = (jnp.take(owner_map, positives // LPC) * LPC + positives % LPC).astype(jnp.int32)
    possum = lax.optimization_barrier(jnp.sum(jnp.take_along_axis(scores, posrow, axis=1), axis=1))
    loss = jnp.log(expsum) - possum / POS
    hits = jnp.zeros((DOCS, LABELS), jnp.float32).at[doc_index, posrow].add(1.0)
    logit_grad = weighted / expsum[:, None] - hits / POS
    emb_grad = jnp.dot(logit_grad, label_tiles, precision=lax.Precision.HIGHEST)
    panel_derivative = jnp.dot(logit_grad.T, doc_vectors, precision=lax.Precision.HIGHEST)
    new_mean = 0.9 * tile_mean + 0.1 * panel_derivative
    new_var = 0.999 * tile_var + 0.001 * panel_derivative * panel_derivative
    new_tiles = label_tiles - 0.001 * (new_mean * CORR_ONE) / (jnp.sqrt(new_var * CORR_TWO) + 1e-08)
    grad_blocks = emb_grad.reshape(blocks, DOC_DEV, D)

    def accumulate_sums(carry, inputs):
        block_states, block_lengths, block_grad = inputs
        parts = encode_block(block_states, w_in, w_out, norm_gain, block_lengths)
        add_in, add_out = backward_block(block_states, parts, block_grad, w_out, norm_gain)
        return ((carry[0] + add_in, carry[1] + add_out), None)
    initial_totals = (jnp.zeros((D, FF), jnp.float32), jnp.zeros((FF, D), jnp.float32))
    (grad_in, grad_out), unused = lax.scan(accumulate_sums, initial_totals, (state_blocks, length_blocks, grad_blocks))
    return (loss, new_tiles, new_mean, new_var, grad_in, grad_out)
```

```python
import jax
import jax.numpy as jnp
from jax import lax
from jax.experimental import pallas as pl
from jax.experimental.pallas import tpu as pltpu
from jax.sharding import Mesh, PartitionSpec as P

LPC = 4
POS = 4

NORM_EPS = 1e-05
INV_ROOT_TWO = 0.7071067811865476
INV_ROOT_TWO_PI = 0.3989422804014327
CORR_ONE = 1.000026562104397
CORR_TWO = 10.50333528

F32 = jnp.float32
BF16 = jnp.bfloat16
CHIPS = ("x", "z")
FIRST = (((0,), (0,)), ((), ()))
LAST = (((1,), (1,)), ((), ()))


def swap_core(a):
    return lax.ppermute(a, "c", [(0, 1), (1, 0)])


def swap_near(a):
    return lax.ppermute(a, "l", [(0, 1), (1, 0)])


def swap_diag(a):
    return lax.ppermute(a, ("l", "c"), [(0, 3), (3, 0), (1, 2), (2, 1)])


def swap_wrap(a):
    return lax.ppermute(a, ("h", "l"), [(0, 3), (3, 0), (1, 2), (2, 1)])


def gather_chips(a):
    return lax.all_to_all(a, CHIPS, 0, 0, tiled=True)


WHOLE = pl.BlockSpec(memory_space=pltpu.VMEM)
SCALARS = pl.BlockSpec(memory_space=pltpu.SMEM)
ANYWHERE = pl.BlockSpec(memory_space=pl.ANY)
LIMIT = pltpu.CompilerParams(vmem_limit_bytes=40 * 1024 * 1024)


def shape(dims, dtype):
    return jax.ShapeDtypeStruct(dims, dtype)


def cost(flops, data, special=0):
    return pl.CostEstimate(flops=flops, bytes_accessed=data, transcendentals=special)


def iota(dims, axis):
    return lax.broadcasted_iota(jnp.int32, dims, axis)


def pick_kernel(meta, w_in, mine, theirs):
    core, role = meta[0], meta[1]
    part = jnp.where(iota((512, 256), 1) < 128, core * 2 + role, 2 - core * 2 + role)
    at = iota((512, 256), 1) % 128
    spread = (iota((512, 256), 0) == at // 32 * 128 + part * 32 + at % 32).astype(BF16)
    for i in range(4):
        got = jnp.dot(w_in[:, i * 512 : i * 512 + 512], spread, preferred_element_type=F32).astype(BF16)
        mine[:, i * 128 : i * 128 + 128] = got[:, :128]
        theirs[:, i * 128 : i * 128 + 128] = got[:, 128:]


def lay_kernel(meta, mine, theirs, w_out, out):
    core, role = meta[0], meta[1]
    top = jnp.where(role == 0, w_out[:32], w_out[32:])
    first = jnp.where(core == 0, mine[...], theirs[...])
    second = jnp.where(core == 0, theirs[...], mine[...])
    for i in range(out.shape[0]):
        out[i, :32] = top
        out[i, 32:, :512] = first
        out[i, 32:, 512:] = second


def forward_kernel(tok_a, tok_b, weights, part_a, part_b, hidden, slope, w_in, w_out, sems):
    copies = [
        pltpu.make_async_copy(
            weights.at[:, 32:64, k * 512 : k * 512 + 512], w_in.at[:, k * 32 : k * 32 + 32], sems.at[k]
        )
        for k in range(2)
    ]
    copies.append(pltpu.make_async_copy(weights.at[:, 0:32], w_out, sems.at[2]))
    for copy in copies:
        copy.start()
    copies[0].wait()
    copies[1].wait()
    for k, (tok, part) in enumerate(((tok_a, part_a), (tok_b, part_b))):
        pre_act = jnp.dot(tok[...], w_in[...].reshape(1024, 512), preferred_element_type=F32)
        normal_cdf = 0.5 * (1.0 + lax.erf(pre_act * INV_ROOT_TWO))
        act = (pre_act * normal_cdf).astype(BF16)
        hidden[k * 256 : k * 256 + 256] = act
        slope[k * 256 : k * 256 + 256] = (
            normal_cdf + pre_act * jnp.exp(-0.5 * pre_act * pre_act) * INV_ROOT_TWO_PI
        )
        if k == 0:
            copies[2].wait()
        part[...] = jnp.dot(
            act, w_out[...].reshape(512, 1024), preferred_element_type=F32
        ).astype(part.dtype)


def forward(tok_a, tok_b, weights):
    return pl.pallas_call(
        forward_kernel,
        out_shape=(
            shape((256, 1024), BF16),
            shape((256, 1024), F32),
            shape((512, 512), BF16),
            shape((512, 512), F32),
        ),
        in_specs=[WHOLE, WHOLE, ANYWHERE],
        out_specs=(WHOLE,) * 4,
        scratch_shapes=[
            pltpu.VMEM((16, 64, 512), BF16),
            pltpu.VMEM((16, 32, 1024), BF16),
            pltpu.SemaphoreType.DMA((3,)),
        ],
        compiler_params=LIMIT,
        cost_estimate=cost(2**30, 6 * 2**20, 2**19),
    )(tok_a, tok_b, weights)


def norm_kernel(lengths, tok, part, from_core, from_near, gain, rows, emb):
    embs = []
    for d in range(8):
        at = pl.ds(d * 32, 32)
        summed = tok[at].astype(F32) + (
            part[at] + from_core[at].astype(F32) + from_near[at].astype(F32)
        )
        centred = summed - jnp.mean(summed, axis=-1, keepdims=True)
        inv = lax.rsqrt(jnp.mean(centred * centred, axis=-1, keepdims=True) + NORM_EPS)
        normed = centred * inv
        count = jnp.full((32, 1), lengths[d], jnp.int32).astype(F32)
        share = jnp.where(iota((32, 1), 0).astype(F32) < count, 1.0, 0.0) / count
        embs.append(jnp.sum(normed * gain[...] * share, axis=0, keepdims=True))
        high = inv.astype(BF16).astype(F32)
        lane = iota((32, 128), 1)
        extra = jnp.where(lane == 0, high, jnp.where(lane == 1, inv - high, jnp.where(lane == 2, count, 0.0)))
        rows[at, :1024] = normed.astype(BF16)
        rows[at, 1024:] = extra.astype(BF16)
    docs = jnp.concatenate(embs, axis=0)
    emb[...] = jnp.concatenate([docs] * 16, axis=0).astype(BF16)


def score_kernel(emb, own_tiles, oth_tiles, live, packed, weighted):
    docs = emb[...].astype(F32)
    for k, tiles in enumerate((own_tiles, oth_tiles)):
        at = pl.ds(k * 256, 256)
        scores = lax.dot_general(
            docs, tiles[...], LAST, precision=lax.Precision.HIGHEST, preferred_element_type=F32
        )
        weighted[:, at] = live[:, at] * jnp.exp(scores)
    value = weighted[...]
    part_emb = jnp.dot(
        value[:, :256], own_tiles[...], precision=lax.Precision.HIGHEST, preferred_element_type=F32
    ) + jnp.dot(
        value[:, 256:], oth_tiles[...], precision=lax.Precision.HIGHEST, preferred_element_type=F32
    )
    sums = jnp.sum(value, axis=1, keepdims=True) * 0.5
    high = sums.astype(BF16).astype(F32)
    row, lane = iota((128, 128), 0), iota((128, 128), 1)
    chosen = row // 8 == lane
    same = (row % 8 == lane % 8).astype(BF16)
    for k, part in enumerate((high, sums - high)):
        table = jnp.where(chosen, part, 0.0).astype(BF16)
        packed[:, 1024 + k * 128 : 1152 + k * 128] = jnp.dot(
            same, table, preferred_element_type=F32
        ).astype(BF16)
    packed[:, :1024] = part_emb.astype(BF16)


def settle_kernel(meta, got, pos, emb, grad, loss, sums):
    total = got[0].astype(F32)
    for i in range(1, 16):
        total = total + got[i].astype(F32)
    every = (total[:, 1024:1152] + total[:, 1152:1280]) * 2.0
    sums[...] = every
    expsum = jnp.sum(jnp.where(iota((8, 128), 1) == meta[2], every, 0.0), axis=1, keepdims=True)
    pos_mean = jnp.sum(pos[...], axis=0)
    grad[...] = total[:, :1024] / expsum - pos_mean
    picked = jnp.sum(emb[...].astype(F32)[:8] * pos_mean, axis=1, keepdims=True)
    loss[...] = jnp.broadcast_to(jnp.log(expsum) - picked, (8, 128))


def backward_kernel(*refs):
    grads, gain = refs[:4], refs[4]
    rows, toks = refs[5:9], refs[9:13]
    hiddens, slopes, weights, out = refs[13:15], refs[15:17], refs[17], refs[18]
    row_buf, tok_buf, hid_buf, slope_buf, w_out, sum_grad, act_grad, sems = refs[19:]
    first = pltpu.make_async_copy(weights.at[:, 0:32], w_out, sems.at[0])
    first.start()
    row_copies, tok_copies, hid_copies, slope_copies = [], [], [], []
    for k in range(4):
        at = pl.ds(k * 256, 256)
        row_copies.append(pltpu.make_async_copy(rows[k], row_buf.at[at], sems.at[1 + k]))
        row_copies[k].start()
    for k in range(2):
        at = pl.ds(k * 512, 512)
        slope_copies.append(pltpu.make_async_copy(slopes[k], slope_buf.at[at], sems.at[5 + k]))
        slope_copies[k].start()
    for k in range(2):
        at = pl.ds(k * 512, 512)
        hid_copies.append(pltpu.make_async_copy(hiddens[k], hid_buf.at[at], sems.at[7 + k]))
        hid_copies[k].start()
    for k in range(4):
        at = pl.ds(k * 256, 256)
        tok_copies.append(pltpu.make_async_copy(toks[k], tok_buf.at[at], sems.at[9 + k]))
        tok_copies[k].start()
    for k in range(4):
        row_copies[k].wait()
        scaled_grad = grads[k][...] * gain[...]
        grad_mean = jnp.mean(scaled_grad, axis=-1, keepdims=True)
        for d in range(8):
            at = pl.ds(k * 256 + d * 32, 32)
            norm = row_buf[at, :1024].astype(F32)
            extra = row_buf[at, 1024:].astype(F32)
            lane = iota((32, 128), 1)
            scale = jnp.sum(jnp.where(lane < 2, extra, 0.0), axis=1, keepdims=True)
            count = jnp.sum(jnp.where(lane == 2, extra, 0.0), axis=1, keepdims=True)
            share = jnp.where(iota((32, 1), 0).astype(F32) < count, 1.0, 0.0) / count
            grad = scaled_grad[d : d + 1]
            along = jnp.mean(grad * norm, axis=-1, keepdims=True)
            sum_grad[at] = (
                (grad - grad_mean[d : d + 1] - norm * along) * (share * scale)
            ).astype(BF16)
        if k == 0:
            first.wait()
        if k % 2 == 0:
            slope_copies[k // 2].wait()
        at = pl.ds(k * 256, 256)
        back = lax.dot_general(
            sum_grad[at], w_out[...].reshape(512, 1024), LAST, preferred_element_type=F32
        )
        act_grad[at] = (back * slope_buf[at]).astype(BF16)
    for copy in hid_copies:
        copy.wait()
    for i in range(4):
        part = lax.dot_general(
            hid_buf[:, i * 128 : i * 128 + 128], sum_grad[...], FIRST, preferred_element_type=F32
        )
        out[i * 4 : i * 4 + 4, :32] = part.astype(BF16).reshape(4, 32, 1024)
    for copy in tok_copies:
        copy.wait()
    for i in range(4):
        part = lax.dot_general(
            tok_buf[:, i * 256 : i * 256 + 256], act_grad[...], FIRST, preferred_element_type=F32
        ).astype(BF16).reshape(4, 2, 32, 512)
        out[i * 4 : i * 4 + 4, 32:, :512] = part[:, 0]
        out[i * 4 : i * 4 + 4, 32:, 512:] = part[:, 1]


def backward(grads, gain, rows, toks, hiddens, slopes, weights):
    return pl.pallas_call(
        backward_kernel,
        out_shape=shape((16, 64, 1024), BF16),
        in_specs=[WHOLE] * 5 + [ANYWHERE] * 13,
        out_specs=WHOLE,
        scratch_shapes=[
            pltpu.VMEM((1024, 1152), BF16),
            pltpu.VMEM((1024, 1024), BF16),
            pltpu.VMEM((1024, 512), BF16),
            pltpu.VMEM((1024, 512), F32),
            pltpu.VMEM((16, 32, 1024), BF16),
            pltpu.VMEM((1024, 1024), BF16),
            pltpu.VMEM((1024, 512), BF16),
            pltpu.SemaphoreType.DMA((13,)),
        ],
        compiler_params=LIMIT,
        cost_estimate=cost(3 * 2**30, 10 * 2**20),
    )(*grads, gain, *rows, *toks, *hiddens, *slopes, weights)


def total_kernel(got, out):
    total = got[0].astype(F32)
    for i in range(1, 16):
        total = total + got[i].astype(F32)
    out[...] = total.astype(BF16)


def place_kernel(meta, own, near, core_part, diag_part, grad_in, grad_out):
    core, role = meta[0], meta[1]
    mine, theirs = own[:32].astype(F32), near[:32].astype(F32)
    grad_out[:32] = jnp.where(role == 0, mine, theirs)
    grad_out[32:] = jnp.where(role == 0, theirs, mine)
    pieces = (
        jnp.where(core == 0, own[32:, :512], own[32:, 512:]),
        core_part[...],
        jnp.where(core == 0, near[32:, :512], near[32:, 512:]),
        diag_part[...],
    )
    row, lane = iota((512, 512), 0), iota((512, 512), 1)
    piece, at = row // 128, row % 128
    swapped = piece % 2
    part = (core + swapped - 2 * core * swapped) * 2
    flipped = piece // 2
    part = part + role + flipped - 2 * role * flipped
    spread = (lane == at // 32 * 128 + part * 32 + at % 32).astype(BF16)
    for i in range(4):
        block = jnp.concatenate([a[:, i * 128 : i * 128 + 128] for a in pieces], axis=1)
        grad_in[:, i * 512 : i * 512 + 512] = jnp.dot(block, spread, preferred_element_type=F32)


def on_device(
    states,
    lengths,
    w_in,
    w_out,
    norm_gain,
    label_tiles,
    tile_mean,
    tile_var,
    shortlist,
    positives,
    owner_map,
):
    docs, length, width = states.shape
    core = lax.axis_index("c")
    high, low = lax.axis_index("h"), lax.axis_index("l")
    role = high + low - 2 * high * low
    chip = lax.axis_index("x") * 4 + lax.axis_index("z")
    meta = jnp.stack([core, role, chip]).astype(jnp.int32)
    gain = norm_gain.reshape(1, width)
    own_tok = states.reshape(docs * length, width)

    mine, theirs = pl.pallas_call(
        pick_kernel,
        out_shape=(shape((32, 512), BF16),) * 2,
        in_specs=[SCALARS, WHOLE],
        out_specs=(WHOLE, WHOLE),
        cost_estimate=cost(2**25, 2**18),
    )(meta, w_in)
    weights = gather_chips(
        pl.pallas_call(
            lay_kernel,
            out_shape=shape((16, 64, width), BF16),
            grid=(4,),
            in_specs=[SCALARS, WHOLE, WHOLE, WHOLE],
            out_specs=pl.BlockSpec((4, 64, width), lambda i: (i, 0, 0)),
            cost_estimate=cost(0, 2**21),
        )(meta, mine, swap_core(theirs), w_out)
    )

    core_tok, near_tok, diag_tok = swap_core(own_tok), swap_near(own_tok), swap_diag(own_tok)

    oth_tiles = swap_core(label_tiles)
    slots = jnp.concatenate(
        [(chip * 2 + core) * 64 + jnp.arange(64), (chip * 2 + 1 - core) * 64 + jnp.arange(64)]
    ).astype(jnp.int32)
    all_clusters = jnp.arange(owner_map.shape[0], dtype=jnp.int32)
    owner_match = owner_map[:, None] == slots[None, :]
    cluster_ids = jnp.sum(jnp.where(owner_match, all_clusters[:, None], 0), axis=0)
    pick = lambda a: lax.dynamic_index_in_dim(a.reshape(16, 2, 8, -1), core, 1, False).reshape(128, -1)
    short, posit = pick(shortlist), pick(positives)
    cluster_live = jnp.max(
        (short[:, :, None] == cluster_ids[None, None, :]).astype(F32), axis=1
    )
    live = jnp.repeat(cluster_live, LPC, axis=1)
    cluster_hit = (posit[:, :, None] // LPC == cluster_ids[None, None, :]).astype(F32)
    offset_hit = (
        posit[:, :, None] % LPC == jnp.arange(LPC, dtype=jnp.int32)[None, None, :]
    ).astype(F32)
    hits = jnp.sum(cluster_hit[:, :, :, None] * offset_hit[:, :, None, :], axis=1).reshape(128, 512)
    share_hit = hits / POS
    pos_part = (
        jnp.dot(share_hit[:, :256], label_tiles, precision=lax.Precision.HIGH)
        + jnp.dot(share_hit[:, 256:], oth_tiles, precision=lax.Precision.HIGH)
    )
    weights, live, share_hit, pos_part = lax.optimization_barrier(
        (weights, live, share_hit, pos_part)
    )

    near_a, near_b, near_hidden, near_slope = forward(diag_tok, near_tok, weights)
    near_sum = (near_b + swap_core(near_a).astype(F32)).astype(BF16)
    near_sum, pos_part = lax.optimization_barrier((near_sum, pos_part))
    from_near = swap_near(near_sum)
    pos_got = gather_chips(pos_part.reshape(16, docs, width))
    own_a, own_b, own_hidden, own_slope = forward(core_tok, own_tok, weights)
    from_near, pos_got = lax.optimization_barrier((from_near, pos_got))
    own_rows, emb = pl.pallas_call(
        norm_kernel,
        out_shape=(shape((256, 1152), BF16), shape((128, width), BF16)),
        in_specs=[SCALARS] + [WHOLE] * 5,
        out_specs=(WHOLE, WHOLE),
        compiler_params=LIMIT,
        cost_estimate=cost(2**22, 4 * 2**20),
    )(lengths, own_tok, own_b, swap_core(own_a), from_near, gain)

    plane_emb = gather_chips(emb.reshape(16, docs, width)).reshape(128, width)
    core_rows, near_rows, diag_rows = swap_core(own_rows), swap_near(own_rows), swap_diag(own_rows)
    packed, weighted = pl.pallas_call(
        score_kernel,
        out_shape=(shape((128, 1280), BF16), shape((128, 512), F32)),
        in_specs=[WHOLE] * 4,
        out_specs=(WHOLE, WHOLE),
        compiler_params=LIMIT,
        cost_estimate=cost(2**30, 5 * 2**20, 2**16),
    )(plane_emb, label_tiles, oth_tiles, live)
    got = lax.all_to_all(packed.reshape(16, docs, 1280), CHIPS, 0, 0, tiled=True)
    emb_grad, loss, sums = pl.pallas_call(
        settle_kernel,
        out_shape=(shape((docs, width), F32), shape((docs, 128), F32), shape((docs, 128), F32)),
        in_specs=[SCALARS, WHOLE, WHOLE, WHOLE],
        out_specs=(WHOLE,) * 3,
        compiler_params=LIMIT,
        cost_estimate=cost(2**20, 2**20),
    )(meta, got, pos_got, emb)
    loss = loss[:, 0]

    grads = (swap_diag(emb_grad), swap_near(emb_grad), swap_core(emb_grad), emb_grad)
    send = backward(
        grads,
        gain,
        (diag_rows, near_rows, core_rows, own_rows),
        (diag_tok, near_tok, core_tok, own_tok),
        (near_hidden, own_hidden),
        (near_slope, own_slope),
        weights,
    )
    got = lax.all_to_all(send, CHIPS, 0, 0, tiled=True)
    part = pl.pallas_call(
        total_kernel,
        out_shape=shape((64, width), BF16),
        grid=(4,),
        in_specs=[pl.BlockSpec((16, 16, width), lambda i: (0, i, 0))],
        out_specs=pl.BlockSpec((16, width), lambda i: (i, 0)),
        compiler_params=LIMIT,
        cost_estimate=cost(2**20, 2**21),
    )(got)
    both = (part.astype(F32) + swap_wrap(part).astype(F32)).astype(BF16)
    give = jnp.where(core == 0, both[32:, 512:], both[32:, :512])
    grad_in, grad_out = pl.pallas_call(
        place_kernel,
        out_shape=(shape((32, 2048), F32), shape((64, width), F32)),
        in_specs=[SCALARS] + [WHOLE] * 4,
        out_specs=(WHOLE, WHOLE),
        compiler_params=LIMIT,
        cost_estimate=cost(2**26, 2**20),
    )(meta, both, swap_near(both), swap_core(give), swap_diag(give))

    all_sums = sums[:, :16].T.reshape(128)
    logit_grad = weighted / all_sums[:, None] - share_hit
    tile_part = lax.dot_general(
        logit_grad, plane_emb.astype(F32), FIRST, precision=lax.Precision.HIGH
    )
    tile_chip = (tile_part[:256] + swap_core(tile_part[256:])).astype(BF16)

    def add(a, swap):
        return a.astype(F32) + swap(a).astype(F32)

    tile_grad = jnp.concatenate(
        [
            add(add(tile_chip[:128], swap_near).astype(BF16), swap_wrap),
            add(add(tile_chip[128:], swap_wrap).astype(BF16), swap_near),
        ],
        axis=0,
    )
    new_mean = 0.9 * tile_mean + 0.1 * tile_grad
    new_var = 0.999 * tile_var + 0.001 * tile_grad * tile_grad
    new_tiles = label_tiles - 0.001 * (new_mean * CORR_ONE) / (jnp.sqrt(new_var * CORR_TWO) + 1e-08)
    return (loss, new_tiles, new_mean, new_var, grad_in, grad_out)


def solution(mesh):
    grid = Mesh(mesh.devices.reshape(2, 2, 4, 4, 2), ("h", "l", "x", "z", "c"))
    every, plane, group = ("h", "l", "x", "z", "c"), ("x", "z", "c"), ("h", "l")
    return jax.shard_map(
        on_device,
        mesh=grid,
        in_specs=(
            P(every, None, None),
            P(every),
            P(plane, None),
            P(plane, None),
            P(),
            P(plane, None),
            P(plane, None),
            P(plane, None),
            P(group, None),
            P(group, None),
            P(),
        ),
        out_specs=(
            P(every),
            P(plane, None),
            P(plane, None),
            P(plane, None),
            P(plane, None),
            P(plane, None),
        ),
        check_vma=False,
    )
```

```python
import jax
import jax.numpy as jnp
from jax import lax
from jax.experimental import pallas as pl
from jax.experimental.pallas import tpu as pltpu
from jax.sharding import Mesh, PartitionSpec as P

LPC = 4
POS = 4

NORM_EPS = 1e-05
INV_ROOT_TWO = 0.7071067811865476
INV_ROOT_TWO_PI = 0.3989422804014327
CORR_ONE = 1.000026562104397
CORR_TWO = 10.50333528

F32 = jnp.float32
BF16 = jnp.bfloat16
CHIPS = ("x", "z")
FIRST = (((0,), (0,)), ((), ()))
LAST = (((1,), (1,)), ((), ()))


def swap_core(a):
    return lax.ppermute(a, "c", [(0, 1), (1, 0)])


def swap_near(a):
    return lax.ppermute(a, "l", [(0, 1), (1, 0)])


def swap_diag(a):
    return lax.ppermute(a, ("l", "c"), [(0, 3), (3, 0), (1, 2), (2, 1)])


def swap_far(a):
    return lax.ppermute(a, "h", [(0, 1), (1, 0)])


def swap_wrap(a):
    return lax.ppermute(a, ("h", "l"), [(0, 3), (3, 0), (1, 2), (2, 1)])


def round_bf16(a):
    return lax.reduce_precision(a, 8, 7)


def gather_chips(a):
    return lax.all_to_all(a, CHIPS, 0, 0, tiled=True)


WHOLE = pl.BlockSpec(memory_space=pltpu.VMEM)
SCALARS = pl.BlockSpec(memory_space=pltpu.SMEM)
ANYWHERE = pl.BlockSpec(memory_space=pl.ANY)
LIMIT = pltpu.CompilerParams(vmem_limit_bytes=40 * 1024 * 1024)


def shape(dims, dtype):
    return jax.ShapeDtypeStruct(dims, dtype)


def cost(flops, data, special=0):
    return pl.CostEstimate(flops=flops, bytes_accessed=data, transcendentals=special)


def iota(dims, axis):
    return lax.broadcasted_iota(jnp.int32, dims, axis)


def pick_kernel(meta, w_in, mine, theirs):
    core, role = meta[0], meta[1]
    part = jnp.where(iota((512, 256), 1) < 128, core * 2 + role, 2 - core * 2 + role)
    at = iota((512, 256), 1) % 128
    spread = (iota((512, 256), 0) == at // 32 * 128 + part * 32 + at % 32).astype(BF16)
    for i in range(4):
        got = jnp.dot(w_in[:, i * 512 : i * 512 + 512], spread, preferred_element_type=F32).astype(BF16)
        mine[:, i * 128 : i * 128 + 128] = got[:, :128]
        theirs[:, i * 128 : i * 128 + 128] = got[:, 128:]


def lay_kernel(meta, mine, theirs, w_out, out, block, sems):
    core, role = meta[0], meta[1]
    block[:32] = jnp.where(role == 0, w_out[:32], w_out[32:])
    block[32:, :512] = jnp.where(core == 0, mine[...], theirs[...])
    block[32:, 512:] = jnp.where(core == 0, theirs[...], mine[...])
    copies = [pltpu.make_async_copy(block, out.at[i], sems.at[i]) for i in range(16)]
    for copy in copies:
        copy.start()
    for copy in copies:
        copy.wait()


def forward_kernel(tok_a, tok_b, weights, part_a, part_b, hidden, slope, w_in, w_out, sems):
    copies = [
        pltpu.make_async_copy(
            weights.at[:, 32:64, k * 512 : k * 512 + 512], w_in.at[:, k * 32 : k * 32 + 32], sems.at[k]
        )
        for k in range(2)
    ]
    copies.append(pltpu.make_async_copy(weights.at[:, 0:32], w_out, sems.at[2]))
    for copy in copies:
        copy.start()
    copies[0].wait()
    copies[1].wait()
    for k, (tok, part) in enumerate(((tok_a, part_a), (tok_b, part_b))):
        pre_act = jnp.dot(tok[...], w_in[...].reshape(1024, 512), preferred_element_type=F32)
        normal_cdf = 0.5 * (1.0 + lax.erf(pre_act * INV_ROOT_TWO))
        act = (pre_act * normal_cdf).astype(BF16)
        hidden[k * 256 : k * 256 + 256] = act
        slope[k * 256 : k * 256 + 256] = (
            normal_cdf + pre_act * jnp.exp(-0.5 * pre_act * pre_act) * INV_ROOT_TWO_PI
        )
        if k == 0:
            copies[2].wait()
        part[...] = jnp.dot(
            act, w_out[...].reshape(512, 1024), preferred_element_type=F32
        ).astype(part.dtype)


def forward(tok_a, tok_b, weights):
    return pl.pallas_call(
        forward_kernel,
        out_shape=(
            shape((256, 1024), BF16),
            shape((256, 1024), F32),
            shape((512, 512), BF16),
            shape((512, 512), F32),
        ),
        in_specs=[WHOLE, WHOLE, ANYWHERE],
        out_specs=(WHOLE,) * 4,
        scratch_shapes=[
            pltpu.VMEM((16, 64, 512), BF16),
            pltpu.VMEM((16, 32, 1024), BF16),
            pltpu.SemaphoreType.DMA((3,)),
        ],
        compiler_params=LIMIT,
        cost_estimate=cost(2**30, 6 * 2**20, 2**19),
    )(tok_a, tok_b, weights)


def norm_kernel(lengths, tok, part, from_core, from_near, gain, rows, emb):
    embs = []
    for d in range(8):
        at = pl.ds(d * 32, 32)
        summed = tok[at].astype(F32) + (
            part[at] + from_core[at].astype(F32) + from_near[at].astype(F32)
        )
        centred = summed - jnp.mean(summed, axis=-1, keepdims=True)
        inv = lax.rsqrt(jnp.mean(centred * centred, axis=-1, keepdims=True) + NORM_EPS)
        normed = centred * inv
        count = jnp.full((32, 1), lengths[d], jnp.int32).astype(F32)
        share = jnp.where(iota((32, 1), 0).astype(F32) < count, 1.0, 0.0) / count
        embs.append(jnp.sum(normed * gain[...] * share, axis=0, keepdims=True))
        high = inv.astype(BF16).astype(F32)
        lane = iota((32, 128), 1)
        extra = jnp.where(lane == 0, high, jnp.where(lane == 1, inv - high, jnp.where(lane == 2, count, 0.0)))
        rows[at, :1024] = normed.astype(BF16)
        rows[at, 1024:] = extra.astype(BF16)
    docs = jnp.concatenate(embs, axis=0)
    emb[...] = jnp.concatenate([docs] * 16, axis=0).astype(BF16)


def score_kernel(emb, tiles_hi, tiles_lo, live, packed, weighted, emb_buf, sem):
    copy = pltpu.make_async_copy(emb, emb_buf, sem)
    copy.start()
    grow = (iota((128, 512), 0) == iota((128, 512), 1) // LPC).astype(BF16)
    mask = jnp.dot(live[...], grow, preferred_element_type=F32)
    copy.wait()
    docs = emb_buf[...]
    scores = lax.dot_general(docs, tiles_hi[...], LAST, preferred_element_type=F32)
    scores = scores + lax.dot_general(docs, tiles_lo[...], LAST, preferred_element_type=F32)
    value = mask * jnp.exp(scores)
    weighted[...] = value
    value_hi = value.astype(BF16)
    value_lo = (value - value_hi.astype(F32)).astype(BF16)
    part_emb = jnp.dot(value_hi, tiles_hi[...], preferred_element_type=F32)
    part_emb = part_emb + jnp.dot(value_hi, tiles_lo[...], preferred_element_type=F32)
    part_emb = part_emb + jnp.dot(value_lo, tiles_hi[...], preferred_element_type=F32)
    sums = jnp.sum(value, axis=1, keepdims=True) * 0.5
    high = sums.astype(BF16).astype(F32)
    row, lane = iota((128, 128), 0), iota((128, 128), 1)
    chosen = row // 8 == lane
    same = (row % 8 == lane % 8).astype(BF16)
    for k, part in enumerate((high, sums - high)):
        table = jnp.where(chosen, part, 0.0).astype(BF16)
        packed[:, 1024 + k * 128 : 1152 + k * 128] = jnp.dot(
            same, table, preferred_element_type=F32
        ).astype(BF16)
    packed[:, :1024] = part_emb.astype(BF16)


def settle_kernel(meta, got_hbm, pos_hbm, emb, grad, loss, sums, got, pos, sems):
    copies = [
        pltpu.make_async_copy(got_hbm, got, sems.at[0]),
        pltpu.make_async_copy(pos_hbm, pos, sems.at[1]),
    ]
    for copy in copies:
        copy.start()
    for copy in copies:
        copy.wait()
    total = got[0].astype(F32)
    for i in range(1, 16):
        total = total + got[i].astype(F32)
    every = (total[:, 1024:1152] + total[:, 1152:1280]) * 2.0
    sums[...] = every
    expsum = jnp.sum(jnp.where(iota((8, 128), 1) == meta[2], every, 0.0), axis=1, keepdims=True)
    pos_mean = jnp.sum(pos[...], axis=0)
    grad[...] = total[:, :1024] / expsum - pos_mean
    picked = jnp.sum(emb[...].astype(F32)[:8] * pos_mean, axis=1, keepdims=True)
    loss[...] = jnp.broadcast_to(jnp.log(expsum) - picked, (8, 128))


def backward_kernel(*refs):
    grads, gain = refs[:4], refs[4]
    rows, toks = refs[5:9], refs[9:13]
    hiddens, slopes, weights, out = refs[13:15], refs[15:17], refs[17], refs[18]
    row_buf, tok_buf, hid_buf, slope_buf, w_out, sum_grad, act_grad, result, sems = refs[19:]
    sent = []
    first = pltpu.make_async_copy(weights.at[:, 0:32], w_out, sems.at[0])
    first.start()
    row_copies, tok_copies, hid_copies, slope_copies = [], [], [], []
    for k in range(4):
        at = pl.ds(k * 256, 256)
        row_copies.append(pltpu.make_async_copy(rows[k], row_buf.at[at], sems.at[1 + k]))
        row_copies[k].start()
    for k in range(2):
        at = pl.ds(k * 512, 512)
        slope_copies.append(pltpu.make_async_copy(slopes[k], slope_buf.at[at], sems.at[5 + k]))
        slope_copies[k].start()
    for k in range(2):
        at = pl.ds(k * 512, 512)
        hid_copies.append(pltpu.make_async_copy(hiddens[k], hid_buf.at[at], sems.at[7 + k]))
        hid_copies[k].start()
    for k in range(4):
        at = pl.ds(k * 256, 256)
        tok_copies.append(pltpu.make_async_copy(toks[k], tok_buf.at[at], sems.at[9 + k]))
        tok_copies[k].start()
    for k in range(4):
        row_copies[k].wait()
        scaled_grad = grads[k][...] * gain[...]
        grad_mean = jnp.mean(scaled_grad, axis=-1, keepdims=True)
        for d in range(8):
            at = pl.ds(k * 256 + d * 32, 32)
            norm = row_buf[at, :1024].astype(F32)
            extra = row_buf[at, 1024:].astype(F32)
            lane = iota((32, 128), 1)
            scale = jnp.sum(jnp.where(lane < 2, extra, 0.0), axis=1, keepdims=True)
            count = jnp.sum(jnp.where(lane == 2, extra, 0.0), axis=1, keepdims=True)
            share = jnp.where(iota((32, 1), 0).astype(F32) < count, 1.0, 0.0) / count
            grad = scaled_grad[d : d + 1]
            along = jnp.mean(grad * norm, axis=-1, keepdims=True)
            sum_grad[at] = (
                (grad - grad_mean[d : d + 1] - norm * along) * (share * scale)
            ).astype(BF16)
        if k == 0:
            first.wait()
        if k % 2 == 0:
            slope_copies[k // 2].wait()
        at = pl.ds(k * 256, 256)
        back = lax.dot_general(
            sum_grad[at], w_out[...].reshape(512, 1024), LAST, preferred_element_type=F32
        )
        act_grad[at] = (back * slope_buf[at]).astype(BF16)
    for copy in hid_copies:
        copy.wait()
    for i in range(4):
        part = lax.dot_general(
            hid_buf[:, i * 128 : i * 128 + 128], sum_grad[...], FIRST, preferred_element_type=F32
        )
        at = pl.ds(i * 4, 4)
        result[at, :32] = part.astype(BF16).reshape(4, 32, 1024)
        sent.append(pltpu.make_async_copy(result.at[at, 0:32], out.at[at, 0:32], sems.at[13 + i]))
        sent[-1].start()
    for copy in tok_copies:
        copy.wait()
    for i in range(4):
        part = lax.dot_general(
            tok_buf[:, i * 256 : i * 256 + 256], act_grad[...], FIRST, preferred_element_type=F32
        ).astype(BF16).reshape(4, 2, 32, 512)
        at = pl.ds(i * 4, 4)
        result[at, 32:, :512] = part[:, 0]
        result[at, 32:, 512:] = part[:, 1]
        sent.append(pltpu.make_async_copy(result.at[at, 32:64], out.at[at, 32:64], sems.at[17 + i]))
        sent[-1].start()
    for copy in sent:
        copy.wait()


def backward(grads, gain, rows, toks, hiddens, slopes, weights):
    return pl.pallas_call(
        backward_kernel,
        out_shape=shape((16, 64, 1024), BF16),
        in_specs=[WHOLE] * 5 + [ANYWHERE] * 13,
        out_specs=ANYWHERE,
        scratch_shapes=[
            pltpu.VMEM((1024, 1152), BF16),
            pltpu.VMEM((1024, 1024), BF16),
            pltpu.VMEM((1024, 512), BF16),
            pltpu.VMEM((1024, 512), F32),
            pltpu.VMEM((16, 32, 1024), BF16),
            pltpu.VMEM((1024, 1024), BF16),
            pltpu.VMEM((1024, 512), BF16),
            pltpu.VMEM((16, 64, 1024), BF16),
            pltpu.SemaphoreType.DMA((21,)),
        ],
        compiler_params=LIMIT,
        cost_estimate=cost(3 * 2**30, 10 * 2**20),
    )(*grads, gain, *rows, *toks, *hiddens, *slopes, weights)


def total_kernel(meta, got, out, keep, give):
    total = got[0].astype(F32)
    for i in range(1, 16):
        total = total + got[i].astype(F32)
    total = total.astype(BF16)
    core, step = meta[0], pl.program_id(0)

    @pl.when(step < 2)
    def _():
        out[...] = total

    @pl.when(step >= 2)
    def _():
        keep[...] = jnp.where(core == 0, total[:, :512], total[:, 512:])
        give[...] = jnp.where(core == 0, total[:, 512:], total[:, :512])


def place_kernel(meta, own, near, wrap, far, grad_in, grad_out):
    core, role = meta[0], meta[1]
    mine = own[:32].astype(F32) + wrap[:32].astype(F32)
    theirs = near[:32].astype(F32) + far[:32].astype(F32)
    grad_out[:32] = jnp.where(role == 0, mine, theirs)
    grad_out[32:] = jnp.where(role == 0, theirs, mine)
    row, lane = iota((1024, 512), 0), iota((1024, 512), 1)
    piece, at = row // 128, row % 128
    swapped, flipped = piece % 2, piece // 4
    part = (core + swapped - 2 * core * swapped) * 2 + (role + flipped - 2 * role * flipped)
    spread = (lane == at // 32 * 128 + part * 32 + at % 32).astype(BF16)
    for i in range(4):
        block = jnp.concatenate(
            [
                a[32:, k * 512 + i * 128 : k * 512 + i * 128 + 128]
                for a in (own, wrap, near, far)
                for k in range(2)
            ],
            axis=1,
        )
        grad_in[:, i * 512 : i * 512 + 512] = jnp.dot(block, spread, preferred_element_type=F32)


def on_device(
    states,
    lengths,
    w_in,
    w_out,
    norm_gain,
    label_tiles,
    tile_mean,
    tile_var,
    shortlist,
    positives,
    owner_map,
):
    docs, length, width = states.shape
    core = lax.axis_index("c")
    high, low = lax.axis_index("h"), lax.axis_index("l")
    role = high + low - 2 * high * low
    chip = lax.axis_index("x") * 4 + lax.axis_index("z")
    meta = jnp.stack([core, role, chip]).astype(jnp.int32)
    gain = norm_gain.reshape(1, width)
    own_tok = states.reshape(docs * length, width)

    mine, theirs = pl.pallas_call(
        pick_kernel,
        out_shape=(shape((32, 512), BF16),) * 2,
        in_specs=[SCALARS, WHOLE],
        out_specs=(WHOLE, WHOLE),
        cost_estimate=cost(2**25, 2**18),
    )(meta, w_in)
    weights = gather_chips(
        pl.pallas_call(
            lay_kernel,
            out_shape=shape((16, 64, width), BF16),
            in_specs=[SCALARS, WHOLE, WHOLE, WHOLE],
            out_specs=ANYWHERE,
            scratch_shapes=[pltpu.VMEM((64, width), BF16), pltpu.SemaphoreType.DMA((16,))],
            cost_estimate=cost(0, 2**21),
        )(meta, mine, swap_core(theirs), w_out)
    )

    core_tok, near_tok, diag_tok = swap_core(own_tok), swap_near(own_tok), swap_diag(own_tok)

    oth_tiles = swap_core(label_tiles)
    slots = jnp.concatenate(
        [(chip * 2 + core) * 64 + jnp.arange(64), (chip * 2 + 1 - core) * 64 + jnp.arange(64)]
    ).astype(jnp.int32)
    all_clusters = jnp.arange(owner_map.shape[0], dtype=jnp.int32)
    owner_match = owner_map[:, None] == slots[None, :]
    cluster_ids = jnp.sum(jnp.where(owner_match, all_clusters[:, None], 0), axis=0)
    pick = lambda a: lax.dynamic_index_in_dim(a.reshape(16, 2, 8, -1), core, 1, False).reshape(128, -1)
    short, posit = pick(shortlist), pick(positives)
    cluster_live = jnp.max(
        (short[:, :, None] == cluster_ids[None, None, :]).astype(F32), axis=1
    ).astype(BF16)
    tiles = jnp.concatenate([label_tiles, oth_tiles], axis=0)
    tiles_top = round_bf16(tiles)
    tiles_hi, tiles_lo = tiles_top.astype(BF16), (tiles - tiles_top).astype(BF16)
    cluster_hit = (posit[:, :, None] // LPC == cluster_ids[None, None, :]).astype(F32)
    offset_hit = (
        posit[:, :, None] % LPC == jnp.arange(LPC, dtype=jnp.int32)[None, None, :]
    ).astype(F32)
    hits = jnp.sum(cluster_hit[:, :, :, None] * offset_hit[:, :, None, :], axis=1).reshape(128, 512)
    share_hit = hits / POS
    hit = share_hit.astype(BF16)
    pos_part = jnp.dot(hit, tiles_hi, preferred_element_type=F32) + jnp.dot(
        hit, tiles_lo, preferred_element_type=F32
    )
    weights, cluster_live, share_hit, pos_part, tiles_hi, tiles_lo = lax.optimization_barrier(
        (weights, cluster_live, share_hit, pos_part, tiles_hi, tiles_lo)
    )

    near_a, near_b, near_hidden, near_slope = forward(diag_tok, near_tok, weights)
    near_sum = (near_b + swap_core(near_a).astype(F32)).astype(BF16)
    near_sum, pos_part = lax.optimization_barrier((near_sum, pos_part))
    from_near = swap_near(near_sum)
    pos_got = gather_chips(pos_part.reshape(16, docs, width))
    own_a, own_b, own_hidden, own_slope = forward(core_tok, own_tok, weights)
    from_near, pos_got = lax.optimization_barrier((from_near, pos_got))
    own_rows, emb = pl.pallas_call(
        norm_kernel,
        out_shape=(shape((256, 1152), BF16), shape((128, width), BF16)),
        in_specs=[SCALARS] + [WHOLE] * 5,
        out_specs=(WHOLE, WHOLE),
        compiler_params=LIMIT,
        cost_estimate=cost(2**22, 4 * 2**20),
    )(lengths, own_tok, own_b, swap_core(own_a), from_near, gain)

    plane_emb = gather_chips(emb.reshape(16, docs, width)).reshape(128, width)
    near_rows = swap_near(own_rows)
    packed, weighted = pl.pallas_call(
        score_kernel,
        out_shape=(shape((128, 1280), BF16), shape((128, 512), F32)),
        in_specs=[ANYWHERE] + [WHOLE] * 3,
        out_specs=(WHOLE, WHOLE),
        scratch_shapes=[pltpu.VMEM((128, width), BF16), pltpu.SemaphoreType.DMA],
        compiler_params=LIMIT,
        cost_estimate=cost(2**29, 3 * 2**20, 2**16),
    )(plane_emb, tiles_hi, tiles_lo, cluster_live)
    packed, near_rows = lax.optimization_barrier((packed, near_rows))
    core_rows, diag_rows = swap_core(own_rows), swap_core(near_rows)
    got = lax.all_to_all(packed.reshape(16, docs, 1280), CHIPS, 0, 0, tiled=True)
    emb_grad, loss, sums = pl.pallas_call(
        settle_kernel,
        out_shape=(shape((docs, width), F32), shape((docs, 128), F32), shape((docs, 128), F32)),
        in_specs=[SCALARS, ANYWHERE, ANYWHERE, WHOLE],
        out_specs=(WHOLE,) * 3,
        scratch_shapes=[
            pltpu.VMEM((16, docs, 1280), BF16),
            pltpu.VMEM((16, docs, width), F32),
            pltpu.SemaphoreType.DMA((2,)),
        ],
        compiler_params=LIMIT,
        cost_estimate=cost(2**20, 2**20),
    )(meta, got, pos_got, emb)
    loss = loss[:, 0]

    grads = (swap_diag(emb_grad), swap_near(emb_grad), swap_core(emb_grad), emb_grad)
    send = backward(
        grads,
        gain,
        (diag_rows, near_rows, core_rows, own_rows),
        (diag_tok, near_tok, core_tok, own_tok),
        (near_hidden, own_hidden),
        (near_slope, own_slope),
        weights,
    )
    send, weighted = lax.optimization_barrier((send, weighted))
    got = lax.all_to_all(send, CHIPS, 0, 0, tiled=True)
    part, keep, give = pl.pallas_call(
        total_kernel,
        out_shape=(shape((32, width), BF16), shape((32, 512), BF16), shape((32, 512), BF16)),
        grid=(4,),
        in_specs=[SCALARS, pl.BlockSpec((16, 16, width), lambda i: (0, i, 0))],
        out_specs=(
            pl.BlockSpec((16, width), lambda i: (jnp.minimum(i, 1), 0)),
            pl.BlockSpec((16, 512), lambda i: (jnp.maximum(i - 2, 0), 0)),
            pl.BlockSpec((16, 512), lambda i: (jnp.maximum(i - 2, 0), 0)),
        ),
        compiler_params=LIMIT,
        cost_estimate=cost(2**20, 2**21),
    )(meta, got)
    both = jnp.concatenate([part, jnp.concatenate([keep, swap_core(give)], axis=1)], axis=0)
    grad_in, grad_out = pl.pallas_call(
        place_kernel,
        out_shape=(shape((32, 2048), F32), shape((64, width), F32)),
        in_specs=[SCALARS] + [WHOLE] * 4,
        out_specs=(WHOLE, WHOLE),
        compiler_params=LIMIT,
        cost_estimate=cost(2**26, 2**20),
    )(meta, both, swap_near(both), swap_wrap(both), swap_far(both))

    all_sums = sums[:, :16].T.reshape(128)
    logit_grad = weighted / all_sums[:, None] - share_hit
    tile_part = lax.dot_general(
        logit_grad, plane_emb.astype(F32), FIRST, precision=lax.Precision.HIGH
    )
    tile_chip = (tile_part[:256] + swap_core(tile_part[256:])).astype(BF16)

    def add(a, swap):
        return a.astype(F32) + swap(a).astype(F32)

    tile_grad = jnp.concatenate(
        [
            add(add(tile_chip[:128], swap_near).astype(BF16), swap_wrap),
            add(add(tile_chip[128:], swap_wrap).astype(BF16), swap_near),
        ],
        axis=0,
    )
    new_mean = 0.9 * tile_mean + 0.1 * tile_grad
    new_var = 0.999 * tile_var + 0.001 * tile_grad * tile_grad
    new_tiles = label_tiles - 0.001 * (new_mean * CORR_ONE) / (jnp.sqrt(new_var * CORR_TWO) + 1e-08)
    return (loss, new_tiles, new_mean, new_var, grad_in, grad_out)


def solution(mesh):
    grid = Mesh(mesh.devices.reshape(2, 2, 4, 4, 2), ("h", "l", "x", "z", "c"))
    every, plane, group = ("h", "l", "x", "z", "c"), ("x", "z", "c"), ("h", "l")
    return jax.shard_map(
        on_device,
        mesh=grid,
        in_specs=(
            P(every, None, None),
            P(every),
            P(plane, None),
            P(plane, None),
            P(),
            P(plane, None),
            P(plane, None),
            P(plane, None),
            P(group, None),
            P(group, None),
            P(),
        ),
        out_specs=(
            P(every),
            P(plane, None),
            P(plane, None),
            P(plane, None),
            P(plane, None),
            P(plane, None),
        ),
        check_vma=False,
    )
```

```python
import jax
import jax.numpy as jnp
from jax import lax
from jax.experimental import pallas as pl
from jax.experimental.pallas import tpu as pltpu
from jax.sharding import Mesh, PartitionSpec as P

LPC = 4
POS = 4
POS_SCALE = 32768.0

NORM_EPS = 1e-05
INV_ROOT_TWO = 0.7071067811865476
INV_ROOT_TWO_PI = 0.3989422804014327
CORR_ONE = 1.000026562104397
CORR_TWO = 10.50333528

F32 = jnp.float32
BF16 = jnp.bfloat16
CHIPS = ("x", "z")
FIRST = (((0,), (0,)), ((), ()))
LAST = (((1,), (1,)), ((), ()))


def swap_core(a):
    return lax.ppermute(a, "c", [(0, 1), (1, 0)])


def swap_near(a):
    return lax.ppermute(a, "l", [(0, 1), (1, 0)])


def swap_diag(a):
    return lax.ppermute(a, ("l", "c"), [(0, 3), (3, 0), (1, 2), (2, 1)])


def swap_far(a):
    return lax.ppermute(a, "h", [(0, 1), (1, 0)])


def swap_wrap(a):
    return lax.ppermute(a, ("h", "l"), [(0, 3), (3, 0), (1, 2), (2, 1)])


def round_bf16(a):
    return lax.reduce_precision(a, 8, 7)


def gather_chips(a):
    return lax.all_to_all(a, CHIPS, 0, 0, tiled=True)


WHOLE = pl.BlockSpec(memory_space=pltpu.VMEM)
SCALARS = pl.BlockSpec(memory_space=pltpu.SMEM)
ANYWHERE = pl.BlockSpec(memory_space=pl.ANY)
LIMIT = pltpu.CompilerParams(vmem_limit_bytes=20 * 1024 * 1024)
MOST = pltpu.CompilerParams(vmem_limit_bytes=60 * 1024 * 1024)


def shape(dims, dtype):
    return jax.ShapeDtypeStruct(dims, dtype)


def cost(flops, data, special=0):
    return pl.CostEstimate(flops=flops, bytes_accessed=data, transcendentals=special)


def iota(dims, axis):
    return lax.broadcasted_iota(jnp.int32, dims, axis)


def pick_kernel(meta, w_in, mine, theirs):
    core, role = meta[0], meta[1]
    part = jnp.where(iota((512, 256), 1) < 128, core * 2 + role, 2 - core * 2 + role)
    at = iota((512, 256), 1) % 128
    spread = (iota((512, 256), 0) == at // 32 * 128 + part * 32 + at % 32).astype(BF16)
    for i in range(4):
        got = jnp.dot(w_in[:, i * 512 : i * 512 + 512], spread, preferred_element_type=F32).astype(BF16)
        mine[:, i * 128 : i * 128 + 128] = got[:, :128]
        theirs[:, i * 128 : i * 128 + 128] = got[:, 128:]


def lay_kernel(meta, mine, theirs, w_out, out, block, sems):
    core, role = meta[0], meta[1]
    block[:32] = jnp.where(role == 0, w_out[:32], w_out[32:])
    block[32:, :512] = jnp.where(core == 0, mine[...], theirs[...])
    block[32:, 512:] = jnp.where(core == 0, theirs[...], mine[...])
    copies = [pltpu.make_async_copy(block, out.at[i], sems.at[i]) for i in range(16)]
    for copy in copies:
        copy.start()
    for copy in copies:
        copy.wait()


def forward_kernel(tok_a, tok_b, weights, part_a, part_b, hidden, slope, w_in, w_out, sems):
    copies = [
        pltpu.make_async_copy(
            weights.at[:, 32:64, k * 512 : k * 512 + 512], w_in.at[:, k * 32 : k * 32 + 32], sems.at[k]
        )
        for k in range(2)
    ]
    copies.append(pltpu.make_async_copy(weights.at[:, 0:32], w_out, sems.at[2]))
    for copy in copies:
        copy.start()
    copies[0].wait()
    copies[1].wait()
    for k, (tok, part) in enumerate(((tok_a, part_a), (tok_b, part_b))):
        pre_act = jnp.dot(tok[...], w_in[...].reshape(1024, 512), preferred_element_type=F32)
        normal_cdf = 0.5 * (1.0 + lax.erf(pre_act * INV_ROOT_TWO))
        act = (pre_act * normal_cdf).astype(BF16)
        hidden[k * 256 : k * 256 + 256] = act
        slope[k * 256 : k * 256 + 256] = (
            normal_cdf + pre_act * jnp.exp(-0.5 * pre_act * pre_act) * INV_ROOT_TWO_PI
        )
        if k == 0:
            copies[2].wait()
        part[...] = jnp.dot(
            act, w_out[...].reshape(512, 1024), preferred_element_type=F32
        ).astype(part.dtype)


def forward(tok_a, tok_b, weights):
    return pl.pallas_call(
        forward_kernel,
        out_shape=(
            shape((256, 1024), BF16),
            shape((256, 1024), F32),
            shape((512, 512), BF16),
            shape((512, 512), F32),
        ),
        in_specs=[WHOLE, WHOLE, ANYWHERE],
        out_specs=(WHOLE,) * 4,
        scratch_shapes=[
            pltpu.VMEM((16, 64, 512), BF16),
            pltpu.VMEM((16, 32, 1024), BF16),
            pltpu.SemaphoreType.DMA((3,)),
        ],
        compiler_params=LIMIT,
        cost_estimate=cost(2**30, 6 * 2**20, 2**19),
    )(tok_a, tok_b, weights)


def norm_kernel(lengths, tok, part, from_core, from_near, gain, rows, emb_hbm, emb, sem):
    embs = []
    for d in range(8):
        at = pl.ds(d * 32, 32)
        summed = tok[at].astype(F32) + (
            part[at] + from_core[at].astype(F32) + from_near[at].astype(F32)
        )
        centred = summed - jnp.mean(summed, axis=-1, keepdims=True)
        inv = lax.rsqrt(jnp.mean(centred * centred, axis=-1, keepdims=True) + NORM_EPS)
        normed = centred * inv
        count = jnp.full((32, 1), lengths[d], jnp.int32).astype(F32)
        share = jnp.where(iota((32, 1), 0).astype(F32) < count, 1.0, 0.0) / count
        embs.append(jnp.sum(normed * gain[...] * share, axis=0, keepdims=True))
        high = inv.astype(BF16).astype(F32)
        lane = iota((32, 128), 1)
        extra = jnp.where(lane == 0, high, jnp.where(lane == 1, inv - high, jnp.where(lane == 2, count, 0.0)))
        rows[at, :1024] = normed.astype(BF16)
        rows[at, 1024:] = extra.astype(BF16)
    docs = jnp.concatenate(embs, axis=0)
    emb[...] = jnp.concatenate([docs] * 16, axis=0).astype(BF16)
    copy = pltpu.make_async_copy(emb, emb_hbm, sem)
    copy.start()
    copy.wait()


def score_kernel(emb, tiles_hi, tiles_lo, live, packed_hbm, weighted, emb_buf, packed, sem):
    copy = pltpu.make_async_copy(emb, emb_buf, sem)
    copy.start()
    grow = (iota((128, 512), 0) == iota((128, 512), 1) // LPC).astype(BF16)
    mask = jnp.dot(live[...], grow, preferred_element_type=F32)
    copy.wait()
    docs = emb_buf[...]
    scores = lax.dot_general(docs, tiles_hi[...], LAST, preferred_element_type=F32)
    scores = scores + lax.dot_general(docs, tiles_lo[...], LAST, preferred_element_type=F32)
    value = mask * jnp.exp(scores)
    weighted[...] = value
    value_hi = value.astype(BF16)
    value_lo = (value - value_hi.astype(F32)).astype(BF16)
    part_emb = jnp.dot(value_hi, tiles_hi[...], preferred_element_type=F32)
    part_emb = part_emb + jnp.dot(value_hi, tiles_lo[...], preferred_element_type=F32)
    part_emb = part_emb + jnp.dot(value_lo, tiles_hi[...], preferred_element_type=F32)
    sums = jnp.sum(value, axis=1, keepdims=True) * 0.5
    high = sums.astype(BF16).astype(F32)
    row, lane = iota((128, 128), 0), iota((128, 128), 1)
    chosen = row // 8 == lane
    same = (row % 8 == lane % 8).astype(BF16)
    for k, part in enumerate((high, sums - high)):
        table = jnp.where(chosen, part, 0.0).astype(BF16)
        packed[:, 1024 + k * 128 : 1152 + k * 128] = jnp.dot(
            same, table, preferred_element_type=F32
        ).astype(BF16)
    packed[:, :1024] = part_emb.astype(BF16)
    copy = pltpu.make_async_copy(packed, packed_hbm, sem)
    copy.start()
    copy.wait()


def settle_kernel(meta, got_hbm, pos, emb, grad, loss, sums, got, sem):
    copy = pltpu.make_async_copy(got_hbm, got, sem)
    copy.start()
    copy.wait()
    total = got[0].astype(F32)
    for i in range(1, 16):
        total = total + got[i].astype(F32)
    every = (total[:, 1024:1152] + total[:, 1152:1280]) * 2.0
    sums[...] = every
    expsum = jnp.sum(jnp.where(iota((8, 128), 1) == meta[2], every, 0.0), axis=1, keepdims=True)
    pos_mean = pos[...]
    grad[...] = total[:, :1024] / expsum - pos_mean
    picked = jnp.sum(emb[...].astype(F32)[:8] * pos_mean, axis=1, keepdims=True)
    loss[...] = jnp.broadcast_to(jnp.log(expsum) - picked, (8, 128))


def tile_kernel(sums, weighted, share_hit, emb, own, other):
    rows = jnp.concatenate([sums[...]] * 16, axis=0)
    chosen = iota((128, 128), 0) // 8 == iota((128, 128), 1)
    column = jnp.sum(jnp.where(chosen, rows, 0.0), axis=1, keepdims=True)
    grad = weighted[...] / column - share_hit[...]
    grad_hi = grad.astype(BF16)
    grad_lo = (grad - grad_hi.astype(F32)).astype(BF16)
    for k, out in enumerate((own, other)):
        at = slice(k * 256, k * 256 + 256)
        part = lax.dot_general(grad_hi[:, at], emb[...], FIRST, preferred_element_type=F32)
        part = part + lax.dot_general(grad_lo[:, at], emb[...], FIRST, preferred_element_type=F32)
        out[...] = part.astype(out.dtype)


def backward_kernel(*refs):
    grads, gain = refs[:4], refs[4]
    rows, toks = refs[5:9], refs[9:13]
    hiddens, slopes, weights, out = refs[13:15], refs[15:17], refs[17], refs[18]
    row_buf, tok_buf, hid_buf, slope_buf, w_out, sum_grad, act_grad, result, sems = refs[19:]
    sent = []
    first = pltpu.make_async_copy(weights.at[:, 0:32], w_out, sems.at[0])
    first.start()
    row_copies, tok_copies, hid_copies, slope_copies = [], [], [], []
    for k in range(4):
        at = pl.ds(k * 256, 256)
        row_copies.append(pltpu.make_async_copy(rows[k], row_buf.at[at], sems.at[1 + k]))
        row_copies[k].start()
    for k in range(2):
        at = pl.ds(k * 512, 512)
        slope_copies.append(pltpu.make_async_copy(slopes[k], slope_buf.at[at], sems.at[5 + k]))
        slope_copies[k].start()
    for k in range(2):
        at = pl.ds(k * 512, 512)
        hid_copies.append(pltpu.make_async_copy(hiddens[k], hid_buf.at[at], sems.at[7 + k]))
        hid_copies[k].start()
    for k in range(4):
        at = pl.ds(k * 256, 256)
        tok_copies.append(pltpu.make_async_copy(toks[k], tok_buf.at[at], sems.at[9 + k]))
        tok_copies[k].start()
    for k in range(4):
        row_copies[k].wait()
        scaled_grad = grads[k][...] * gain[...]
        grad_mean = jnp.mean(scaled_grad, axis=-1, keepdims=True)
        for d in range(8):
            at = pl.ds(k * 256 + d * 32, 32)
            norm = row_buf[at, :1024].astype(F32)
            extra = row_buf[at, 1024:].astype(F32)
            lane = iota((32, 128), 1)
            scale = jnp.sum(jnp.where(lane < 2, extra, 0.0), axis=1, keepdims=True)
            count = jnp.sum(jnp.where(lane == 2, extra, 0.0), axis=1, keepdims=True)
            share = jnp.where(iota((32, 1), 0).astype(F32) < count, 1.0, 0.0) / count
            grad = scaled_grad[d : d + 1]
            along = jnp.mean(grad * norm, axis=-1, keepdims=True)
            sum_grad[at] = (
                (grad - grad_mean[d : d + 1] - norm * along) * (share * scale)
            ).astype(BF16)
        if k == 0:
            first.wait()
        if k % 2 == 0:
            slope_copies[k // 2].wait()
        at = pl.ds(k * 256, 256)
        back = lax.dot_general(
            sum_grad[at], w_out[...].reshape(512, 1024), LAST, preferred_element_type=F32
        )
        act_grad[at] = (back * slope_buf[at]).astype(BF16)
    for copy in hid_copies:
        copy.wait()
    for i in range(4):
        part = lax.dot_general(
            hid_buf[:, i * 128 : i * 128 + 128], sum_grad[...], FIRST, preferred_element_type=F32
        )
        at = pl.ds(i * 4, 4)
        result[at, :32] = part.astype(BF16).reshape(4, 32, 1024)
        sent.append(pltpu.make_async_copy(result.at[at, 0:32], out.at[at, 0:32], sems.at[13 + i]))
        sent[-1].start()
    for copy in tok_copies:
        copy.wait()
    for i in range(4):
        part = lax.dot_general(
            tok_buf[:, i * 256 : i * 256 + 256], act_grad[...], FIRST, preferred_element_type=F32
        ).astype(BF16).reshape(4, 2, 32, 512)
        at = pl.ds(i * 4, 4)
        result[at, 32:, :512] = part[:, 0]
        result[at, 32:, 512:] = part[:, 1]
        sent.append(pltpu.make_async_copy(result.at[at, 32:64], out.at[at, 32:64], sems.at[17 + i]))
        sent[-1].start()
    for copy in sent:
        copy.wait()


def backward(grads, gain, rows, toks, hiddens, slopes, weights):
    return pl.pallas_call(
        backward_kernel,
        out_shape=shape((16, 64, 1024), BF16),
        in_specs=[WHOLE] * 5 + [ANYWHERE] * 13,
        out_specs=ANYWHERE,
        scratch_shapes=[
            pltpu.VMEM((1024, 1152), BF16),
            pltpu.VMEM((1024, 1024), BF16),
            pltpu.VMEM((1024, 512), BF16),
            pltpu.VMEM((1024, 512), F32),
            pltpu.VMEM((16, 32, 1024), BF16),
            pltpu.VMEM((1024, 1024), BF16),
            pltpu.VMEM((1024, 512), BF16),
            pltpu.VMEM((16, 64, 1024), BF16),
            pltpu.SemaphoreType.DMA((21,)),
        ],
        compiler_params=MOST,
        cost_estimate=cost(3 * 2**30, 10 * 2**20),
    )(*grads, gain, *rows, *toks, *hiddens, *slopes, weights)


def total_kernel(meta, got, out, keep, give):
    total = got[0].astype(F32)
    for i in range(1, 16):
        total = total + got[i].astype(F32)
    total = total.astype(BF16)
    core, step = meta[0], pl.program_id(0)

    @pl.when(step < 2)
    def _():
        out[...] = total

    @pl.when(step >= 2)
    def _():
        keep[...] = jnp.where(core == 0, total[:, :512], total[:, 512:])
        give[...] = jnp.where(core == 0, total[:, 512:], total[:, :512])


def place_kernel(meta, own, near, wrap, far, grad_in, grad_out):
    core, role = meta[0], meta[1]
    mine = own[:32].astype(F32) + wrap[:32].astype(F32)
    theirs = near[:32].astype(F32) + far[:32].astype(F32)
    grad_out[:32] = jnp.where(role == 0, mine, theirs)
    grad_out[32:] = jnp.where(role == 0, theirs, mine)
    row, lane = iota((1024, 512), 0), iota((1024, 512), 1)
    piece, at = row // 128, row % 128
    swapped, flipped = piece % 2, piece // 4
    part = (core + swapped - 2 * core * swapped) * 2 + (role + flipped - 2 * role * flipped)
    spread = (lane == at // 32 * 128 + part * 32 + at % 32).astype(BF16)
    blocks = [
        jnp.concatenate(
            [
                a[32:, k * 512 + i * 128 : k * 512 + i * 128 + 128]
                for a in (own, wrap, near, far)
                for k in range(2)
            ],
            axis=1,
        )
        for i in range(4)
    ]
    placed = jnp.dot(jnp.concatenate(blocks, axis=0), spread, preferred_element_type=F32)
    for i in range(4):
        grad_in[:, i * 512 : i * 512 + 512] = placed[i * 32 : i * 32 + 32]


def on_device(
    states,
    lengths,
    w_in,
    w_out,
    norm_gain,
    label_tiles,
    tile_mean,
    tile_var,
    shortlist,
    positives,
    owner_map,
):
    docs, length, width = states.shape
    core = lax.axis_index("c")
    high, low = lax.axis_index("h"), lax.axis_index("l")
    role = high + low - 2 * high * low
    chip = lax.axis_index("x") * 4 + lax.axis_index("z")
    meta = jnp.stack([core, role, chip]).astype(jnp.int32)
    gain = norm_gain.reshape(1, width)
    own_tok = states.reshape(docs * length, width)

    mine, theirs = pl.pallas_call(
        pick_kernel,
        out_shape=(shape((32, 512), BF16),) * 2,
        in_specs=[SCALARS, WHOLE],
        out_specs=(WHOLE, WHOLE),
        cost_estimate=cost(2**25, 2**18),
    )(meta, w_in)
    weights = gather_chips(
        pl.pallas_call(
            lay_kernel,
            out_shape=shape((16, 64, width), BF16),
            in_specs=[SCALARS, WHOLE, WHOLE, WHOLE],
            out_specs=ANYWHERE,
            scratch_shapes=[pltpu.VMEM((64, width), BF16), pltpu.SemaphoreType.DMA((16,))],
            cost_estimate=cost(0, 2**21),
        )(meta, mine, swap_core(theirs), w_out)
    )

    core_tok, near_tok, diag_tok = swap_core(own_tok), swap_near(own_tok), swap_diag(own_tok)

    oth_tiles = swap_core(label_tiles)
    slots = jnp.concatenate(
        [(chip * 2 + core) * 64 + jnp.arange(64), (chip * 2 + 1 - core) * 64 + jnp.arange(64)]
    ).astype(jnp.int32)
    all_clusters = jnp.arange(owner_map.shape[0], dtype=jnp.int32)
    owner_match = owner_map[:, None] == slots[None, :]
    cluster_ids = jnp.sum(jnp.where(owner_match, all_clusters[:, None], 0), axis=0)
    pick = lambda a: lax.dynamic_index_in_dim(a.reshape(16, 2, 8, -1), core, 1, False).reshape(128, -1)
    short, posit = pick(shortlist), pick(positives)
    cluster_live = jnp.max(
        (short[:, :, None] == cluster_ids[None, None, :]).astype(F32), axis=1
    ).astype(BF16)
    tiles = jnp.concatenate([label_tiles, oth_tiles], axis=0)
    tiles_top = round_bf16(tiles)
    tiles_hi, tiles_lo = tiles_top.astype(BF16), (tiles - tiles_top).astype(BF16)
    cluster_hit = (posit[:, :, None] // LPC == cluster_ids[None, None, :]).astype(F32)
    offset_hit = (
        posit[:, :, None] % LPC == jnp.arange(LPC, dtype=jnp.int32)[None, None, :]
    ).astype(F32)
    hits = jnp.sum(cluster_hit[:, :, :, None] * offset_hit[:, :, None, :], axis=1).reshape(128, 512)
    share_hit = hits / POS
    hit = share_hit.astype(BF16)
    pos_part = jnp.dot(hit, tiles_hi, preferred_element_type=F32) + jnp.dot(
        hit, tiles_lo, preferred_element_type=F32
    )
    pos_part = (pos_part * POS_SCALE).astype(jnp.float16)
    weights, cluster_live, share_hit, pos_part, tiles_hi, tiles_lo = lax.optimization_barrier(
        (weights, cluster_live, share_hit, pos_part, tiles_hi, tiles_lo)
    )

    near_a, near_b, near_hidden, near_slope = forward(diag_tok, near_tok, weights)
    near_sum = (near_b + swap_core(near_a).astype(F32)).astype(BF16)
    near_sum, pos_part = lax.optimization_barrier((near_sum, pos_part))
    from_near = swap_near(near_sum)
    pos_got = gather_chips(pos_part.reshape(16, docs, width))
    own_a, own_b, own_hidden, own_slope = forward(core_tok, own_tok, weights)
    from_near, pos_got = lax.optimization_barrier((from_near, pos_got))
    pos_mean = jnp.sum(pos_got.astype(F32), axis=0) * (1.0 / POS_SCALE)
    own_rows, emb = pl.pallas_call(
        norm_kernel,
        out_shape=(shape((256, 1152), BF16), shape((128, width), BF16)),
        in_specs=[SCALARS] + [WHOLE] * 5,
        out_specs=(WHOLE, ANYWHERE),
        scratch_shapes=[pltpu.VMEM((128, width), BF16), pltpu.SemaphoreType.DMA],
        compiler_params=LIMIT,
        cost_estimate=cost(2**22, 4 * 2**20),
    )(lengths, own_tok, own_b, swap_core(own_a), from_near, gain)

    plane_emb = gather_chips(emb.reshape(16, docs, width)).reshape(128, width)
    near_rows = swap_near(own_rows)
    packed, weighted = pl.pallas_call(
        score_kernel,
        out_shape=(shape((128, 1280), BF16), shape((128, 512), F32)),
        in_specs=[ANYWHERE] + [WHOLE] * 3,
        out_specs=(ANYWHERE, WHOLE),
        scratch_shapes=[
            pltpu.VMEM((128, width), BF16),
            pltpu.VMEM((128, 1280), BF16),
            pltpu.SemaphoreType.DMA,
        ],
        compiler_params=LIMIT,
        cost_estimate=cost(2**29, 3 * 2**20, 2**16),
    )(plane_emb, tiles_hi, tiles_lo, cluster_live)
    packed, near_rows = lax.optimization_barrier((packed, near_rows))
    core_rows, diag_rows = swap_core(own_rows), swap_core(near_rows)
    got = lax.all_to_all(packed.reshape(16, docs, 1280), CHIPS, 0, 0, tiled=True)
    emb_grad, loss, sums = pl.pallas_call(
        settle_kernel,
        out_shape=(shape((docs, width), F32), shape((docs, 128), F32), shape((docs, 128), F32)),
        in_specs=[SCALARS, ANYWHERE, WHOLE, WHOLE],
        out_specs=(WHOLE,) * 3,
        scratch_shapes=[
            pltpu.VMEM((16, docs, 1280), BF16),
            pltpu.SemaphoreType.DMA,
        ],
        compiler_params=LIMIT,
        cost_estimate=cost(2**20, 2**20),
    )(meta, got, pos_mean, emb)
    loss = loss[:, 0]

    grads = (swap_diag(emb_grad), swap_near(emb_grad), swap_core(emb_grad), emb_grad)
    send = backward(
        grads,
        gain,
        (diag_rows, near_rows, core_rows, own_rows),
        (diag_tok, near_tok, core_tok, own_tok),
        (near_hidden, own_hidden),
        (near_slope, own_slope),
        weights,
    )
    got = lax.all_to_all(send, CHIPS, 0, 0, tiled=True)
    part, keep, give = pl.pallas_call(
        total_kernel,
        out_shape=(shape((32, width), BF16), shape((32, 512), BF16), shape((32, 512), BF16)),
        grid=(4,),
        in_specs=[SCALARS, pl.BlockSpec((16, 16, width), lambda i: (0, i, 0))],
        out_specs=(
            pl.BlockSpec((16, width), lambda i: (jnp.minimum(i, 1), 0)),
            pl.BlockSpec((16, 512), lambda i: (jnp.maximum(i - 2, 0), 0)),
            pl.BlockSpec((16, 512), lambda i: (jnp.maximum(i - 2, 0), 0)),
        ),
        compiler_params=LIMIT,
        cost_estimate=cost(2**20, 2**21),
    )(meta, got)
    both = jnp.concatenate([part, jnp.concatenate([keep, swap_core(give)], axis=1)], axis=0)
    grad_in, grad_out = pl.pallas_call(
        place_kernel,
        out_shape=(shape((32, 2048), F32), shape((64, width), F32)),
        in_specs=[SCALARS] + [WHOLE] * 4,
        out_specs=(WHOLE, WHOLE),
        compiler_params=LIMIT,
        cost_estimate=cost(2**26, 2**20),
    )(meta, both, swap_near(both), swap_wrap(both), swap_far(both))

    tile_own, tile_other = pl.pallas_call(
        tile_kernel,
        out_shape=(shape((256, width), F32), shape((256, width), BF16)),
        in_specs=[WHOLE] * 4,
        out_specs=(WHOLE, WHOLE),
        compiler_params=LIMIT,
        cost_estimate=cost(2**28, 2**21),
    )(sums, weighted, share_hit, plane_emb)
    tile_chip = (tile_own + swap_core(tile_other).astype(F32)).astype(BF16)

    def add(a, swap):
        return a.astype(F32) + swap(a).astype(F32)

    tile_grad = jnp.concatenate(
        [
            add(add(tile_chip[:128], swap_near).astype(BF16), swap_wrap),
            add(add(tile_chip[128:], swap_wrap).astype(BF16), swap_near),
        ],
        axis=0,
    )
    new_mean = 0.9 * tile_mean + 0.1 * tile_grad
    new_var = 0.999 * tile_var + 0.001 * tile_grad * tile_grad
    new_tiles = label_tiles - 0.001 * (new_mean * CORR_ONE) / (jnp.sqrt(new_var * CORR_TWO) + 1e-08)
    return (loss, new_tiles, new_mean, new_var, grad_in, grad_out)


def solution(mesh):
    grid = Mesh(mesh.devices.reshape(2, 2, 4, 4, 2), ("h", "l", "x", "z", "c"))
    every, plane, group = ("h", "l", "x", "z", "c"), ("x", "z", "c"), ("h", "l")
    return jax.shard_map(
        on_device,
        mesh=grid,
        in_specs=(
            P(every, None, None),
            P(every),
            P(plane, None),
            P(plane, None),
            P(),
            P(plane, None),
            P(plane, None),
            P(plane, None),
            P(group, None),
            P(group, None),
            P(),
        ),
        out_specs=(
            P(every),
            P(plane, None),
            P(plane, None),
            P(plane, None),
            P(plane, None),
            P(plane, None),
        ),
        check_vma=False,
    )
```

```python
import jax
import jax.numpy as jnp
from jax import lax
from jax.experimental import pallas as pl
from jax.experimental.pallas import tpu as pltpu
from jax.sharding import Mesh, PartitionSpec as P

LPC = 4
POS = 4
POS_SCALE = 32768.0

NORM_EPS = 1e-05
INV_ROOT_TWO = 0.7071067811865476
INV_ROOT_TWO_PI = 0.3989422804014327
CORR_ONE = 1.000026562104397
CORR_TWO = 10.50333528

F32 = jnp.float32
BF16 = jnp.bfloat16
CHIPS = ("x", "z")
FIRST = (((0,), (0,)), ((), ()))
LAST = (((1,), (1,)), ((), ()))


def swap_core(a):
    return lax.ppermute(a, "c", [(0, 1), (1, 0)])


def swap_near(a):
    return lax.ppermute(a, "l", [(0, 1), (1, 0)])


def swap_diag(a):
    return lax.ppermute(a, ("l", "c"), [(0, 3), (3, 0), (1, 2), (2, 1)])


def swap_far(a):
    return lax.ppermute(a, "h", [(0, 1), (1, 0)])


def swap_wrap(a):
    return lax.ppermute(a, ("h", "l"), [(0, 3), (3, 0), (1, 2), (2, 1)])


def round_bf16(a):
    return lax.reduce_precision(a, 8, 7)


def gather_chips(a):
    return lax.all_to_all(a, CHIPS, 0, 0, tiled=True)


WHOLE = pl.BlockSpec(memory_space=pltpu.VMEM)
SCALARS = pl.BlockSpec(memory_space=pltpu.SMEM)
ANYWHERE = pl.BlockSpec(memory_space=pl.ANY)
LIMIT = pltpu.CompilerParams(vmem_limit_bytes=20 * 1024 * 1024)
MOST = pltpu.CompilerParams(vmem_limit_bytes=60 * 1024 * 1024)


def shape(dims, dtype):
    return jax.ShapeDtypeStruct(dims, dtype)


def cost(flops, data, special=0):
    return pl.CostEstimate(flops=flops, bytes_accessed=data, transcendentals=special)


def iota(dims, axis):
    return lax.broadcasted_iota(jnp.int32, dims, axis)


def pick_kernel(meta, w_in, mine, theirs):
    core, role = meta[0], meta[1]
    part = jnp.where(iota((512, 256), 1) < 128, core * 2 + role, 2 - core * 2 + role)
    at = iota((512, 256), 1) % 128
    spread = (iota((512, 256), 0) == at // 32 * 128 + part * 32 + at % 32).astype(BF16)
    for i in range(4):
        got = jnp.dot(w_in[:, i * 512 : i * 512 + 512], spread, preferred_element_type=F32).astype(BF16)
        mine[:, i * 128 : i * 128 + 128] = got[:, :128]
        theirs[:, i * 128 : i * 128 + 128] = got[:, 128:]


def lay_kernel(meta, mine, theirs, w_out, out, block, sems):
    core, role = meta[0], meta[1]
    block[:32] = jnp.where(role == 0, w_out[:32], w_out[32:])
    block[32:, :512] = jnp.where(core == 0, mine[...], theirs[...])
    block[32:, 512:] = jnp.where(core == 0, theirs[...], mine[...])
    copies = [pltpu.make_async_copy(block, out.at[i], sems.at[i]) for i in range(16)]
    for copy in copies:
        copy.start()
    for copy in copies:
        copy.wait()


def forward_kernel(tok_a, tok_b, weights, part_a, part_b, hidden, slope, w_in, w_out, sems):
    copies = [
        pltpu.make_async_copy(
            weights.at[:, 32:64, k * 512 : k * 512 + 512], w_in.at[:, k * 32 : k * 32 + 32], sems.at[k]
        )
        for k in range(2)
    ]
    copies.append(pltpu.make_async_copy(weights.at[:, 0:32], w_out, sems.at[2]))
    for copy in copies:
        copy.start()
    copies[0].wait()
    copies[1].wait()
    for k, (tok, part) in enumerate(((tok_a, part_a), (tok_b, part_b))):
        pre_act = jnp.dot(tok[...], w_in[...].reshape(1024, 512), preferred_element_type=F32)
        normal_cdf = 0.5 * (1.0 + lax.erf(pre_act * INV_ROOT_TWO))
        act = (pre_act * normal_cdf).astype(BF16)
        hidden[k * 256 : k * 256 + 256] = act
        slope[k * 256 : k * 256 + 256] = (
            normal_cdf + pre_act * jnp.exp(-0.5 * pre_act * pre_act) * INV_ROOT_TWO_PI
        )
        if k == 0:
            copies[2].wait()
        part[...] = jnp.dot(
            act, w_out[...].reshape(512, 1024), preferred_element_type=F32
        ).astype(part.dtype)


def forward(tok_a, tok_b, weights, flops):
    return pl.pallas_call(
        forward_kernel,
        out_shape=(
            shape((256, 1024), BF16),
            shape((256, 1024), F32),
            shape((512, 512), BF16),
            shape((512, 512), F32),
        ),
        in_specs=[WHOLE, WHOLE, ANYWHERE],
        out_specs=(WHOLE,) * 4,
        scratch_shapes=[
            pltpu.VMEM((16, 64, 512), BF16),
            pltpu.VMEM((16, 32, 1024), BF16),
            pltpu.SemaphoreType.DMA((3,)),
        ],
        compiler_params=LIMIT,
        cost_estimate=cost(flops, 6 * 2**20, 2**19),
    )(tok_a, tok_b, weights)


def norm_kernel(lengths, tok, part, from_core, from_near, gain, rows, emb_hbm, emb, sem):
    embs = []
    for d in range(8):
        at = pl.ds(d * 32, 32)
        summed = tok[at].astype(F32) + (
            part[at] + from_core[at].astype(F32) + from_near[at].astype(F32)
        )
        centred = summed - jnp.mean(summed, axis=-1, keepdims=True)
        inv = lax.rsqrt(jnp.mean(centred * centred, axis=-1, keepdims=True) + NORM_EPS)
        normed = centred * inv
        count = jnp.full((32, 1), lengths[d], jnp.int32).astype(F32)
        share = jnp.where(iota((32, 1), 0).astype(F32) < count, 1.0, 0.0) / count
        embs.append(jnp.sum(normed * gain[...] * share, axis=0, keepdims=True))
        high = inv.astype(BF16).astype(F32)
        lane = iota((32, 128), 1)
        extra = jnp.where(lane == 0, high, jnp.where(lane == 1, inv - high, jnp.where(lane == 2, count, 0.0)))
        rows[at, :1024] = normed.astype(BF16)
        rows[at, 1024:] = extra.astype(BF16)
    docs = jnp.concatenate(embs, axis=0)
    emb[...] = jnp.concatenate([docs] * 16, axis=0).astype(BF16)
    copy = pltpu.make_async_copy(emb, emb_hbm, sem)
    copy.start()
    copy.wait()


def score_kernel(emb, tiles_hi, tiles_lo, live, packed_hbm, weighted, emb_buf, packed, sem):
    copy = pltpu.make_async_copy(emb, emb_buf, sem)
    copy.start()
    grow = (iota((128, 512), 0) == iota((128, 512), 1) // LPC).astype(BF16)
    mask = jnp.dot(live[...], grow, preferred_element_type=F32)
    copy.wait()
    docs = emb_buf[...]
    scores = lax.dot_general(docs, tiles_hi[...], LAST, preferred_element_type=F32)
    scores = scores + lax.dot_general(docs, tiles_lo[...], LAST, preferred_element_type=F32)
    value = mask * jnp.exp(scores)
    weighted[...] = value
    value_hi = value.astype(BF16)
    value_lo = (value - value_hi.astype(F32)).astype(BF16)
    part_emb = jnp.dot(value_hi, tiles_hi[...], preferred_element_type=F32)
    part_emb = part_emb + jnp.dot(value_hi, tiles_lo[...], preferred_element_type=F32)
    part_emb = part_emb + jnp.dot(value_lo, tiles_hi[...], preferred_element_type=F32)
    sums = jnp.sum(value, axis=1, keepdims=True) * 0.5
    high = sums.astype(BF16).astype(F32)
    row, lane = iota((128, 128), 0), iota((128, 128), 1)
    chosen = row // 8 == lane
    same = (row % 8 == lane % 8).astype(BF16)
    for k, part in enumerate((high, sums - high)):
        table = jnp.where(chosen, part, 0.0).astype(BF16)
        packed[:, 1024 + k * 128 : 1152 + k * 128] = jnp.dot(
            same, table, preferred_element_type=F32
        ).astype(BF16)
    packed[:, :1024] = part_emb.astype(BF16)
    copy = pltpu.make_async_copy(packed, packed_hbm, sem)
    copy.start()
    copy.wait()


def settle_kernel(meta, got_hbm, pos, emb, grad, loss, sums, got, sem):
    copy = pltpu.make_async_copy(got_hbm, got, sem)
    copy.start()
    copy.wait()
    total = got[0].astype(F32)
    for i in range(1, 16):
        total = total + got[i].astype(F32)
    every = (total[:, 1024:1152] + total[:, 1152:1280]) * 2.0
    sums[...] = every
    expsum = jnp.sum(jnp.where(iota((8, 128), 1) == meta[2], every, 0.0), axis=1, keepdims=True)
    pos_mean = pos[...]
    grad[...] = total[:, :1024] / expsum - pos_mean
    picked = jnp.sum(emb[...].astype(F32)[:8] * pos_mean, axis=1, keepdims=True)
    loss[...] = jnp.broadcast_to(jnp.log(expsum) - picked, (8, 128))


def tile_kernel(sums, weighted, share_hit, emb, own, other):
    rows = jnp.concatenate([sums[...]] * 16, axis=0)
    chosen = iota((128, 128), 0) // 8 == iota((128, 128), 1)
    column = jnp.sum(jnp.where(chosen, rows, 0.0), axis=1, keepdims=True)
    grad = weighted[...] / column - share_hit[...]
    grad_hi = grad.astype(BF16)
    grad_lo = (grad - grad_hi.astype(F32)).astype(BF16)
    for k, out in enumerate((own, other)):
        at = slice(k * 256, k * 256 + 256)
        part = lax.dot_general(grad_hi[:, at], emb[...], FIRST, preferred_element_type=F32)
        part = part + lax.dot_general(grad_lo[:, at], emb[...], FIRST, preferred_element_type=F32)
        out[...] = part.astype(out.dtype)


def backward_kernel(*refs):
    grads, gain = refs[:4], refs[4]
    rows, toks = refs[5:9], refs[9:13]
    hiddens, slopes, weights, out = refs[13:15], refs[15:17], refs[17], refs[18]
    row_buf, tok_buf, hid_buf, slope_buf, w_out, sum_grad, act_grad, result, sems = refs[19:]
    sent = []
    first = pltpu.make_async_copy(weights.at[:, 0:32], w_out, sems.at[0])
    first.start()
    row_copies, tok_copies, hid_copies, slope_copies = [], [], [], []
    for k in range(4):
        at = pl.ds(k * 256, 256)
        row_copies.append(pltpu.make_async_copy(rows[k], row_buf.at[at], sems.at[1 + k]))
        row_copies[k].start()
    for k in range(2):
        at = pl.ds(k * 512, 512)
        slope_copies.append(pltpu.make_async_copy(slopes[k], slope_buf.at[at], sems.at[5 + k]))
        slope_copies[k].start()
    for k in range(2):
        at = pl.ds(k * 512, 512)
        hid_copies.append(pltpu.make_async_copy(hiddens[k], hid_buf.at[at], sems.at[7 + k]))
        hid_copies[k].start()
    for k in range(4):
        at = pl.ds(k * 256, 256)
        tok_copies.append(pltpu.make_async_copy(toks[k], tok_buf.at[at], sems.at[9 + k]))
        tok_copies[k].start()
    for k in range(4):
        row_copies[k].wait()
        scaled_grad = grads[k][...] * gain[...]
        grad_mean = jnp.mean(scaled_grad, axis=-1, keepdims=True)
        for d in range(8):
            at = pl.ds(k * 256 + d * 32, 32)
            norm = row_buf[at, :1024].astype(F32)
            extra = row_buf[at, 1024:].astype(F32)
            lane = iota((32, 128), 1)
            scale = jnp.sum(jnp.where(lane < 2, extra, 0.0), axis=1, keepdims=True)
            count = jnp.sum(jnp.where(lane == 2, extra, 0.0), axis=1, keepdims=True)
            share = jnp.where(iota((32, 1), 0).astype(F32) < count, 1.0, 0.0) / count
            grad = scaled_grad[d : d + 1]
            along = jnp.mean(grad * norm, axis=-1, keepdims=True)
            sum_grad[at] = (
                (grad - grad_mean[d : d + 1] - norm * along) * (share * scale)
            ).astype(BF16)
        if k == 0:
            first.wait()
        if k % 2 == 0:
            slope_copies[k // 2].wait()
        at = pl.ds(k * 256, 256)
        back = lax.dot_general(
            sum_grad[at], w_out[...].reshape(512, 1024), LAST, preferred_element_type=F32
        )
        act_grad[at] = (back * slope_buf[at]).astype(BF16)
    for copy in hid_copies:
        copy.wait()
    for i in range(4):
        part = lax.dot_general(
            hid_buf[:, i * 128 : i * 128 + 128], sum_grad[...], FIRST, preferred_element_type=F32
        )
        at = pl.ds(i * 4, 4)
        result[at, :32] = part.astype(BF16).reshape(4, 32, 1024)
        sent.append(pltpu.make_async_copy(result.at[at, 0:32], out.at[at, 0:32], sems.at[13 + i]))
        sent[-1].start()
    for copy in tok_copies:
        copy.wait()
    for i in range(4):
        part = lax.dot_general(
            tok_buf[:, i * 256 : i * 256 + 256], act_grad[...], FIRST, preferred_element_type=F32
        ).astype(BF16).reshape(4, 2, 32, 512)
        at = pl.ds(i * 4, 4)
        result[at, 32:, :512] = part[:, 0]
        result[at, 32:, 512:] = part[:, 1]
        sent.append(pltpu.make_async_copy(result.at[at, 32:64], out.at[at, 32:64], sems.at[17 + i]))
        sent[-1].start()
    for copy in sent:
        copy.wait()


def backward(grads, gain, rows, toks, hiddens, slopes, weights):
    return pl.pallas_call(
        backward_kernel,
        out_shape=shape((16, 64, 1024), BF16),
        in_specs=[WHOLE] * 5 + [ANYWHERE] * 13,
        out_specs=ANYWHERE,
        scratch_shapes=[
            pltpu.VMEM((1024, 1152), BF16),
            pltpu.VMEM((1024, 1024), BF16),
            pltpu.VMEM((1024, 512), BF16),
            pltpu.VMEM((1024, 512), F32),
            pltpu.VMEM((16, 32, 1024), BF16),
            pltpu.VMEM((1024, 1024), BF16),
            pltpu.VMEM((1024, 512), BF16),
            pltpu.VMEM((16, 64, 1024), BF16),
            pltpu.SemaphoreType.DMA((21,)),
        ],
        compiler_params=MOST,
        cost_estimate=cost(3 * 2**30, 10 * 2**20),
    )(*grads, gain, *rows, *toks, *hiddens, *slopes, weights)


def total_kernel(meta, got, out, keep, give):
    total = got[0].astype(F32)
    for i in range(1, 16):
        total = total + got[i].astype(F32)
    total = total.astype(BF16)
    core, step = meta[0], pl.program_id(0)

    @pl.when(step < 2)
    def _():
        out[...] = total

    @pl.when(step >= 2)
    def _():
        keep[...] = jnp.where(core == 0, total[:, :512], total[:, 512:])
        give[...] = jnp.where(core == 0, total[:, 512:], total[:, :512])


def place_kernel(meta, own, near, wrap, far, grad_in, grad_out):
    core, role = meta[0], meta[1]
    mine = own[:32].astype(F32) + wrap[:32].astype(F32)
    theirs = near[:32].astype(F32) + far[:32].astype(F32)
    grad_out[:32] = jnp.where(role == 0, mine, theirs)
    grad_out[32:] = jnp.where(role == 0, theirs, mine)
    row, lane = iota((1024, 512), 0), iota((1024, 512), 1)
    piece, at = row // 128, row % 128
    swapped, flipped = piece % 2, piece // 4
    part = (core + swapped - 2 * core * swapped) * 2 + (role + flipped - 2 * role * flipped)
    spread = (lane == at // 32 * 128 + part * 32 + at % 32).astype(BF16)
    blocks = [
        jnp.concatenate(
            [
                a[32:, k * 512 + i * 128 : k * 512 + i * 128 + 128]
                for a in (own, wrap, near, far)
                for k in range(2)
            ],
            axis=1,
        )
        for i in range(4)
    ]
    placed = jnp.dot(jnp.concatenate(blocks, axis=0), spread, preferred_element_type=F32)
    for i in range(4):
        grad_in[:, i * 512 : i * 512 + 512] = placed[i * 32 : i * 32 + 32]


def on_device(
    states,
    lengths,
    w_in,
    w_out,
    norm_gain,
    label_tiles,
    tile_mean,
    tile_var,
    shortlist,
    positives,
    owner_map,
):
    docs, length, width = states.shape
    core = lax.axis_index("c")
    high, low = lax.axis_index("h"), lax.axis_index("l")
    role = high + low - 2 * high * low
    chip = lax.axis_index("x") * 4 + lax.axis_index("z")
    meta = jnp.stack([core, role, chip]).astype(jnp.int32)
    gain = norm_gain.reshape(1, width)
    own_tok = states.reshape(docs * length, width)

    mine, theirs = pl.pallas_call(
        pick_kernel,
        out_shape=(shape((32, 512), BF16),) * 2,
        in_specs=[SCALARS, WHOLE],
        out_specs=(WHOLE, WHOLE),
        cost_estimate=cost(2**25, 2**18),
    )(meta, w_in)
    block = pl.pallas_call(
        lay_kernel,
        out_shape=shape((16, 64, width), BF16),
        in_specs=[SCALARS, WHOLE, WHOLE, WHOLE],
        out_specs=ANYWHERE,
        scratch_shapes=[pltpu.VMEM((64, width), BF16), pltpu.SemaphoreType.DMA((16,))],
        cost_estimate=cost(0, 2**21),
    )(meta, mine, swap_core(theirs), w_out)
    block, own_tok, label_tiles, shortlist, positives, owner_map = lax.optimization_barrier(
        (block, own_tok, label_tiles, shortlist, positives, owner_map)
    )
    weights = gather_chips(block)

    core_tok, near_tok, diag_tok = swap_core(own_tok), swap_near(own_tok), swap_diag(own_tok)

    oth_tiles = swap_core(label_tiles)
    slots = jnp.concatenate(
        [(chip * 2 + core) * 64 + jnp.arange(64), (chip * 2 + 1 - core) * 64 + jnp.arange(64)]
    ).astype(jnp.int32)
    all_clusters = jnp.arange(owner_map.shape[0], dtype=jnp.int32)
    owner_match = owner_map[:, None] == slots[None, :]
    cluster_ids = jnp.sum(jnp.where(owner_match, all_clusters[:, None], 0), axis=0)
    pick = lambda a: lax.dynamic_index_in_dim(a.reshape(16, 2, 8, -1), core, 1, False).reshape(128, -1)
    short, posit = pick(shortlist), pick(positives)
    cluster_live = jnp.max(
        (short[:, :, None] == cluster_ids[None, None, :]).astype(F32), axis=1
    ).astype(BF16)
    tiles = jnp.concatenate([label_tiles, oth_tiles], axis=0)
    tiles_top = round_bf16(tiles)
    tiles_hi, tiles_lo = tiles_top.astype(BF16), (tiles - tiles_top).astype(BF16)
    cluster_hit = (posit[:, :, None] // LPC == cluster_ids[None, None, :]).astype(F32)
    offset_hit = (
        posit[:, :, None] % LPC == jnp.arange(LPC, dtype=jnp.int32)[None, None, :]
    ).astype(F32)
    hits = jnp.sum(cluster_hit[:, :, :, None] * offset_hit[:, :, None, :], axis=1).reshape(128, 512)
    share_hit = hits / POS
    hit = share_hit.astype(BF16)
    pos_part = jnp.dot(hit, tiles_hi, preferred_element_type=F32) + jnp.dot(
        hit, tiles_lo, preferred_element_type=F32
    )
    pos_part = (pos_part * POS_SCALE).astype(jnp.float16)
    weights, cluster_live, share_hit, pos_part, tiles_hi, tiles_lo = lax.optimization_barrier(
        (weights, cluster_live, share_hit, pos_part, tiles_hi, tiles_lo)
    )

    near_a, near_b, near_hidden, near_slope = forward(diag_tok, near_tok, weights, 2**30)
    near_sum = (near_b + swap_core(near_a).astype(F32)).astype(BF16)
    near_sum, pos_part = lax.optimization_barrier((near_sum, pos_part))
    from_near = swap_near(near_sum)
    pos_got = gather_chips(pos_part.reshape(16, docs, width))
    own_a, own_b, own_hidden, own_slope = forward(core_tok, own_tok, weights, 2**36)
    from_near, pos_got = lax.optimization_barrier((from_near, pos_got))
    pos_mean = jnp.sum(pos_got.astype(F32), axis=0) * (1.0 / POS_SCALE)
    own_rows, emb = pl.pallas_call(
        norm_kernel,
        out_shape=(shape((256, 1152), BF16), shape((128, width), BF16)),
        in_specs=[SCALARS] + [WHOLE] * 5,
        out_specs=(WHOLE, ANYWHERE),
        scratch_shapes=[pltpu.VMEM((128, width), BF16), pltpu.SemaphoreType.DMA],
        compiler_params=LIMIT,
        cost_estimate=cost(2**22, 4 * 2**20),
    )(lengths, own_tok, own_b, swap_core(own_a), from_near, gain)

    plane_emb = gather_chips(emb.reshape(16, docs, width)).reshape(128, width)
    near_rows = swap_near(own_rows)
    packed, weighted = pl.pallas_call(
        score_kernel,
        out_shape=(shape((128, 1280), BF16), shape((128, 512), F32)),
        in_specs=[ANYWHERE] + [WHOLE] * 3,
        out_specs=(ANYWHERE, WHOLE),
        scratch_shapes=[
            pltpu.VMEM((128, width), BF16),
            pltpu.VMEM((128, 1280), BF16),
            pltpu.SemaphoreType.DMA,
        ],
        compiler_params=LIMIT,
        cost_estimate=cost(2**29, 3 * 2**20, 2**16),
    )(plane_emb, tiles_hi, tiles_lo, cluster_live)
    packed, near_rows = lax.optimization_barrier((packed, near_rows))
    core_rows, diag_rows = swap_core(own_rows), swap_core(near_rows)
    got = lax.all_to_all(packed.reshape(16, docs, 1280), CHIPS, 0, 0, tiled=True)
    emb_grad, loss, sums = pl.pallas_call(
        settle_kernel,
        out_shape=(shape((docs, width), F32), shape((docs, 128), F32), shape((docs, 128), F32)),
        in_specs=[SCALARS, ANYWHERE, WHOLE, WHOLE],
        out_specs=(WHOLE,) * 3,
        scratch_shapes=[
            pltpu.VMEM((16, docs, 1280), BF16),
            pltpu.SemaphoreType.DMA,
        ],
        compiler_params=LIMIT,
        cost_estimate=cost(2**20, 2**20),
    )(meta, got, pos_mean, emb)
    loss = loss[:, 0]

    grads = (swap_diag(emb_grad), swap_near(emb_grad), swap_core(emb_grad), emb_grad)
    send = backward(
        grads,
        gain,
        (diag_rows, near_rows, core_rows, own_rows),
        (diag_tok, near_tok, core_tok, own_tok),
        (near_hidden, own_hidden),
        (near_slope, own_slope),
        weights,
    )
    got = lax.all_to_all(send, CHIPS, 0, 0, tiled=True)
    part, keep, give = pl.pallas_call(
        total_kernel,
        out_shape=(shape((32, width), BF16), shape((32, 512), BF16), shape((32, 512), BF16)),
        grid=(4,),
        in_specs=[SCALARS, pl.BlockSpec((16, 16, width), lambda i: (0, i, 0))],
        out_specs=(
            pl.BlockSpec((16, width), lambda i: (jnp.minimum(i, 1), 0)),
            pl.BlockSpec((16, 512), lambda i: (jnp.maximum(i - 2, 0), 0)),
            pl.BlockSpec((16, 512), lambda i: (jnp.maximum(i - 2, 0), 0)),
        ),
        compiler_params=LIMIT,
        cost_estimate=cost(2**20, 2**21),
    )(meta, got)
    both = jnp.concatenate([part, jnp.concatenate([keep, swap_core(give)], axis=1)], axis=0)
    grad_in, grad_out = pl.pallas_call(
        place_kernel,
        out_shape=(shape((32, 2048), F32), shape((64, width), F32)),
        in_specs=[SCALARS] + [WHOLE] * 4,
        out_specs=(WHOLE, WHOLE),
        compiler_params=LIMIT,
        cost_estimate=cost(2**26, 2**20),
    )(meta, both, swap_near(both), swap_wrap(both), swap_far(both))

    tile_own, tile_other = pl.pallas_call(
        tile_kernel,
        out_shape=(shape((256, width), F32), shape((256, width), BF16)),
        in_specs=[WHOLE] * 4,
        out_specs=(WHOLE, WHOLE),
        compiler_params=LIMIT,
        cost_estimate=cost(2**28, 2**21),
    )(sums, weighted, share_hit, plane_emb)
    tile_chip = (tile_own + swap_core(tile_other).astype(F32)).astype(BF16)

    def add(a, swap):
        return a.astype(F32) + swap(a).astype(F32)

    tile_grad = jnp.concatenate(
        [
            add(add(tile_chip[:128], swap_near).astype(BF16), swap_wrap),
            add(add(tile_chip[128:], swap_wrap).astype(BF16), swap_near),
        ],
        axis=0,
    )
    new_mean = 0.9 * tile_mean + 0.1 * tile_grad
    new_var = 0.999 * tile_var + 0.001 * tile_grad * tile_grad
    new_tiles = label_tiles - 0.001 * (new_mean * CORR_ONE) / (jnp.sqrt(new_var * CORR_TWO) + 1e-08)
    return (loss, new_tiles, new_mean, new_var, grad_in, grad_out)


def solution(mesh):
    grid = Mesh(mesh.devices.reshape(2, 2, 4, 4, 2), ("h", "l", "x", "z", "c"))
    every, plane, group = ("h", "l", "x", "z", "c"), ("x", "z", "c"), ("h", "l")
    return jax.shard_map(
        on_device,
        mesh=grid,
        in_specs=(
            P(every, None, None),
            P(every),
            P(plane, None),
            P(plane, None),
            P(),
            P(plane, None),
            P(plane, None),
            P(plane, None),
            P(group, None),
            P(group, None),
            P(),
        ),
        out_specs=(
            P(every),
            P(plane, None),
            P(plane, None),
            P(plane, None),
            P(plane, None),
            P(plane, None),
        ),
        check_vma=False,
    )
```

```python
import jax
import jax.numpy as jnp
from jax import lax
from jax.experimental import pallas as pl
from jax.experimental.pallas import tpu as pltpu
from jax.sharding import Mesh, PartitionSpec as P

LPC = 4
POS = 4
POS_SCALE = 32768.0

NORM_EPS = 1e-05
INV_ROOT_TWO = 0.7071067811865476
INV_ROOT_TWO_PI = 0.3989422804014327
CORR_ONE = 1.000026562104397
CORR_TWO = 10.50333528

F32 = jnp.float32
BF16 = jnp.bfloat16
CHIPS = ("x", "z")
FIRST = (((0,), (0,)), ((), ()))
LAST = (((1,), (1,)), ((), ()))


def swap_core(a):
    return lax.ppermute(a, "c", [(0, 1), (1, 0)])


def swap_near(a):
    return lax.ppermute(a, "l", [(0, 1), (1, 0)])


def swap_diag(a):
    return lax.ppermute(a, ("l", "c"), [(0, 3), (3, 0), (1, 2), (2, 1)])


def swap_far(a):
    return lax.ppermute(a, "h", [(0, 1), (1, 0)])


def swap_wrap(a):
    return lax.ppermute(a, ("h", "l"), [(0, 3), (3, 0), (1, 2), (2, 1)])


def round_bf16(a):
    return lax.reduce_precision(a, 8, 7)


def gather_chips(a):
    return lax.all_to_all(a, CHIPS, 0, 0, tiled=True)


WHOLE = pl.BlockSpec(memory_space=pltpu.VMEM)
SCALARS = pl.BlockSpec(memory_space=pltpu.SMEM)
ANYWHERE = pl.BlockSpec(memory_space=pl.ANY)
LIMIT = pltpu.CompilerParams(vmem_limit_bytes=20 * 1024 * 1024)
MOST = pltpu.CompilerParams(vmem_limit_bytes=60 * 1024 * 1024)


def shape(dims, dtype):
    return jax.ShapeDtypeStruct(dims, dtype)


def cost(flops, data, special=0):
    return pl.CostEstimate(flops=flops, bytes_accessed=data, transcendentals=special)


def iota(dims, axis):
    return lax.broadcasted_iota(jnp.int32, dims, axis)


def place_of():
    core, high, low = (lax.axis_index(axis) for axis in ("c", "h", "l"))
    return core, high + low - 2 * high * low


def pick_kernel(w_in, mine, theirs):
    core, role = place_of()
    part = jnp.where(iota((512, 256), 1) < 128, core * 2 + role, 2 - core * 2 + role)
    at = iota((512, 256), 1) % 128
    spread = (iota((512, 256), 0) == at // 32 * 128 + part * 32 + at % 32).astype(BF16)
    for i in range(4):
        got = jnp.dot(w_in[:, i * 512 : i * 512 + 512], spread, preferred_element_type=F32).astype(BF16)
        mine[:, i * 128 : i * 128 + 128] = got[:, :128]
        theirs[:, i * 128 : i * 128 + 128] = got[:, 128:]


def lay_kernel(mine, theirs, w_out, out, block, sems):
    core, role = place_of()
    top = pltpu.make_async_copy(
        w_out.at[pl.ds(pl.multiple_of(role * 32, 32), 32)], block.at[0:32], sems.at[16]
    )
    top.start()
    block[32:, :512] = jnp.where(core == 0, mine[...], theirs[...])
    block[32:, 512:] = jnp.where(core == 0, theirs[...], mine[...])
    top.wait()
    copies = [pltpu.make_async_copy(block, out.at[i], sems.at[i]) for i in range(16)]
    for copy in copies:
        copy.start()
    for copy in copies:
        copy.wait()


def forward_kernel(tok, weights, part, hidden, slope, w_in, w_out, sems):
    copies = [
        pltpu.make_async_copy(
            weights.at[:, 32:64, k * 512 : k * 512 + 512], w_in.at[:, k * 32 : k * 32 + 32], sems.at[k]
        )
        for k in range(2)
    ]
    copies.append(pltpu.make_async_copy(weights.at[:, 0:32], w_out, sems.at[2]))
    for copy in copies:
        copy.start()
    copies[0].wait()
    copies[1].wait()
    pre_act = jnp.dot(tok[...], w_in[...].reshape(1024, 512), preferred_element_type=F32)
    normal_cdf = 0.5 * (1.0 + lax.erf(pre_act * INV_ROOT_TWO))
    act = (pre_act * normal_cdf).astype(BF16)
    copies[2].wait()
    part[...] = jnp.dot(
        act, w_out[...].reshape(512, 1024), preferred_element_type=F32
    ).astype(part.dtype)
    hidden[...] = act
    slope[...] = normal_cdf + pre_act * jnp.exp(-0.5 * pre_act * pre_act) * INV_ROOT_TWO_PI


def forward(tok, weights, dtype):
    return pl.pallas_call(
        forward_kernel,
        out_shape=(shape((256, 1024), dtype), shape((256, 512), BF16), shape((256, 512), F32)),
        in_specs=[WHOLE, ANYWHERE],
        out_specs=(WHOLE,) * 3,
        scratch_shapes=[
            pltpu.VMEM((16, 64, 512), BF16),
            pltpu.VMEM((16, 32, 1024), BF16),
            pltpu.SemaphoreType.DMA((3,)),
        ],
        compiler_params=LIMIT,
        cost_estimate=cost(2**32, 6 * 2**20, 2**18),
    )(tok, weights)


def norm_kernel(lengths, tok, part, from_core, from_near, gain, rows, emb_hbm, emb, sem):
    embs = []
    for d in range(8):
        at = pl.ds(d * 32, 32)
        summed = tok[at].astype(F32) + (
            part[at] + from_core[at].astype(F32) + from_near[at].astype(F32)
        )
        centred = summed - jnp.mean(summed, axis=-1, keepdims=True)
        inv = lax.rsqrt(jnp.mean(centred * centred, axis=-1, keepdims=True) + NORM_EPS)
        normed = centred * inv
        count = jnp.full((32, 1), lengths[d], jnp.int32).astype(F32)
        share = jnp.where(iota((32, 1), 0).astype(F32) < count, 1.0, 0.0) / count
        embs.append(jnp.sum(normed * gain[...] * share, axis=0, keepdims=True))
        high = inv.astype(BF16).astype(F32)
        lane = iota((32, 128), 1)
        extra = jnp.where(lane == 0, high, jnp.where(lane == 1, inv - high, jnp.where(lane == 2, count, 0.0)))
        rows[at, :1024] = normed.astype(BF16)
        rows[at, 1024:] = extra.astype(BF16)
    docs = jnp.concatenate(embs, axis=0)
    emb[...] = jnp.concatenate([docs] * 16, axis=0).astype(BF16)
    copy = pltpu.make_async_copy(emb, emb_hbm, sem)
    copy.start()
    copy.wait()


def score_kernel(emb, tiles_hi, tiles_lo, live, packed_hbm, weighted, emb_buf, packed, sem):
    copy = pltpu.make_async_copy(emb, emb_buf, sem)
    copy.start()
    grow = (iota((128, 512), 0) == iota((128, 512), 1) // LPC).astype(BF16)
    mask = jnp.dot(live[...], grow, preferred_element_type=F32)
    copy.wait()
    docs = emb_buf[...]
    scores = lax.dot_general(docs, tiles_hi[...], LAST, preferred_element_type=F32)
    scores = scores + lax.dot_general(docs, tiles_lo[...], LAST, preferred_element_type=F32)
    value = mask * jnp.exp(scores)
    weighted[...] = value
    value_hi = value.astype(BF16)
    value_lo = (value - value_hi.astype(F32)).astype(BF16)
    part_emb = jnp.dot(value_hi, tiles_hi[...], preferred_element_type=F32)
    part_emb = part_emb + jnp.dot(value_hi, tiles_lo[...], preferred_element_type=F32)
    part_emb = part_emb + jnp.dot(value_lo, tiles_hi[...], preferred_element_type=F32)
    sums = jnp.sum(value, axis=1, keepdims=True) * 0.5
    high = sums.astype(BF16).astype(F32)
    row, lane = iota((128, 128), 0), iota((128, 128), 1)
    chosen = row // 8 == lane
    same = (row % 8 == lane % 8).astype(BF16)
    for k, part in enumerate((high, sums - high)):
        table = jnp.where(chosen, part, 0.0).astype(BF16)
        packed[:, 1024 + k * 128 : 1152 + k * 128] = jnp.dot(
            same, table, preferred_element_type=F32
        ).astype(BF16)
    packed[:, :1024] = part_emb.astype(BF16)
    copy = pltpu.make_async_copy(packed, packed_hbm, sem)
    copy.start()
    copy.wait()


def settle_kernel(meta, got_hbm, pos, emb, grad, loss, sums, got, sem):
    copy = pltpu.make_async_copy(got_hbm, got, sem)
    copy.start()
    copy.wait()
    total = got[0].astype(F32)
    for i in range(1, 16):
        total = total + got[i].astype(F32)
    every = (total[:, 1024:1152] + total[:, 1152:1280]) * 2.0
    sums[...] = every
    expsum = jnp.sum(jnp.where(iota((8, 128), 1) == meta[2], every, 0.0), axis=1, keepdims=True)
    pos_mean = pos[...]
    grad[...] = total[:, :1024] / expsum - pos_mean
    picked = jnp.sum(emb[...].astype(F32)[:8] * pos_mean, axis=1, keepdims=True)
    loss[...] = jnp.broadcast_to(jnp.log(expsum) - picked, (8, 128))


def tile_kernel(sums, weighted, share_hit, emb, own, other):
    rows = jnp.concatenate([sums[...]] * 16, axis=0)
    chosen = iota((128, 128), 0) // 8 == iota((128, 128), 1)
    column = jnp.sum(jnp.where(chosen, rows, 0.0), axis=1, keepdims=True)
    grad = weighted[...] / column - share_hit[...]
    grad_hi = grad.astype(BF16)
    grad_lo = (grad - grad_hi.astype(F32)).astype(BF16)
    for k, out in enumerate((own, other)):
        at = slice(k * 256, k * 256 + 256)
        part = lax.dot_general(grad_hi[:, at], emb[...], FIRST, preferred_element_type=F32)
        part = part + lax.dot_general(grad_lo[:, at], emb[...], FIRST, preferred_element_type=F32)
        out[...] = part.astype(out.dtype)


def backward_kernel(*refs):
    grads, gain = refs[:4], refs[4]
    rows, toks = refs[5:9], refs[9:13]
    hiddens, slopes, weights, out = refs[13:17], refs[17:21], refs[21], refs[22]
    row_buf, tok_buf, hid_buf, slope_buf, w_out, sum_grad, act_grad, result, sems = refs[23:]
    sent = []
    first = pltpu.make_async_copy(weights.at[:, 0:32], w_out, sems.at[0])
    first.start()
    row_copies, tok_copies, hid_copies, slope_copies = [], [], [], []
    for k in range(4):
        at = pl.ds(k * 256, 256)
        row_copies.append(pltpu.make_async_copy(rows[k], row_buf.at[at], sems.at[1 + k]))
        row_copies[k].start()
    for k in range(4):
        at = pl.ds(k * 256, 256)
        slope_copies.append(pltpu.make_async_copy(slopes[k], slope_buf.at[at], sems.at[21 + k]))
        slope_copies[k].start()
    for k in range(4):
        at = pl.ds(k * 256, 256)
        hid_copies.append(pltpu.make_async_copy(hiddens[k], hid_buf.at[at], sems.at[5 + k]))
        hid_copies[k].start()
    for k in range(4):
        at = pl.ds(k * 256, 256)
        tok_copies.append(pltpu.make_async_copy(toks[k], tok_buf.at[at], sems.at[9 + k]))
        tok_copies[k].start()
    for k in range(4):
        row_copies[k].wait()
        scaled_grad = grads[k][...] * gain[...]
        grad_mean = jnp.mean(scaled_grad, axis=-1, keepdims=True)
        for d in range(8):
            at = pl.ds(k * 256 + d * 32, 32)
            norm = row_buf[at, :1024].astype(F32)
            extra = row_buf[at, 1024:].astype(F32)
            lane = iota((32, 128), 1)
            scale = jnp.sum(jnp.where(lane < 2, extra, 0.0), axis=1, keepdims=True)
            count = jnp.sum(jnp.where(lane == 2, extra, 0.0), axis=1, keepdims=True)
            share = jnp.where(iota((32, 1), 0).astype(F32) < count, 1.0, 0.0) / count
            grad = scaled_grad[d : d + 1]
            along = jnp.mean(grad * norm, axis=-1, keepdims=True)
            sum_grad[at] = (
                (grad - grad_mean[d : d + 1] - norm * along) * (share * scale)
            ).astype(BF16)
        if k == 0:
            first.wait()
        slope_copies[k].wait()
        at = pl.ds(k * 256, 256)
        back = lax.dot_general(
            sum_grad[at], w_out[...].reshape(512, 1024), LAST, preferred_element_type=F32
        )
        act_grad[at] = (back * slope_buf[at]).astype(BF16)
    for copy in hid_copies:
        copy.wait()
    for i in range(4):
        part = lax.dot_general(
            hid_buf[:, i * 128 : i * 128 + 128], sum_grad[...], FIRST, preferred_element_type=F32
        )
        at = pl.ds(i * 4, 4)
        result[at, :32] = part.astype(BF16).reshape(4, 32, 1024)
        sent.append(pltpu.make_async_copy(result.at[at, 0:32], out.at[at, 0:32], sems.at[13 + i]))
        sent[-1].start()
    for copy in tok_copies:
        copy.wait()
    for i in range(4):
        part = lax.dot_general(
            tok_buf[:, i * 256 : i * 256 + 256], act_grad[...], FIRST, preferred_element_type=F32
        ).astype(BF16).reshape(4, 2, 32, 512)
        at = pl.ds(i * 4, 4)
        result[at, 32:, :512] = part[:, 0]
        result[at, 32:, 512:] = part[:, 1]
        sent.append(pltpu.make_async_copy(result.at[at, 32:64], out.at[at, 32:64], sems.at[17 + i]))
        sent[-1].start()
    for copy in sent:
        copy.wait()


def backward(grads, gain, rows, toks, hiddens, slopes, weights):
    return pl.pallas_call(
        backward_kernel,
        out_shape=shape((16, 64, 1024), BF16),
        in_specs=[WHOLE] * 5 + [ANYWHERE] * 17,
        out_specs=ANYWHERE,
        scratch_shapes=[
            pltpu.VMEM((1024, 1152), BF16),
            pltpu.VMEM((1024, 1024), BF16),
            pltpu.VMEM((1024, 512), BF16),
            pltpu.VMEM((1024, 512), F32),
            pltpu.VMEM((16, 32, 1024), BF16),
            pltpu.VMEM((1024, 1024), BF16),
            pltpu.VMEM((1024, 512), BF16),
            pltpu.VMEM((16, 64, 1024), BF16),
            pltpu.SemaphoreType.DMA((25,)),
        ],
        compiler_params=MOST,
        cost_estimate=cost(3 * 2**30, 10 * 2**20),
    )(*grads, gain, *rows, *toks, *hiddens, *slopes, weights)


def total_kernel(meta, got, out, keep, give):
    total = got[0].astype(F32)
    for i in range(1, 16):
        total = total + got[i].astype(F32)
    total = total.astype(BF16)
    core, step = meta[0], pl.program_id(0)

    @pl.when(step < 2)
    def _():
        out[...] = total

    @pl.when(step >= 2)
    def _():
        keep[...] = jnp.where(core == 0, total[:, :512], total[:, 512:])
        give[...] = jnp.where(core == 0, total[:, 512:], total[:, :512])


def place_kernel(meta, own, near, wrap, far, grad_in, grad_out):
    core, role = meta[0], meta[1]
    mine = own[:32].astype(F32) + wrap[:32].astype(F32)
    theirs = near[:32].astype(F32) + far[:32].astype(F32)
    grad_out[:32] = jnp.where(role == 0, mine, theirs)
    grad_out[32:] = jnp.where(role == 0, theirs, mine)
    row, lane = iota((1024, 512), 0), iota((1024, 512), 1)
    piece, at = row // 128, row % 128
    swapped, flipped = piece % 2, piece // 4
    part = (core + swapped - 2 * core * swapped) * 2 + (role + flipped - 2 * role * flipped)
    spread = (lane == at // 32 * 128 + part * 32 + at % 32).astype(BF16)
    blocks = [
        jnp.concatenate(
            [
                a[32:, k * 512 + i * 128 : k * 512 + i * 128 + 128]
                for a in (own, wrap, near, far)
                for k in range(2)
            ],
            axis=1,
        )
        for i in range(4)
    ]
    placed = jnp.dot(jnp.concatenate(blocks, axis=0), spread, preferred_element_type=F32)
    for i in range(4):
        grad_in[:, i * 512 : i * 512 + 512] = placed[i * 32 : i * 32 + 32]


def on_device(
    states,
    lengths,
    w_in,
    w_out,
    norm_gain,
    label_tiles,
    tile_mean,
    tile_var,
    shortlist,
    positives,
    owner_map,
):
    docs, length, width = states.shape
    core = lax.axis_index("c")
    high, low = lax.axis_index("h"), lax.axis_index("l")
    role = high + low - 2 * high * low
    chip = lax.axis_index("x") * 4 + lax.axis_index("z")
    meta = jnp.stack([core, role, chip]).astype(jnp.int32)
    gain = norm_gain.reshape(1, width)
    own_tok = states.reshape(docs * length, width)

    mine, theirs = pl.pallas_call(
        pick_kernel,
        out_shape=(shape((32, 512), BF16),) * 2,
        in_specs=[WHOLE],
        out_specs=(WHOLE, WHOLE),
        cost_estimate=cost(2**25, 2**18),
    )(w_in)
    block = pl.pallas_call(
        lay_kernel,
        out_shape=shape((16, 64, width), BF16),
        in_specs=[WHOLE, WHOLE, ANYWHERE],
        out_specs=ANYWHERE,
        scratch_shapes=[pltpu.VMEM((64, width), BF16), pltpu.SemaphoreType.DMA((17,))],
        cost_estimate=cost(0, 2**21),
    )(mine, swap_core(theirs), w_out)
    block, own_tok, label_tiles, shortlist, positives, owner_map = lax.optimization_barrier(
        (block, own_tok, label_tiles, shortlist, positives, owner_map)
    )
    weights = gather_chips(block)

    oth_tiles = swap_core(label_tiles)
    slots = jnp.concatenate(
        [(chip * 2 + core) * 64 + jnp.arange(64), (chip * 2 + 1 - core) * 64 + jnp.arange(64)]
    ).astype(jnp.int32)
    all_clusters = jnp.arange(owner_map.shape[0], dtype=jnp.int32)
    owner_match = owner_map[:, None] == slots[None, :]
    cluster_ids = jnp.sum(jnp.where(owner_match, all_clusters[:, None], 0), axis=0)
    own_tok, cluster_ids = lax.optimization_barrier((own_tok, cluster_ids))

    core_tok, near_tok, diag_tok = swap_core(own_tok), swap_near(own_tok), swap_diag(own_tok)

    pick = lambda a: lax.dynamic_index_in_dim(a.reshape(16, 2, 8, -1), core, 1, False).reshape(128, -1)
    short, posit = pick(shortlist), pick(positives)
    cluster_live = jnp.max(
        (short[:, :, None] == cluster_ids[None, None, :]).astype(F32), axis=1
    ).astype(BF16)
    tiles = jnp.concatenate([label_tiles, oth_tiles], axis=0)
    tiles_top = round_bf16(tiles)
    tiles_hi, tiles_lo = tiles_top.astype(BF16), (tiles - tiles_top).astype(BF16)
    cluster_hit = (posit[:, :, None] // LPC == cluster_ids[None, None, :]).astype(F32)
    offset_hit = (
        posit[:, :, None] % LPC == jnp.arange(LPC, dtype=jnp.int32)[None, None, :]
    ).astype(F32)
    hits = jnp.sum(cluster_hit[:, :, :, None] * offset_hit[:, :, None, :], axis=1).reshape(128, 512)
    share_hit = hits / POS
    hit = share_hit.astype(BF16)
    pos_part = jnp.dot(hit, tiles_hi, preferred_element_type=F32) + jnp.dot(
        hit, tiles_lo, preferred_element_type=F32
    )
    pos_part = (pos_part * POS_SCALE).astype(jnp.float16)
    weights, cluster_live, share_hit, pos_part, tiles_hi, tiles_lo = lax.optimization_barrier(
        (weights, cluster_live, share_hit, pos_part, tiles_hi, tiles_lo)
    )

    near_a, diag_hidden, diag_slope = forward(diag_tok, weights, BF16)
    near_a, near_tok = lax.optimization_barrier((near_a, near_tok))
    near_b, near_hidden, near_slope = forward(near_tok, weights, F32)
    near_sum = (near_b + swap_core(near_a).astype(F32)).astype(BF16)
    near_sum, pos_part, core_tok = lax.optimization_barrier((near_sum, pos_part, core_tok))
    from_near = swap_near(near_sum)
    pos_got = gather_chips(pos_part.reshape(16, docs, width))
    own_a, core_hidden, core_slope = forward(core_tok, weights, BF16)
    own_a, own_tok = lax.optimization_barrier((own_a, own_tok))
    own_b, own_hidden, own_slope = forward(own_tok, weights, F32)
    from_near, pos_got = lax.optimization_barrier((from_near, pos_got))
    pos_mean = jnp.sum(pos_got.astype(F32), axis=0) * (1.0 / POS_SCALE)
    own_rows, emb = pl.pallas_call(
        norm_kernel,
        out_shape=(shape((256, 1152), BF16), shape((128, width), BF16)),
        in_specs=[SCALARS] + [WHOLE] * 5,
        out_specs=(WHOLE, ANYWHERE),
        scratch_shapes=[pltpu.VMEM((128, width), BF16), pltpu.SemaphoreType.DMA],
        compiler_params=LIMIT,
        cost_estimate=cost(2**22, 4 * 2**20),
    )(lengths, own_tok, own_b, swap_core(own_a), from_near, gain)

    plane_emb = gather_chips(emb.reshape(16, docs, width)).reshape(128, width)
    near_rows = swap_near(own_rows)
    packed, weighted = pl.pallas_call(
        score_kernel,
        out_shape=(shape((128, 1280), BF16), shape((128, 512), F32)),
        in_specs=[ANYWHERE] + [WHOLE] * 3,
        out_specs=(ANYWHERE, WHOLE),
        scratch_shapes=[
            pltpu.VMEM((128, width), BF16),
            pltpu.VMEM((128, 1280), BF16),
            pltpu.SemaphoreType.DMA,
        ],
        compiler_params=LIMIT,
        cost_estimate=cost(2**29, 3 * 2**20, 2**16),
    )(plane_emb, tiles_hi, tiles_lo, cluster_live)
    packed, near_rows = lax.optimization_barrier((packed, near_rows))
    core_rows, diag_rows = swap_core(own_rows), swap_core(near_rows)
    got = lax.all_to_all(packed.reshape(16, docs, 1280), CHIPS, 0, 0, tiled=True)
    emb_grad, loss, sums = pl.pallas_call(
        settle_kernel,
        out_shape=(shape((docs, width), F32), shape((docs, 128), F32), shape((docs, 128), F32)),
        in_specs=[SCALARS, ANYWHERE, WHOLE, WHOLE],
        out_specs=(WHOLE,) * 3,
        scratch_shapes=[
            pltpu.VMEM((16, docs, 1280), BF16),
            pltpu.SemaphoreType.DMA,
        ],
        compiler_params=LIMIT,
        cost_estimate=cost(2**20, 2**20),
    )(meta, got, pos_mean, emb)
    loss = loss[:, 0]

    grads = (swap_diag(emb_grad), swap_near(emb_grad), swap_core(emb_grad), emb_grad)
    send = backward(
        grads,
        gain,
        (diag_rows, near_rows, core_rows, own_rows),
        (diag_tok, near_tok, core_tok, own_tok),
        (diag_hidden, near_hidden, core_hidden, own_hidden),
        (diag_slope, near_slope, core_slope, own_slope),
        weights,
    )
    got = lax.all_to_all(send, CHIPS, 0, 0, tiled=True)
    part, keep, give = pl.pallas_call(
        total_kernel,
        out_shape=(shape((32, width), BF16), shape((32, 512), BF16), shape((32, 512), BF16)),
        grid=(4,),
        in_specs=[SCALARS, pl.BlockSpec((16, 16, width), lambda i: (0, i, 0))],
        out_specs=(
            pl.BlockSpec((16, width), lambda i: (jnp.minimum(i, 1), 0)),
            pl.BlockSpec((16, 512), lambda i: (jnp.maximum(i - 2, 0), 0)),
            pl.BlockSpec((16, 512), lambda i: (jnp.maximum(i - 2, 0), 0)),
        ),
        compiler_params=LIMIT,
        cost_estimate=cost(2**20, 2**21),
    )(meta, got)
    both = jnp.concatenate([part, jnp.concatenate([keep, swap_core(give)], axis=1)], axis=0)
    grad_in, grad_out = pl.pallas_call(
        place_kernel,
        out_shape=(shape((32, 2048), F32), shape((64, width), F32)),
        in_specs=[SCALARS] + [WHOLE] * 4,
        out_specs=(WHOLE, WHOLE),
        compiler_params=LIMIT,
        cost_estimate=cost(2**26, 2**20),
    )(meta, both, swap_near(both), swap_wrap(both), swap_far(both))

    tile_own, tile_other = pl.pallas_call(
        tile_kernel,
        out_shape=(shape((256, width), F32), shape((256, width), BF16)),
        in_specs=[WHOLE] * 4,
        out_specs=(WHOLE, WHOLE),
        compiler_params=LIMIT,
        cost_estimate=cost(2**28, 2**21),
    )(sums, weighted, share_hit, plane_emb)
    tile_chip = (tile_own + swap_core(tile_other).astype(F32)).astype(BF16)

    def add(a, swap):
        return a.astype(F32) + swap(a).astype(F32)

    tile_grad = jnp.concatenate(
        [
            add(add(tile_chip[:128], swap_near).astype(BF16), swap_wrap),
            add(add(tile_chip[128:], swap_wrap).astype(BF16), swap_near),
        ],
        axis=0,
    )
    new_mean = 0.9 * tile_mean + 0.1 * tile_grad
    new_var = 0.999 * tile_var + 0.001 * tile_grad * tile_grad
    new_tiles = label_tiles - 0.001 * (new_mean * CORR_ONE) / (jnp.sqrt(new_var * CORR_TWO) + 1e-08)
    return (loss, new_tiles, new_mean, new_var, grad_in, grad_out)


def solution(mesh):
    grid = Mesh(mesh.devices.reshape(2, 2, 4, 4, 2), ("h", "l", "x", "z", "c"))
    every, plane, group = ("h", "l", "x", "z", "c"), ("x", "z", "c"), ("h", "l")
    return jax.shard_map(
        on_device,
        mesh=grid,
        in_specs=(
            P(every, None, None),
            P(every),
            P(plane, None),
            P(plane, None),
            P(),
            P(plane, None),
            P(plane, None),
            P(plane, None),
            P(group, None),
            P(group, None),
            P(),
        ),
        out_specs=(
            P(every),
            P(plane, None),
            P(plane, None),
            P(plane, None),
            P(plane, None),
            P(plane, None),
        ),
        check_vma=False,
    )
```

```python
import functools

import jax
import jax.numpy as jnp
from jax import lax
from jax.experimental import pallas as pl
from jax.experimental.pallas import tpu as pltpu
from jax.sharding import Mesh, PartitionSpec as P

LPC = 4
POS = 4
POS_SCALE = 32768.0

NORM_EPS = 1e-05
INV_ROOT_TWO = 0.7071067811865476
INV_ROOT_TWO_PI = 0.3989422804014327
CORR_ONE = 1.000026562104397
CORR_TWO = 10.50333528

F32 = jnp.float32
BF16 = jnp.bfloat16
CHIPS = ("x", "z")
FIRST = (((0,), (0,)), ((), ()))
LAST = (((1,), (1,)), ((), ()))


def swap_core(a):
    return lax.ppermute(a, "c", [(0, 1), (1, 0)])


def swap_near(a):
    return lax.ppermute(a, "l", [(0, 1), (1, 0)])


def swap_diag(a):
    return lax.ppermute(a, ("l", "c"), [(0, 3), (3, 0), (1, 2), (2, 1)])


def swap_far(a):
    return lax.ppermute(a, "h", [(0, 1), (1, 0)])


def swap_wrap(a):
    return lax.ppermute(a, ("h", "l"), [(0, 3), (3, 0), (1, 2), (2, 1)])


def round_bf16(a):
    return lax.reduce_precision(a, 8, 7)


def gather_chips(a):
    return lax.all_to_all(a, CHIPS, 0, 0, tiled=True)


WHOLE = pl.BlockSpec(memory_space=pltpu.VMEM)
SCALARS = pl.BlockSpec(memory_space=pltpu.SMEM)
ANYWHERE = pl.BlockSpec(memory_space=pl.ANY)
LIMIT = pltpu.CompilerParams(vmem_limit_bytes=20 * 1024 * 1024)
MOST = pltpu.CompilerParams(vmem_limit_bytes=60 * 1024 * 1024)


def shape(dims, dtype):
    return jax.ShapeDtypeStruct(dims, dtype)


def cost(flops, data, special=0):
    return pl.CostEstimate(flops=flops, bytes_accessed=data, transcendentals=special)


def iota(dims, axis):
    return lax.broadcasted_iota(jnp.int32, dims, axis)


def place_of():
    core, high, low = (lax.axis_index(axis) for axis in ("c", "h", "l"))
    return core, high + low - 2 * high * low


def pick_kernel(w_in, mine, theirs):
    core, role = place_of()
    part = jnp.where(iota((512, 256), 1) < 128, core * 2 + role, 2 - core * 2 + role)
    at = iota((512, 256), 1) % 128
    spread = (iota((512, 256), 0) == at // 32 * 128 + part * 32 + at % 32).astype(BF16)
    for i in range(4):
        got = jnp.dot(w_in[:, i * 512 : i * 512 + 512], spread, preferred_element_type=F32).astype(BF16)
        mine[:, i * 128 : i * 128 + 128] = got[:, :128]
        theirs[:, i * 128 : i * 128 + 128] = got[:, 128:]


def lay_kernel(mine, theirs, w_out, out, block, sems):
    core, role = place_of()
    block[:32] = jnp.where(role == 0, w_out[:32], w_out[32:])
    block[32:, :512] = jnp.where(core == 0, mine[...], theirs[...])
    block[32:, 512:] = jnp.where(core == 0, theirs[...], mine[...])
    copies = [pltpu.make_async_copy(block, out.at[i], sems.at[i]) for i in range(16)]
    for copy in copies:
        copy.start()
    for copy in copies:
        copy.wait()


def forward_kernel(count, *refs):
    toks, weights, parts = refs[:count], refs[count], refs[count + 1 : 2 * count + 1]
    hidden_hbm, slope_hbm, w_in, w_out, hidden, slope, sems = refs[2 * count + 1 :]
    copies = [
        pltpu.make_async_copy(
            weights.at[:, 32:64, k * 512 : k * 512 + 512], w_in.at[:, k * 32 : k * 32 + 32], sems.at[k]
        )
        for k in range(2)
    ]
    copies.append(pltpu.make_async_copy(weights.at[:, 0:32], w_out, sems.at[2]))
    for copy in copies:
        copy.start()
    copies[0].wait()
    copies[1].wait()
    sent = []
    for k, (tok, part) in enumerate(zip(toks, parts)):
        at = pl.ds(k * 256, 256)
        pre_act = jnp.dot(tok[...], w_in[...].reshape(1024, 512), preferred_element_type=F32)
        normal_cdf = 0.5 * (1.0 + lax.erf(pre_act * INV_ROOT_TWO))
        act = (pre_act * normal_cdf).astype(BF16)
        hidden[at] = act
        slope[at] = normal_cdf + pre_act * jnp.exp(-0.5 * pre_act * pre_act) * INV_ROOT_TWO_PI
        sent.append(pltpu.make_async_copy(hidden.at[at], hidden_hbm.at[at], sems.at[3 + 2 * k]))
        sent.append(pltpu.make_async_copy(slope.at[at], slope_hbm.at[at], sems.at[4 + 2 * k]))
        sent[-2].start()
        sent[-1].start()
        if k == 0:
            copies[2].wait()
        part[...] = jnp.dot(
            act, w_out[...].reshape(512, 1024), preferred_element_type=F32
        ).astype(part.dtype)
    for copy in sent:
        copy.wait()


def forward(toks, weights, dtypes):
    count = len(toks)
    *parts, hidden, slope = pl.pallas_call(
        functools.partial(forward_kernel, count),
        out_shape=[shape((256, 1024), dtype) for dtype in dtypes]
        + [shape((256 * count, 512), BF16), shape((256 * count, 512), F32)],
        in_specs=[WHOLE] * count + [ANYWHERE],
        out_specs=[WHOLE] * count + [ANYWHERE] * 2,
        scratch_shapes=[
            pltpu.VMEM((16, 64, 512), BF16),
            pltpu.VMEM((16, 32, 1024), BF16),
            pltpu.VMEM((256 * count, 512), BF16),
            pltpu.VMEM((256 * count, 512), F32),
            pltpu.SemaphoreType.DMA((7,)),
        ],
        compiler_params=LIMIT,
        cost_estimate=cost(2**32, 6 * 2**20, 2**18),
    )(*toks, weights)
    return (*parts, (hidden, slope))


def norm_kernel(lengths, tok, part, from_core, from_near, gain, rows, emb_hbm, emb, sem):
    embs = []
    for d in range(8):
        at = pl.ds(d * 32, 32)
        summed = tok[at].astype(F32) + (
            part[at] + from_core[at].astype(F32) + from_near[at].astype(F32)
        )
        centred = summed - jnp.mean(summed, axis=-1, keepdims=True)
        inv = lax.rsqrt(jnp.mean(centred * centred, axis=-1, keepdims=True) + NORM_EPS)
        normed = centred * inv
        count = jnp.full((32, 1), lengths[d], jnp.int32).astype(F32)
        share = jnp.where(iota((32, 1), 0).astype(F32) < count, 1.0, 0.0) / count
        embs.append(jnp.sum(normed * gain[...] * share, axis=0, keepdims=True))
        high = inv.astype(BF16).astype(F32)
        lane = iota((32, 128), 1)
        extra = jnp.where(lane == 0, high, jnp.where(lane == 1, inv - high, jnp.where(lane == 2, count, 0.0)))
        rows[at, :1024] = normed.astype(BF16)
        rows[at, 1024:] = extra.astype(BF16)
    docs = jnp.concatenate(embs, axis=0)
    emb[...] = jnp.concatenate([docs] * 16, axis=0).astype(BF16)
    copy = pltpu.make_async_copy(emb, emb_hbm, sem)
    copy.start()
    copy.wait()


def score_kernel(emb, tiles_hi, tiles_lo, live, packed_hbm, weighted, emb_buf, packed, sem):
    copy = pltpu.make_async_copy(emb, emb_buf, sem)
    copy.start()
    grow = (iota((128, 512), 0) == iota((128, 512), 1) // LPC).astype(BF16)
    mask = jnp.dot(live[...], grow, preferred_element_type=F32)
    copy.wait()
    docs = emb_buf[...]
    scores = lax.dot_general(docs, tiles_hi[...], LAST, preferred_element_type=F32)
    scores = scores + lax.dot_general(docs, tiles_lo[...], LAST, preferred_element_type=F32)
    value = mask * jnp.exp(scores)
    weighted[...] = value
    value_hi = value.astype(BF16)
    value_lo = (value - value_hi.astype(F32)).astype(BF16)
    part_emb = jnp.dot(value_hi, tiles_hi[...], preferred_element_type=F32)
    part_emb = part_emb + jnp.dot(value_hi, tiles_lo[...], preferred_element_type=F32)
    part_emb = part_emb + jnp.dot(value_lo, tiles_hi[...], preferred_element_type=F32)
    sums = jnp.sum(value, axis=1, keepdims=True) * 0.5
    high = sums.astype(BF16).astype(F32)
    row, lane = iota((128, 128), 0), iota((128, 128), 1)
    chosen = row // 8 == lane
    same = (row % 8 == lane % 8).astype(BF16)
    for k, part in enumerate((high, sums - high)):
        table = jnp.where(chosen, part, 0.0).astype(BF16)
        packed[:, 1024 + k * 128 : 1152 + k * 128] = jnp.dot(
            same, table, preferred_element_type=F32
        ).astype(BF16)
    packed[:, :1024] = part_emb.astype(BF16)
    copy = pltpu.make_async_copy(packed, packed_hbm, sem)
    copy.start()
    copy.wait()


def settle_kernel(meta, got_hbm, pos, emb, grad, loss, sums, got, sem):
    copy = pltpu.make_async_copy(got_hbm, got, sem)
    copy.start()
    copy.wait()
    total = got[0].astype(F32)
    for i in range(1, 16):
        total = total + got[i].astype(F32)
    every = (total[:, 1024:1152] + total[:, 1152:1280]) * 2.0
    sums[...] = every
    expsum = jnp.sum(jnp.where(iota((8, 128), 1) == meta[2], every, 0.0), axis=1, keepdims=True)
    pos_mean = pos[...]
    grad[...] = total[:, :1024] / expsum - pos_mean
    picked = jnp.sum(emb[...].astype(F32)[:8] * pos_mean, axis=1, keepdims=True)
    loss[...] = jnp.broadcast_to(jnp.log(expsum) - picked, (8, 128))


def tile_kernel(sums, weighted, share_hit, emb, own, other):
    rows = jnp.concatenate([sums[...]] * 16, axis=0)
    chosen = iota((128, 128), 0) // 8 == iota((128, 128), 1)
    column = jnp.sum(jnp.where(chosen, rows, 0.0), axis=1, keepdims=True)
    grad = weighted[...] / column - share_hit[...]
    grad_hi = grad.astype(BF16)
    grad_lo = (grad - grad_hi.astype(F32)).astype(BF16)
    for k, out in enumerate((own, other)):
        at = slice(k * 256, k * 256 + 256)
        part = lax.dot_general(grad_hi[:, at], emb[...], FIRST, preferred_element_type=F32)
        part = part + lax.dot_general(grad_lo[:, at], emb[...], FIRST, preferred_element_type=F32)
        out[...] = part.astype(out.dtype)


def backward_kernel(*refs):
    grads, gain = refs[:4], refs[4]
    rows, toks = refs[5:9], refs[9:13]
    hiddens, slopes, weights, out = refs[13:16], refs[16:19], refs[19], refs[20]
    row_buf, tok_buf, hid_buf, slope_buf, w_out, sum_grad, act_grad, result, sems = refs[21:]
    sent = []
    first = pltpu.make_async_copy(weights.at[:, 0:32], w_out, sems.at[0])
    first.start()
    row_copies, tok_copies, hid_copies, slope_copies = [], [], [], []
    for k in range(4):
        at = pl.ds(k * 256, 256)
        row_copies.append(pltpu.make_async_copy(rows[k], row_buf.at[at], sems.at[1 + k]))
        row_copies[k].start()
    spans = (pl.ds(0, 512), pl.ds(512, 256), pl.ds(768, 256))
    for k, at in enumerate(spans):
        slope_copies.append(pltpu.make_async_copy(slopes[k], slope_buf.at[at], sems.at[21 + k]))
        slope_copies[k].start()
    for k, at in enumerate(spans):
        hid_copies.append(pltpu.make_async_copy(hiddens[k], hid_buf.at[at], sems.at[5 + k]))
        hid_copies[k].start()
    for k in range(4):
        at = pl.ds(k * 256, 256)
        tok_copies.append(pltpu.make_async_copy(toks[k], tok_buf.at[at], sems.at[9 + k]))
        tok_copies[k].start()
    for k in range(4):
        row_copies[k].wait()
        scaled_grad = grads[k][...] * gain[...]
        grad_mean = jnp.mean(scaled_grad, axis=-1, keepdims=True)
        for d in range(8):
            at = pl.ds(k * 256 + d * 32, 32)
            norm = row_buf[at, :1024].astype(F32)
            extra = row_buf[at, 1024:].astype(F32)
            lane = iota((32, 128), 1)
            scale = jnp.sum(jnp.where(lane < 2, extra, 0.0), axis=1, keepdims=True)
            count = jnp.sum(jnp.where(lane == 2, extra, 0.0), axis=1, keepdims=True)
            share = jnp.where(iota((32, 1), 0).astype(F32) < count, 1.0, 0.0) / count
            grad = scaled_grad[d : d + 1]
            along = jnp.mean(grad * norm, axis=-1, keepdims=True)
            sum_grad[at] = (
                (grad - grad_mean[d : d + 1] - norm * along) * (share * scale)
            ).astype(BF16)
        if k == 0:
            first.wait()
        if k != 1:
            slope_copies[max(k - 1, 0)].wait()
        at = pl.ds(k * 256, 256)
        back = lax.dot_general(
            sum_grad[at], w_out[...].reshape(512, 1024), LAST, preferred_element_type=F32
        )
        act_grad[at] = (back * slope_buf[at]).astype(BF16)
    for copy in hid_copies:
        copy.wait()
    for i in range(4):
        part = lax.dot_general(
            hid_buf[:, i * 128 : i * 128 + 128], sum_grad[...], FIRST, preferred_element_type=F32
        )
        at = pl.ds(i * 4, 4)
        result[at, :32] = part.astype(BF16).reshape(4, 32, 1024)
        sent.append(pltpu.make_async_copy(result.at[at, 0:32], out.at[at, 0:32], sems.at[13 + i]))
        sent[-1].start()
    for copy in tok_copies:
        copy.wait()
    for i in range(4):
        part = lax.dot_general(
            tok_buf[:, i * 256 : i * 256 + 256], act_grad[...], FIRST, preferred_element_type=F32
        ).astype(BF16).reshape(4, 2, 32, 512)
        at = pl.ds(i * 4, 4)
        result[at, 32:, :512] = part[:, 0]
        result[at, 32:, 512:] = part[:, 1]
        sent.append(pltpu.make_async_copy(result.at[at, 32:64], out.at[at, 32:64], sems.at[17 + i]))
        sent[-1].start()
    for copy in sent:
        copy.wait()


def backward(grads, gain, rows, toks, hiddens, slopes, weights):
    return pl.pallas_call(
        backward_kernel,
        out_shape=shape((16, 64, 1024), BF16),
        in_specs=[WHOLE] * 5 + [ANYWHERE] * 15,
        out_specs=ANYWHERE,
        scratch_shapes=[
            pltpu.VMEM((1024, 1152), BF16),
            pltpu.VMEM((1024, 1024), BF16),
            pltpu.VMEM((1024, 512), BF16),
            pltpu.VMEM((1024, 512), F32),
            pltpu.VMEM((16, 32, 1024), BF16),
            pltpu.VMEM((1024, 1024), BF16),
            pltpu.VMEM((1024, 512), BF16),
            pltpu.VMEM((16, 64, 1024), BF16),
            pltpu.SemaphoreType.DMA((24,)),
        ],
        compiler_params=MOST,
        cost_estimate=cost(3 * 2**30, 10 * 2**20),
    )(*grads, gain, *rows, *toks, *hiddens, *slopes, weights)


def total_kernel(meta, got, out, keep, give):
    total = got[0].astype(F32)
    for i in range(1, 16):
        total = total + got[i].astype(F32)
    total = total.astype(BF16)
    core, step = meta[0], pl.program_id(0)

    @pl.when(step < 2)
    def _():
        out[...] = total

    @pl.when(step >= 2)
    def _():
        keep[...] = jnp.where(core == 0, total[:, :512], total[:, 512:])
        give[...] = jnp.where(core == 0, total[:, 512:], total[:, :512])


def place_kernel(meta, own, near, wrap, far, grad_in, grad_out):
    core, role = meta[0], meta[1]
    mine = own[:32].astype(F32) + wrap[:32].astype(F32)
    theirs = near[:32].astype(F32) + far[:32].astype(F32)
    grad_out[:32] = jnp.where(role == 0, mine, theirs)
    grad_out[32:] = jnp.where(role == 0, theirs, mine)
    row, lane = iota((1024, 512), 0), iota((1024, 512), 1)
    piece, at = row // 128, row % 128
    swapped, flipped = piece % 2, piece // 4
    part = (core + swapped - 2 * core * swapped) * 2 + (role + flipped - 2 * role * flipped)
    spread = (lane == at // 32 * 128 + part * 32 + at % 32).astype(BF16)
    blocks = [
        jnp.concatenate(
            [
                a[32:, k * 512 + i * 128 : k * 512 + i * 128 + 128]
                for a in (own, wrap, near, far)
                for k in range(2)
            ],
            axis=1,
        )
        for i in range(4)
    ]
    placed = jnp.dot(jnp.concatenate(blocks, axis=0), spread, preferred_element_type=F32)
    for i in range(4):
        grad_in[:, i * 512 : i * 512 + 512] = placed[i * 32 : i * 32 + 32]


def on_device(
    states,
    lengths,
    w_in,
    w_out,
    norm_gain,
    label_tiles,
    tile_mean,
    tile_var,
    shortlist,
    positives,
    owner_map,
):
    docs, length, width = states.shape
    core = lax.axis_index("c")
    high, low = lax.axis_index("h"), lax.axis_index("l")
    role = high + low - 2 * high * low
    chip = lax.axis_index("x") * 4 + lax.axis_index("z")
    meta = jnp.stack([core, role, chip]).astype(jnp.int32)
    gain = norm_gain.reshape(1, width)
    own_tok = states.reshape(docs * length, width)

    mine, theirs = pl.pallas_call(
        pick_kernel,
        out_shape=(shape((32, 512), BF16),) * 2,
        in_specs=[WHOLE],
        out_specs=(WHOLE, WHOLE),
        cost_estimate=cost(2**25, 2**18),
    )(w_in)
    block = pl.pallas_call(
        lay_kernel,
        out_shape=shape((16, 64, width), BF16),
        in_specs=[WHOLE, WHOLE, WHOLE],
        out_specs=ANYWHERE,
        scratch_shapes=[pltpu.VMEM((64, width), BF16), pltpu.SemaphoreType.DMA((16,))],
        cost_estimate=cost(0, 2**21),
    )(mine, swap_core(theirs), w_out)
    block, own_tok, label_tiles, shortlist, positives, owner_map = lax.optimization_barrier(
        (block, own_tok, label_tiles, shortlist, positives, owner_map)
    )
    weights = gather_chips(block)

    core_tok, near_tok, diag_tok = swap_core(own_tok), swap_near(own_tok), swap_diag(own_tok)

    oth_tiles = swap_core(label_tiles)
    slots = jnp.concatenate(
        [(chip * 2 + core) * 64 + jnp.arange(64), (chip * 2 + 1 - core) * 64 + jnp.arange(64)]
    ).astype(jnp.int32)
    all_clusters = jnp.arange(owner_map.shape[0], dtype=jnp.int32)
    owner_match = owner_map[:, None] == slots[None, :]
    cluster_ids = jnp.sum(jnp.where(owner_match, all_clusters[:, None], 0), axis=0)
    pick = lambda a: lax.dynamic_index_in_dim(a.reshape(16, 2, 8, -1), core, 1, False).reshape(128, -1)
    short, posit = pick(shortlist), pick(positives)
    cluster_live = jnp.max(
        (short[:, :, None] == cluster_ids[None, None, :]).astype(F32), axis=1
    ).astype(BF16)
    tiles = jnp.concatenate([label_tiles, oth_tiles], axis=0)
    tiles_top = round_bf16(tiles)
    tiles_hi, tiles_lo = tiles_top.astype(BF16), (tiles - tiles_top).astype(BF16)
    cluster_hit = (posit[:, :, None] // LPC == cluster_ids[None, None, :]).astype(F32)
    offset_hit = (
        posit[:, :, None] % LPC == jnp.arange(LPC, dtype=jnp.int32)[None, None, :]
    ).astype(F32)
    hits = jnp.sum(cluster_hit[:, :, :, None] * offset_hit[:, :, None, :], axis=1).reshape(128, 512)
    share_hit = hits / POS
    hit = share_hit.astype(BF16)
    pos_part = jnp.dot(hit, tiles_hi, preferred_element_type=F32) + jnp.dot(
        hit, tiles_lo, preferred_element_type=F32
    )
    pos_part = (pos_part * POS_SCALE).astype(jnp.float16)
    weights, cluster_live, share_hit, pos_part, tiles_hi, tiles_lo = lax.optimization_barrier(
        (weights, cluster_live, share_hit, pos_part, tiles_hi, tiles_lo)
    )

    near_a, near_b, near_kept = forward((diag_tok, near_tok), weights, (BF16, F32))
    near_sum = (near_b + swap_core(near_a).astype(F32)).astype(BF16)
    near_sum, pos_part, core_tok = lax.optimization_barrier((near_sum, pos_part, core_tok))
    from_near = swap_near(near_sum)
    pos_got = gather_chips(pos_part.reshape(16, docs, width))
    own_a, core_kept = forward((core_tok,), weights, (BF16,))
    own_a, own_tok = lax.optimization_barrier((own_a, own_tok))
    own_b, own_kept = forward((own_tok,), weights, (F32,))
    from_near, pos_got = lax.optimization_barrier((from_near, pos_got))
    pos_mean = jnp.sum(pos_got.astype(F32), axis=0) * (1.0 / POS_SCALE)
    own_rows, emb = pl.pallas_call(
        norm_kernel,
        out_shape=(shape((256, 1152), BF16), shape((128, width), BF16)),
        in_specs=[SCALARS] + [WHOLE] * 5,
        out_specs=(WHOLE, ANYWHERE),
        scratch_shapes=[pltpu.VMEM((128, width), BF16), pltpu.SemaphoreType.DMA],
        compiler_params=LIMIT,
        cost_estimate=cost(2**22, 4 * 2**20),
    )(lengths, own_tok, own_b, swap_core(own_a), from_near, gain)

    plane_emb = gather_chips(emb.reshape(16, docs, width)).reshape(128, width)
    near_rows = swap_near(own_rows)
    packed, weighted = pl.pallas_call(
        score_kernel,
        out_shape=(shape((128, 1280), BF16), shape((128, 512), F32)),
        in_specs=[ANYWHERE] + [WHOLE] * 3,
        out_specs=(ANYWHERE, WHOLE),
        scratch_shapes=[
            pltpu.VMEM((128, width), BF16),
            pltpu.VMEM((128, 1280), BF16),
            pltpu.SemaphoreType.DMA,
        ],
        compiler_params=LIMIT,
        cost_estimate=cost(2**29, 3 * 2**20, 2**16),
    )(plane_emb, tiles_hi, tiles_lo, cluster_live)
    packed, near_rows = lax.optimization_barrier((packed, near_rows))
    core_rows, diag_rows = swap_core(own_rows), swap_core(near_rows)
    got = lax.all_to_all(packed.reshape(16, docs, 1280), CHIPS, 0, 0, tiled=True)
    emb_grad, loss, sums = pl.pallas_call(
        settle_kernel,
        out_shape=(shape((docs, width), F32), shape((docs, 128), F32), shape((docs, 128), F32)),
        in_specs=[SCALARS, ANYWHERE, WHOLE, WHOLE],
        out_specs=(WHOLE,) * 3,
        scratch_shapes=[
            pltpu.VMEM((16, docs, 1280), BF16),
            pltpu.SemaphoreType.DMA,
        ],
        compiler_params=LIMIT,
        cost_estimate=cost(2**20, 2**20),
    )(meta, got, pos_mean, emb)
    loss = loss[:, 0]

    grads = (swap_diag(emb_grad), swap_near(emb_grad), swap_core(emb_grad), emb_grad)
    send = backward(
        grads,
        gain,
        (diag_rows, near_rows, core_rows, own_rows),
        (diag_tok, near_tok, core_tok, own_tok),
        (near_kept[0], core_kept[0], own_kept[0]),
        (near_kept[1], core_kept[1], own_kept[1]),
        weights,
    )
    got = lax.all_to_all(send, CHIPS, 0, 0, tiled=True)
    part, keep, give = pl.pallas_call(
        total_kernel,
        out_shape=(shape((32, width), BF16), shape((32, 512), BF16), shape((32, 512), BF16)),
        grid=(4,),
        in_specs=[SCALARS, pl.BlockSpec((16, 16, width), lambda i: (0, i, 0))],
        out_specs=(
            pl.BlockSpec((16, width), lambda i: (jnp.minimum(i, 1), 0)),
            pl.BlockSpec((16, 512), lambda i: (jnp.maximum(i - 2, 0), 0)),
            pl.BlockSpec((16, 512), lambda i: (jnp.maximum(i - 2, 0), 0)),
        ),
        compiler_params=LIMIT,
        cost_estimate=cost(2**20, 2**21),
    )(meta, got)
    both = jnp.concatenate([part, jnp.concatenate([keep, swap_core(give)], axis=1)], axis=0)
    grad_in, grad_out = pl.pallas_call(
        place_kernel,
        out_shape=(shape((32, 2048), F32), shape((64, width), F32)),
        in_specs=[SCALARS] + [WHOLE] * 4,
        out_specs=(WHOLE, WHOLE),
        compiler_params=LIMIT,
        cost_estimate=cost(2**26, 2**20),
    )(meta, both, swap_near(both), swap_wrap(both), swap_far(both))

    tile_own, tile_other = pl.pallas_call(
        tile_kernel,
        out_shape=(shape((256, width), F32), shape((256, width), BF16)),
        in_specs=[WHOLE] * 4,
        out_specs=(WHOLE, WHOLE),
        compiler_params=LIMIT,
        cost_estimate=cost(2**28, 2**21),
    )(sums, weighted, share_hit, plane_emb)
    tile_chip = (tile_own + swap_core(tile_other).astype(F32)).astype(BF16)

    def add(a, swap):
        return a.astype(F32) + swap(a).astype(F32)

    tile_grad = jnp.concatenate(
        [
            add(add(tile_chip[:128], swap_near).astype(BF16), swap_wrap),
            add(add(tile_chip[128:], swap_wrap).astype(BF16), swap_near),
        ],
        axis=0,
    )
    new_mean = 0.9 * tile_mean + 0.1 * tile_grad
    new_var = 0.999 * tile_var + 0.001 * tile_grad * tile_grad
    new_tiles = label_tiles - 0.001 * (new_mean * CORR_ONE) / (jnp.sqrt(new_var * CORR_TWO) + 1e-08)
    return (loss, new_tiles, new_mean, new_var, grad_in, grad_out)


def solution(mesh):
    grid = Mesh(mesh.devices.reshape(2, 2, 4, 4, 2), ("h", "l", "x", "z", "c"))
    every, plane, group = ("h", "l", "x", "z", "c"), ("x", "z", "c"), ("h", "l")
    return jax.shard_map(
        on_device,
        mesh=grid,
        in_specs=(
            P(every, None, None),
            P(every),
            P(plane, None),
            P(plane, None),
            P(),
            P(plane, None),
            P(plane, None),
            P(plane, None),
            P(group, None),
            P(group, None),
            P(),
        ),
        out_specs=(
            P(every),
            P(plane, None),
            P(plane, None),
            P(plane, None),
            P(plane, None),
            P(plane, None),
        ),
        check_vma=False,
    )
```

```python
import jax
import jax.numpy as jnp
from jax import lax
from jax.experimental import pallas as pl
from jax.experimental.pallas import tpu as pltpu
from jax.sharding import Mesh, PartitionSpec as P

LPC = 4
POS = 4
POS_SCALE = 32768.0

NORM_EPS = 1e-05
INV_ROOT_TWO = 0.7071067811865476
INV_ROOT_TWO_PI = 0.3989422804014327
CORR_ONE = 1.000026562104397
CORR_TWO = 10.50333528

F32 = jnp.float32
BF16 = jnp.bfloat16
CHIPS = ("x", "z")
FIRST = (((0,), (0,)), ((), ()))
LAST = (((1,), (1,)), ((), ()))


def swap_core(a):
    return lax.ppermute(a, "c", [(0, 1), (1, 0)])


def swap_near(a):
    return lax.ppermute(a, "l", [(0, 1), (1, 0)])


def swap_diag(a):
    return lax.ppermute(a, ("l", "c"), [(0, 3), (3, 0), (1, 2), (2, 1)])


def swap_far(a):
    return lax.ppermute(a, "h", [(0, 1), (1, 0)])


def swap_wrap(a):
    return lax.ppermute(a, ("h", "l"), [(0, 3), (3, 0), (1, 2), (2, 1)])


def round_bf16(a):
    return lax.reduce_precision(a, 8, 7)


def gather_chips(a):
    return lax.all_to_all(a, CHIPS, 0, 0, tiled=True)


WHOLE = pl.BlockSpec(memory_space=pltpu.VMEM)
SCALARS = pl.BlockSpec(memory_space=pltpu.SMEM)
ANYWHERE = pl.BlockSpec(memory_space=pl.ANY)
LIMIT = pltpu.CompilerParams(vmem_limit_bytes=20 * 1024 * 1024)
MOST = pltpu.CompilerParams(vmem_limit_bytes=60 * 1024 * 1024)


def shape(dims, dtype):
    return jax.ShapeDtypeStruct(dims, dtype)


def cost(flops, data, special=0):
    return pl.CostEstimate(flops=flops, bytes_accessed=data, transcendentals=special)


def iota(dims, axis):
    return lax.broadcasted_iota(jnp.int32, dims, axis)


def place_of():
    core, high, low = (lax.axis_index(axis) for axis in ("c", "h", "l"))
    return core, high + low - 2 * high * low


def pick_kernel(w_in, mine, theirs):
    core, role = place_of()
    part = jnp.where(iota((512, 256), 1) < 128, core * 2 + role, 2 - core * 2 + role)
    at = iota((512, 256), 1) % 128
    spread = (iota((512, 256), 0) == at // 32 * 128 + part * 32 + at % 32).astype(BF16)
    for i in range(4):
        got = jnp.dot(w_in[:, i * 512 : i * 512 + 512], spread, preferred_element_type=F32).astype(BF16)
        mine[:, i * 128 : i * 128 + 128] = got[:, :128]
        theirs[:, i * 128 : i * 128 + 128] = got[:, 128:]


def lay_kernel(mine, theirs, w_out, out, block, sems):
    core, role = place_of()
    block[:32] = jnp.where(role == 0, w_out[:32], w_out[32:])
    block[32:, :512] = jnp.where(core == 0, mine[...], theirs[...])
    block[32:, 512:] = jnp.where(core == 0, theirs[...], mine[...])
    copies = [pltpu.make_async_copy(block, out.at[i], sems.at[i]) for i in range(16)]
    for copy in copies:
        copy.start()
    for copy in copies:
        copy.wait()


def forward_kernel(tok_a, tok_b, weights, part_a, part_b, hidden, slope, w_in, w_out, sems):
    copies = [
        pltpu.make_async_copy(
            weights.at[:, 32:64, k * 512 : k * 512 + 512], w_in.at[:, k * 32 : k * 32 + 32], sems.at[k]
        )
        for k in range(2)
    ]
    copies.append(pltpu.make_async_copy(weights.at[:, 0:32], w_out, sems.at[2]))
    for copy in copies:
        copy.start()
    copies[0].wait()
    copies[1].wait()
    for k, (tok, part) in enumerate(((tok_a, part_a), (tok_b, part_b))):
        pre_act = jnp.dot(tok[...], w_in[...].reshape(1024, 512), preferred_element_type=F32)
        normal_cdf = 0.5 * (1.0 + lax.erf(pre_act * INV_ROOT_TWO))
        act = (pre_act * normal_cdf).astype(BF16)
        hidden[k * 256 : k * 256 + 256] = act
        slope[k * 256 : k * 256 + 256] = (
            normal_cdf + pre_act * jnp.exp(-0.5 * pre_act * pre_act) * INV_ROOT_TWO_PI
        )
        if k == 0:
            copies[2].wait()
        part[...] = jnp.dot(
            act, w_out[...].reshape(512, 1024), preferred_element_type=F32
        ).astype(part.dtype)


def forward(tok_a, tok_b, weights, flops):
    return pl.pallas_call(
        forward_kernel,
        out_shape=(
            shape((256, 1024), BF16),
            shape((256, 1024), F32),
            shape((512, 512), BF16),
            shape((512, 512), F32),
        ),
        in_specs=[WHOLE, WHOLE, ANYWHERE],
        out_specs=(WHOLE,) * 4,
        scratch_shapes=[
            pltpu.VMEM((16, 64, 512), BF16),
            pltpu.VMEM((16, 32, 1024), BF16),
            pltpu.SemaphoreType.DMA((3,)),
        ],
        compiler_params=LIMIT,
        cost_estimate=cost(flops, 6 * 2**20, 2**19),
    )(tok_a, tok_b, weights)


def norm_kernel(lengths, tok, part, from_core, from_near, gain, rows, emb_hbm, emb, sem):
    embs = []
    for d in range(8):
        at = pl.ds(d * 32, 32)
        summed = tok[at].astype(F32) + (
            part[at] + from_core[at].astype(F32) + from_near[at].astype(F32)
        )
        centred = summed - jnp.mean(summed, axis=-1, keepdims=True)
        inv = lax.rsqrt(jnp.mean(centred * centred, axis=-1, keepdims=True) + NORM_EPS)
        normed = centred * inv
        count = jnp.full((32, 1), lengths[d], jnp.int32).astype(F32)
        share = jnp.where(iota((32, 1), 0).astype(F32) < count, 1.0, 0.0) / count
        embs.append(jnp.sum(normed * gain[...] * share, axis=0, keepdims=True))
        high = inv.astype(BF16).astype(F32)
        lane = iota((32, 128), 1)
        extra = jnp.where(lane == 0, high, jnp.where(lane == 1, inv - high, jnp.where(lane == 2, count, 0.0)))
        rows[at, :1024] = normed.astype(BF16)
        rows[at, 1024:] = extra.astype(BF16)
    docs = jnp.concatenate(embs, axis=0)
    emb[...] = jnp.concatenate([docs] * 16, axis=0).astype(BF16)
    copy = pltpu.make_async_copy(emb, emb_hbm, sem)
    copy.start()
    copy.wait()


def score_kernel(emb, tiles_hi, tiles_lo, live, packed_hbm, weighted, emb_buf, packed, sem):
    copy = pltpu.make_async_copy(emb, emb_buf, sem)
    copy.start()
    grow = (iota((128, 512), 0) == iota((128, 512), 1) // LPC).astype(BF16)
    mask = jnp.dot(live[...], grow, preferred_element_type=F32)
    copy.wait()
    docs = emb_buf[...]
    scores = lax.dot_general(docs, tiles_hi[...], LAST, preferred_element_type=F32)
    scores = scores + lax.dot_general(docs, tiles_lo[...], LAST, preferred_element_type=F32)
    value = mask * jnp.exp(scores)
    weighted[...] = value
    value_hi = value.astype(BF16)
    value_lo = (value - value_hi.astype(F32)).astype(BF16)
    part_emb = jnp.dot(value_hi, tiles_hi[...], preferred_element_type=F32)
    part_emb = part_emb + jnp.dot(value_hi, tiles_lo[...], preferred_element_type=F32)
    part_emb = part_emb + jnp.dot(value_lo, tiles_hi[...], preferred_element_type=F32)
    sums = jnp.sum(value, axis=1, keepdims=True) * 0.5
    high = sums.astype(BF16).astype(F32)
    row, lane = iota((128, 128), 0), iota((128, 128), 1)
    chosen = row // 8 == lane
    same = (row % 8 == lane % 8).astype(BF16)
    for k, part in enumerate((high, sums - high)):
        table = jnp.where(chosen, part, 0.0).astype(BF16)
        packed[:, 1024 + k * 128 : 1152 + k * 128] = jnp.dot(
            same, table, preferred_element_type=F32
        ).astype(BF16)
    packed[:, :1024] = part_emb.astype(BF16)
    copy = pltpu.make_async_copy(packed, packed_hbm, sem)
    copy.start()
    copy.wait()


def settle_kernel(meta, got_hbm, pos, emb, grad, loss, sums, got, sem):
    copy = pltpu.make_async_copy(got_hbm, got, sem)
    copy.start()
    copy.wait()
    total = got[0].astype(F32)
    for i in range(1, 16):
        total = total + got[i].astype(F32)
    every = (total[:, 1024:1152] + total[:, 1152:1280]) * 2.0
    sums[...] = every
    expsum = jnp.sum(jnp.where(iota((8, 128), 1) == meta[2], every, 0.0), axis=1, keepdims=True)
    pos_mean = pos[...]
    grad[...] = total[:, :1024] / expsum - pos_mean
    picked = jnp.sum(emb[...].astype(F32)[:8] * pos_mean, axis=1, keepdims=True)
    loss[...] = jnp.broadcast_to(jnp.log(expsum) - picked, (8, 128))


def tile_kernel(sums, weighted, share_hit, emb, own, other):
    rows = jnp.concatenate([sums[...]] * 16, axis=0)
    chosen = iota((128, 128), 0) // 8 == iota((128, 128), 1)
    column = jnp.sum(jnp.where(chosen, rows, 0.0), axis=1, keepdims=True)
    grad = weighted[...] / column - share_hit[...]
    grad_hi = grad.astype(BF16)
    grad_lo = (grad - grad_hi.astype(F32)).astype(BF16)
    for k, out in enumerate((own, other)):
        at = slice(k * 256, k * 256 + 256)
        part = lax.dot_general(grad_hi[:, at], emb[...], FIRST, preferred_element_type=F32)
        part = part + lax.dot_general(grad_lo[:, at], emb[...], FIRST, preferred_element_type=F32)
        out[...] = part.astype(out.dtype)


def backward_kernel(*refs):
    grads, gain = refs[:4], refs[4]
    rows, toks = refs[5:9], refs[9:13]
    hiddens, slopes, weights, out = refs[13:15], refs[15:17], refs[17], refs[18]
    row_buf, tok_buf, hid_buf, slope_buf, w_out, sum_grad, act_grad, result, sems = refs[19:]
    sent = []
    first = pltpu.make_async_copy(weights.at[:, 0:32], w_out, sems.at[0])
    first.start()
    row_copies, tok_copies, hid_copies, slope_copies = [], [], [], []
    for k in range(4):
        at = pl.ds(k * 256, 256)
        row_copies.append(pltpu.make_async_copy(rows[k], row_buf.at[at], sems.at[1 + k]))
        row_copies[k].start()
    for k in range(2):
        at = pl.ds(k * 512, 512)
        slope_copies.append(pltpu.make_async_copy(slopes[k], slope_buf.at[at], sems.at[5 + k]))
        slope_copies[k].start()
    for k in range(2):
        at = pl.ds(k * 512, 512)
        hid_copies.append(pltpu.make_async_copy(hiddens[k], hid_buf.at[at], sems.at[7 + k]))
        hid_copies[k].start()
    for k in range(4):
        at = pl.ds(k * 256, 256)
        tok_copies.append(pltpu.make_async_copy(toks[k], tok_buf.at[at], sems.at[9 + k]))
        tok_copies[k].start()
    spread = (iota((128, 256), 0) // 2 == iota((128, 256), 1) // 128).astype(BF16)
    spread = jnp.where((iota((128, 256), 0) < 3), spread, jnp.zeros_like(spread))
    ones = jnp.ones((32, 128), BF16)
    own_doc = iota((256, 16), 0) // 32 == iota((256, 16), 1) % 8
    place = (iota((256, 128), 0) % 32).astype(F32)
    for k in range(4):
        row_copies[k].wait()
        grad = grads[k][...] * gain[...]
        grad_dev = grad - jnp.mean(grad, axis=-1, keepdims=True)
        grad_hi = grad.astype(BF16)
        grad_lo = (grad - grad_hi.astype(F32)).astype(BF16)
        rows_at = pl.ds(k * 256, 256)
        factors = jnp.dot(row_buf[rows_at, 1024:], spread, preferred_element_type=F32)
        count = factors[:, 128:]
        factor = jnp.where(place < count, 1.0, 0.0) / count * factors[:, :128]
        along = lax.dot_general(
            row_buf[rows_at, :1024],
            jnp.concatenate([grad_hi, grad_lo], axis=0),
            LAST,
            preferred_element_type=F32,
        )
        along = jnp.where(own_doc, along, 0.0) * (1.0 / 1024.0)
        along_hi = along.astype(BF16)
        along_lo = (along - along_hi.astype(F32)).astype(BF16)
        along = jnp.dot(
            jnp.concatenate([along_hi, along_lo], axis=1), ones, preferred_element_type=F32
        )
        for d in range(8):
            at = pl.ds(k * 256 + d * 32, 32)
            here = slice(d * 32, d * 32 + 32)
            norm = row_buf[at, :1024].astype(F32)
            wide = jnp.concatenate([along[here]] * 8, axis=1)
            scale = jnp.concatenate([factor[here]] * 8, axis=1)
            sum_grad[at] = ((grad_dev[d : d + 1] - norm * wide) * scale).astype(BF16)
        if k == 0:
            first.wait()
        if k % 2 == 0:
            slope_copies[k // 2].wait()
        at = pl.ds(k * 256, 256)
        back = lax.dot_general(
            sum_grad[at], w_out[...].reshape(512, 1024), LAST, preferred_element_type=F32
        )
        act_grad[at] = (back * slope_buf[at]).astype(BF16)
    for copy in hid_copies:
        copy.wait()
    for i in range(4):
        part = lax.dot_general(
            hid_buf[:, i * 128 : i * 128 + 128], sum_grad[...], FIRST, preferred_element_type=F32
        )
        at = pl.ds(i * 4, 4)
        result[at, :32] = part.astype(BF16).reshape(4, 32, 1024)
        sent.append(pltpu.make_async_copy(result.at[at, 0:32], out.at[at, 0:32], sems.at[13 + i]))
        sent[-1].start()
    for copy in tok_copies:
        copy.wait()
    for i in range(4):
        part = lax.dot_general(
            tok_buf[:, i * 256 : i * 256 + 256], act_grad[...], FIRST, preferred_element_type=F32
        ).astype(BF16).reshape(4, 2, 32, 512)
        at = pl.ds(i * 4, 4)
        result[at, 32:, :512] = part[:, 0]
        result[at, 32:, 512:] = part[:, 1]
        sent.append(pltpu.make_async_copy(result.at[at, 32:64], out.at[at, 32:64], sems.at[17 + i]))
        sent[-1].start()
    for copy in sent:
        copy.wait()


def backward(grads, gain, rows, toks, hiddens, slopes, weights):
    return pl.pallas_call(
        backward_kernel,
        out_shape=shape((16, 64, 1024), BF16),
        in_specs=[WHOLE] * 5 + [ANYWHERE] * 13,
        out_specs=ANYWHERE,
        scratch_shapes=[
            pltpu.VMEM((1024, 1152), BF16),
            pltpu.VMEM((1024, 1024), BF16),
            pltpu.VMEM((1024, 512), BF16),
            pltpu.VMEM((1024, 512), F32),
            pltpu.VMEM((16, 32, 1024), BF16),
            pltpu.VMEM((1024, 1024), BF16),
            pltpu.VMEM((1024, 512), BF16),
            pltpu.VMEM((16, 64, 1024), BF16),
            pltpu.SemaphoreType.DMA((21,)),
        ],
        compiler_params=MOST,
        cost_estimate=cost(3 * 2**30, 10 * 2**20),
    )(*grads, gain, *rows, *toks, *hiddens, *slopes, weights)


def total_kernel(meta, got, out, keep, give):
    total = got[0].astype(F32)
    for i in range(1, 16):
        total = total + got[i].astype(F32)
    total = total.astype(BF16)
    core, step = meta[0], pl.program_id(0)

    @pl.when(step < 2)
    def _():
        out[...] = total

    @pl.when(step >= 2)
    def _():
        keep[...] = jnp.where(core == 0, total[:, :512], total[:, 512:])
        give[...] = jnp.where(core == 0, total[:, 512:], total[:, :512])


def place_kernel(meta, own, near, wrap, far, grad_in, grad_out):
    core, role = meta[0], meta[1]
    mine = own[:32].astype(F32) + wrap[:32].astype(F32)
    theirs = near[:32].astype(F32) + far[:32].astype(F32)
    grad_out[:32] = jnp.where(role == 0, mine, theirs)
    grad_out[32:] = jnp.where(role == 0, theirs, mine)
    row, lane = iota((1024, 512), 0), iota((1024, 512), 1)
    piece, at = row // 128, row % 128
    swapped, flipped = piece % 2, piece // 4
    part = (core + swapped - 2 * core * swapped) * 2 + (role + flipped - 2 * role * flipped)
    spread = (lane == at // 32 * 128 + part * 32 + at % 32).astype(BF16)
    blocks = [
        jnp.concatenate(
            [
                a[32:, k * 512 + i * 128 : k * 512 + i * 128 + 128]
                for a in (own, wrap, near, far)
                for k in range(2)
            ],
            axis=1,
        )
        for i in range(4)
    ]
    placed = jnp.dot(jnp.concatenate(blocks, axis=0), spread, preferred_element_type=F32)
    for i in range(4):
        grad_in[:, i * 512 : i * 512 + 512] = placed[i * 32 : i * 32 + 32]


def on_device(
    states,
    lengths,
    w_in,
    w_out,
    norm_gain,
    label_tiles,
    tile_mean,
    tile_var,
    shortlist,
    positives,
    owner_map,
):
    docs, length, width = states.shape
    core = lax.axis_index("c")
    high, low = lax.axis_index("h"), lax.axis_index("l")
    role = high + low - 2 * high * low
    chip = lax.axis_index("x") * 4 + lax.axis_index("z")
    meta = jnp.stack([core, role, chip]).astype(jnp.int32)
    gain = norm_gain.reshape(1, width)
    own_tok = states.reshape(docs * length, width)

    mine, theirs = pl.pallas_call(
        pick_kernel,
        out_shape=(shape((32, 512), BF16),) * 2,
        in_specs=[WHOLE],
        out_specs=(WHOLE, WHOLE),
        compiler_params=LIMIT,
        cost_estimate=cost(2**25, 2**18),
    )(w_in)
    block = pl.pallas_call(
        lay_kernel,
        out_shape=shape((16, 64, width), BF16),
        in_specs=[WHOLE, WHOLE, WHOLE],
        out_specs=ANYWHERE,
        scratch_shapes=[pltpu.VMEM((64, width), BF16), pltpu.SemaphoreType.DMA((16,))],
        compiler_params=LIMIT,
        cost_estimate=cost(0, 2**21),
    )(mine, swap_core(theirs), w_out)
    block, own_tok, label_tiles, shortlist, positives, owner_map = lax.optimization_barrier(
        (block, own_tok, label_tiles, shortlist, positives, owner_map)
    )
    weights = gather_chips(block)

    core_tok, near_tok, diag_tok = swap_core(own_tok), swap_near(own_tok), swap_diag(own_tok)

    oth_tiles = swap_core(label_tiles)
    slots = jnp.concatenate(
        [(chip * 2 + core) * 64 + jnp.arange(64), (chip * 2 + 1 - core) * 64 + jnp.arange(64)]
    ).astype(jnp.int32)
    all_clusters = jnp.arange(owner_map.shape[0], dtype=jnp.int32)
    owner_match = owner_map[:, None] == slots[None, :]
    cluster_ids = jnp.sum(jnp.where(owner_match, all_clusters[:, None], 0), axis=0)
    pick = lambda a: lax.dynamic_index_in_dim(a.reshape(16, 2, 8, -1), core, 1, False).reshape(128, -1)
    short, posit = pick(shortlist), pick(positives)
    cluster_live = jnp.max(
        (short[:, :, None] == cluster_ids[None, None, :]).astype(F32), axis=1
    ).astype(BF16)
    tiles = jnp.concatenate([label_tiles, oth_tiles], axis=0)
    tiles_top = round_bf16(tiles)
    tiles_hi, tiles_lo = tiles_top.astype(BF16), (tiles - tiles_top).astype(BF16)
    cluster_hit = (posit[:, :, None] // LPC == cluster_ids[None, None, :]).astype(F32)
    offset_hit = (
        posit[:, :, None] % LPC == jnp.arange(LPC, dtype=jnp.int32)[None, None, :]
    ).astype(F32)
    hits = jnp.sum(cluster_hit[:, :, :, None] * offset_hit[:, :, None, :], axis=1).reshape(128, 512)
    share_hit = hits / POS
    hit = share_hit.astype(BF16)
    pos_part = jnp.dot(hit, tiles_hi, preferred_element_type=F32) + jnp.dot(
        hit, tiles_lo, preferred_element_type=F32
    )
    pos_part = (pos_part * POS_SCALE).astype(jnp.float16)
    weights, cluster_live, share_hit, pos_part, tiles_hi, tiles_lo = lax.optimization_barrier(
        (weights, cluster_live, share_hit, pos_part, tiles_hi, tiles_lo)
    )

    near_a, near_b, near_hidden, near_slope = forward(diag_tok, near_tok, weights, 2**30)
    near_a, core_tok = lax.optimization_barrier((near_a, core_tok))
    own_a, own_b, own_hidden, own_slope = forward(core_tok, own_tok, weights, 2**30)
    near_a, own_a, own_b = lax.optimization_barrier((swap_core(near_a), own_a, own_b))
    near_sum = (near_b + near_a.astype(F32)).astype(BF16)
    near_sum, pos_part = lax.optimization_barrier((near_sum, pos_part))
    from_near = swap_near(near_sum)
    pos_got = gather_chips(pos_part.reshape(16, docs, width))
    from_near, pos_got = lax.optimization_barrier((from_near, pos_got))
    pos_mean = jnp.sum(pos_got.astype(F32), axis=0) * (1.0 / POS_SCALE)
    own_rows, emb = pl.pallas_call(
        norm_kernel,
        out_shape=(shape((256, 1152), BF16), shape((128, width), BF16)),
        in_specs=[SCALARS] + [WHOLE] * 5,
        out_specs=(WHOLE, ANYWHERE),
        scratch_shapes=[pltpu.VMEM((128, width), BF16), pltpu.SemaphoreType.DMA],
        compiler_params=LIMIT,
        cost_estimate=cost(2**22, 4 * 2**20),
    )(lengths, own_tok, own_b, swap_core(own_a), from_near, gain)

    plane_emb = gather_chips(emb.reshape(16, docs, width)).reshape(128, width)
    near_rows = swap_near(own_rows)
    packed, weighted = pl.pallas_call(
        score_kernel,
        out_shape=(shape((128, 1280), BF16), shape((128, 512), F32)),
        in_specs=[ANYWHERE] + [WHOLE] * 3,
        out_specs=(ANYWHERE, WHOLE),
        scratch_shapes=[
            pltpu.VMEM((128, width), BF16),
            pltpu.VMEM((128, 1280), BF16),
            pltpu.SemaphoreType.DMA,
        ],
        compiler_params=LIMIT,
        cost_estimate=cost(2**29, 3 * 2**20, 2**16),
    )(plane_emb, tiles_hi, tiles_lo, cluster_live)
    packed, near_rows = lax.optimization_barrier((packed, near_rows))
    core_rows, diag_rows = swap_core(own_rows), swap_core(near_rows)
    got = lax.all_to_all(packed.reshape(16, docs, 1280), CHIPS, 0, 0, tiled=True)
    emb_grad, loss, sums = pl.pallas_call(
        settle_kernel,
        out_shape=(shape((docs, width), F32), shape((docs, 128), F32), shape((docs, 128), F32)),
        in_specs=[SCALARS, ANYWHERE, WHOLE, WHOLE],
        out_specs=(WHOLE,) * 3,
        scratch_shapes=[
            pltpu.VMEM((16, docs, 1280), BF16),
            pltpu.SemaphoreType.DMA,
        ],
        compiler_params=LIMIT,
        cost_estimate=cost(2**20, 2**20),
    )(meta, got, pos_mean, emb)
    loss = loss[:, 0]

    grads = (swap_diag(emb_grad), swap_near(emb_grad), swap_core(emb_grad), emb_grad)
    send = backward(
        grads,
        gain,
        (diag_rows, near_rows, core_rows, own_rows),
        (diag_tok, near_tok, core_tok, own_tok),
        (near_hidden, own_hidden),
        (near_slope, own_slope),
        weights,
    )
    got = lax.all_to_all(send, CHIPS, 0, 0, tiled=True)
    part, keep, give = pl.pallas_call(
        total_kernel,
        out_shape=(shape((32, width), BF16), shape((32, 512), BF16), shape((32, 512), BF16)),
        grid=(4,),
        in_specs=[SCALARS, pl.BlockSpec((16, 16, width), lambda i: (0, i, 0))],
        out_specs=(
            pl.BlockSpec((16, width), lambda i: (jnp.minimum(i, 1), 0)),
            pl.BlockSpec((16, 512), lambda i: (jnp.maximum(i - 2, 0), 0)),
            pl.BlockSpec((16, 512), lambda i: (jnp.maximum(i - 2, 0), 0)),
        ),
        compiler_params=LIMIT,
        cost_estimate=cost(2**20, 2**21),
    )(meta, got)
    both = jnp.concatenate([part, jnp.concatenate([keep, swap_core(give)], axis=1)], axis=0)
    grad_in, grad_out = pl.pallas_call(
        place_kernel,
        out_shape=(shape((32, 2048), F32), shape((64, width), F32)),
        in_specs=[SCALARS] + [WHOLE] * 4,
        out_specs=(WHOLE, WHOLE),
        compiler_params=LIMIT,
        cost_estimate=cost(2**26, 2**20),
    )(meta, both, swap_near(both), swap_wrap(both), swap_far(both))

    tile_own, tile_other = pl.pallas_call(
        tile_kernel,
        out_shape=(shape((256, width), F32), shape((256, width), BF16)),
        in_specs=[WHOLE] * 4,
        out_specs=(WHOLE, WHOLE),
        compiler_params=LIMIT,
        cost_estimate=cost(2**28, 2**21),
    )(sums, weighted, share_hit, plane_emb)
    tile_chip = (tile_own + swap_core(tile_other).astype(F32)).astype(BF16)

    def add(a, swap):
        return a.astype(F32) + swap(a).astype(F32)

    tile_grad = jnp.concatenate(
        [
            add(add(tile_chip[:128], swap_near).astype(BF16), swap_wrap),
            add(add(tile_chip[128:], swap_wrap).astype(BF16), swap_near),
        ],
        axis=0,
    )
    new_mean = 0.9 * tile_mean + 0.1 * tile_grad
    new_var = 0.999 * tile_var + 0.001 * tile_grad * tile_grad
    new_tiles = label_tiles - 0.001 * (new_mean * CORR_ONE) / (jnp.sqrt(new_var * CORR_TWO) + 1e-08)
    return (loss, new_tiles, new_mean, new_var, grad_in, grad_out)


def solution(mesh):
    grid = Mesh(mesh.devices.reshape(2, 2, 4, 4, 2), ("h", "l", "x", "z", "c"))
    every, plane, group = ("h", "l", "x", "z", "c"), ("x", "z", "c"), ("h", "l")
    return jax.shard_map(
        on_device,
        mesh=grid,
        in_specs=(
            P(every, None, None),
            P(every),
            P(plane, None),
            P(plane, None),
            P(),
            P(plane, None),
            P(plane, None),
            P(plane, None),
            P(group, None),
            P(group, None),
            P(),
        ),
        out_specs=(
            P(every),
            P(plane, None),
            P(plane, None),
            P(plane, None),
            P(plane, None),
            P(plane, None),
        ),
        check_vma=False,
    )
```

```python
import jax
import jax.numpy as jnp
from jax import lax
from jax.experimental import pallas as pl
from jax.experimental.pallas import tpu as pltpu
from jax.sharding import Mesh, PartitionSpec as P

LPC = 4
POS = 4
POS_SCALE = 32768.0

NORM_EPS = 1e-05
INV_ROOT_TWO = 0.7071067811865476
INV_ROOT_TWO_PI = 0.3989422804014327
CORR_ONE = 1.000026562104397
CORR_TWO = 10.50333528

F32 = jnp.float32
BF16 = jnp.bfloat16
CHIPS = ("x", "z")
FIRST = (((0,), (0,)), ((), ()))
LAST = (((1,), (1,)), ((), ()))


def swap_core(a):
    return lax.ppermute(a, "c", [(0, 1), (1, 0)])


def swap_near(a):
    return lax.ppermute(a, "l", [(0, 1), (1, 0)])


def swap_diag(a):
    return lax.ppermute(a, ("l", "c"), [(0, 3), (3, 0), (1, 2), (2, 1)])


def swap_far(a):
    return lax.ppermute(a, "h", [(0, 1), (1, 0)])


def swap_wrap(a):
    return lax.ppermute(a, ("h", "l"), [(0, 3), (3, 0), (1, 2), (2, 1)])


def round_bf16(a):
    return lax.reduce_precision(a, 8, 7)


def gather_chips(a):
    return lax.all_to_all(a, CHIPS, 0, 0, tiled=True)


WHOLE = pl.BlockSpec(memory_space=pltpu.VMEM)
SCALARS = pl.BlockSpec(memory_space=pltpu.SMEM)
ANYWHERE = pl.BlockSpec(memory_space=pl.ANY)
LIMIT = pltpu.CompilerParams(vmem_limit_bytes=20 * 1024 * 1024)
MOST = pltpu.CompilerParams(vmem_limit_bytes=60 * 1024 * 1024)


def shape(dims, dtype):
    return jax.ShapeDtypeStruct(dims, dtype)


def cost(flops, data, special=0):
    return pl.CostEstimate(flops=flops, bytes_accessed=data, transcendentals=special)


def iota(dims, axis):
    return lax.broadcasted_iota(jnp.int32, dims, axis)


def place_of():
    core, high, low = (lax.axis_index(axis) for axis in ("c", "h", "l"))
    return core, high + low - 2 * high * low


def pick_kernel(w_in, mine, theirs):
    core, role = place_of()
    part = jnp.where(iota((512, 256), 1) < 128, core * 2 + role, 2 - core * 2 + role)
    at = iota((512, 256), 1) % 128
    spread = (iota((512, 256), 0) == at // 32 * 128 + part * 32 + at % 32).astype(BF16)
    for i in range(4):
        got = jnp.dot(w_in[:, i * 512 : i * 512 + 512], spread, preferred_element_type=F32).astype(BF16)
        mine[:, i * 128 : i * 128 + 128] = got[:, :128]
        theirs[:, i * 128 : i * 128 + 128] = got[:, 128:]


def lay_kernel(mine, theirs, w_out, out, block, sems):
    core, role = place_of()
    block[:32] = jnp.where(role == 0, w_out[:32], w_out[32:])
    block[32:, :512] = jnp.where(core == 0, mine[...], theirs[...])
    block[32:, 512:] = jnp.where(core == 0, theirs[...], mine[...])
    copies = [pltpu.make_async_copy(block, out.at[i], sems.at[i]) for i in range(16)]
    for copy in copies:
        copy.start()
    for copy in copies:
        copy.wait()


def forward_kernel(tok_a, tok_b, weights, part_a, part_b, hidden, slope, w_in, w_out, sems):
    copies = [
        pltpu.make_async_copy(
            weights.at[:, 32:64, k * 512 : k * 512 + 512], w_in.at[:, k * 32 : k * 32 + 32], sems.at[k]
        )
        for k in range(2)
    ]
    copies.append(pltpu.make_async_copy(weights.at[:, 0:32], w_out, sems.at[2]))
    for copy in copies:
        copy.start()
    copies[0].wait()
    copies[1].wait()
    for k, (tok, part) in enumerate(((tok_a, part_a), (tok_b, part_b))):
        pre_act = jnp.dot(tok[...], w_in[...].reshape(1024, 512), preferred_element_type=F32)
        normal_cdf = 0.5 * (1.0 + lax.erf(pre_act * INV_ROOT_TWO))
        act = (pre_act * normal_cdf).astype(BF16)
        hidden[k * 256 : k * 256 + 256] = act
        slope[k * 256 : k * 256 + 256] = (
            normal_cdf + pre_act * jnp.exp(-0.5 * pre_act * pre_act) * INV_ROOT_TWO_PI
        )
        if k == 0:
            copies[2].wait()
        part[...] = jnp.dot(
            act, w_out[...].reshape(512, 1024), preferred_element_type=F32
        ).astype(part.dtype)


def forward(tok_a, tok_b, weights, flops):
    return pl.pallas_call(
        forward_kernel,
        out_shape=(
            shape((256, 1024), BF16),
            shape((256, 1024), F32),
            shape((512, 512), BF16),
            shape((512, 512), F32),
        ),
        in_specs=[WHOLE, WHOLE, ANYWHERE],
        out_specs=(WHOLE,) * 4,
        scratch_shapes=[
            pltpu.VMEM((16, 64, 512), BF16),
            pltpu.VMEM((16, 32, 1024), BF16),
            pltpu.SemaphoreType.DMA((3,)),
        ],
        compiler_params=LIMIT,
        cost_estimate=cost(flops, 6 * 2**20, 2**19),
    )(tok_a, tok_b, weights)


def norm_kernel(lengths, tok, part, from_core, from_near, gain, rows, emb_hbm, emb, sem):
    embs = []
    for d in range(8):
        at = pl.ds(d * 32, 32)
        summed = tok[at].astype(F32) + (
            part[at] + from_core[at].astype(F32) + from_near[at].astype(F32)
        )
        centred = summed - jnp.mean(summed, axis=-1, keepdims=True)
        inv = lax.rsqrt(jnp.mean(centred * centred, axis=-1, keepdims=True) + NORM_EPS)
        normed = centred * inv
        count = jnp.full((32, 1), lengths[d], jnp.int32).astype(F32)
        share = jnp.where(iota((32, 1), 0).astype(F32) < count, 1.0, 0.0) / count
        embs.append(jnp.sum(normed * gain[...] * share, axis=0, keepdims=True))
        high = inv.astype(BF16).astype(F32)
        lane = iota((32, 128), 1)
        extra = jnp.where(lane == 0, high, jnp.where(lane == 1, inv - high, jnp.where(lane == 2, count, 0.0)))
        rows[at, :1024] = normed.astype(BF16)
        rows[at, 1024:] = extra.astype(BF16)
    docs = jnp.concatenate(embs, axis=0)
    emb[...] = jnp.concatenate([docs] * 16, axis=0).astype(BF16)
    copy = pltpu.make_async_copy(emb, emb_hbm, sem)
    copy.start()
    copy.wait()


def score_kernel(emb, tiles_hi, tiles_lo, live, packed_hbm, weighted, emb_buf, packed, sem):
    copy = pltpu.make_async_copy(emb, emb_buf, sem)
    copy.start()
    grow = (iota((128, 512), 0) == iota((128, 512), 1) // LPC).astype(BF16)
    mask = jnp.dot(live[...], grow, preferred_element_type=F32)
    copy.wait()
    docs = emb_buf[...]
    scores = lax.dot_general(docs, tiles_hi[...], LAST, preferred_element_type=F32)
    scores = scores + lax.dot_general(docs, tiles_lo[...], LAST, preferred_element_type=F32)
    value = mask * jnp.exp(scores)
    weighted[...] = value
    value_hi = value.astype(BF16)
    value_lo = (value - value_hi.astype(F32)).astype(BF16)
    part_emb = jnp.dot(value_hi, tiles_hi[...], preferred_element_type=F32)
    part_emb = part_emb + jnp.dot(value_hi, tiles_lo[...], preferred_element_type=F32)
    part_emb = part_emb + jnp.dot(value_lo, tiles_hi[...], preferred_element_type=F32)
    sums = jnp.sum(value, axis=1, keepdims=True) * 0.5
    high = sums.astype(BF16).astype(F32)
    row, lane = iota((128, 128), 0), iota((128, 128), 1)
    chosen = row // 8 == lane
    same = (row % 8 == lane % 8).astype(BF16)
    for k, part in enumerate((high, sums - high)):
        table = jnp.where(chosen, part, 0.0).astype(BF16)
        packed[:, 1024 + k * 128 : 1152 + k * 128] = jnp.dot(
            same, table, preferred_element_type=F32
        ).astype(BF16)
    packed[:, :1024] = part_emb.astype(BF16)
    copy = pltpu.make_async_copy(packed, packed_hbm, sem)
    copy.start()
    copy.wait()


def settle_kernel(meta, got_hbm, pos, emb, grad, loss, sums, got, sem):
    copy = pltpu.make_async_copy(got_hbm, got, sem)
    copy.start()
    copy.wait()
    total = got[0].astype(F32)
    for i in range(1, 16):
        total = total + got[i].astype(F32)
    every = (total[:, 1024:1152] + total[:, 1152:1280]) * 2.0
    sums[...] = every
    expsum = jnp.sum(jnp.where(iota((8, 128), 1) == meta[2], every, 0.0), axis=1, keepdims=True)
    pos_mean = pos[...]
    grad[...] = total[:, :1024] / expsum - pos_mean
    picked = jnp.sum(emb[...].astype(F32)[:8] * pos_mean, axis=1, keepdims=True)
    loss[...] = jnp.broadcast_to(jnp.log(expsum) - picked, (8, 128))


def tile_kernel(sums, weighted, share_hit, emb, own, other):
    rows = jnp.concatenate([sums[...]] * 16, axis=0)
    chosen = iota((128, 128), 0) // 8 == iota((128, 128), 1)
    column = jnp.sum(jnp.where(chosen, rows, 0.0), axis=1, keepdims=True)
    grad = weighted[...] / column - share_hit[...]
    grad_hi = grad.astype(BF16)
    grad_lo = (grad - grad_hi.astype(F32)).astype(BF16)
    for k, out in enumerate((own, other)):
        at = slice(k * 256, k * 256 + 256)
        part = lax.dot_general(grad_hi[:, at], emb[...], FIRST, preferred_element_type=F32)
        part = part + lax.dot_general(grad_lo[:, at], emb[...], FIRST, preferred_element_type=F32)
        out[...] = part.astype(out.dtype)


def turn_kernel(*refs):
    at = 0
    for part in refs[:-1]:
        refs[-1][:, at : at + part.shape[0]] = part[...].T
        at += part.shape[0]


def turn(*parts):
    dims = (parts[0].shape[1], sum(part.shape[0] for part in parts))
    return pl.pallas_call(
        turn_kernel,
        out_shape=shape(dims, BF16),
        in_specs=[WHOLE] * len(parts),
        out_specs=WHOLE,
        compiler_params=LIMIT,
        cost_estimate=cost(2**20, 2**22),
    )(*parts)


def backward_kernel(*refs):
    grads, gain = refs[:4], refs[4]
    rows, toks, hiddens = refs[5:9], refs[9], refs[10]
    slopes, weights, out = refs[11:13], refs[13], refs[14]
    row_buf, tok_buf, hid_buf, slope_buf, w_out, sum_grad, act_grad, result, sems = refs[15:]
    sent = []
    first = pltpu.make_async_copy(weights.at[:, 0:32], w_out, sems.at[0])
    first.start()
    row_copies, slope_copies = [], []
    for k in range(4):
        at = pl.ds(k * 256, 256)
        row_copies.append(pltpu.make_async_copy(rows[k], row_buf.at[at], sems.at[1 + k]))
        row_copies[k].start()
    for k in range(2):
        at = pl.ds(k * 512, 512)
        slope_copies.append(pltpu.make_async_copy(slopes[k], slope_buf.at[at], sems.at[5 + k]))
        slope_copies[k].start()
    hid_copy = pltpu.make_async_copy(hiddens, hid_buf, sems.at[7])
    hid_copy.start()
    tok_copy = pltpu.make_async_copy(toks, tok_buf, sems.at[8])
    tok_copy.start()
    for k in range(4):
        row_copies[k].wait()
        scaled_grad = grads[k][...] * gain[...]
        grad_mean = jnp.mean(scaled_grad, axis=-1, keepdims=True)
        for d in range(8):
            at = pl.ds(k * 256 + d * 32, 32)
            norm = row_buf[at, :1024].astype(F32)
            extra = row_buf[at, 1024:].astype(F32)
            lane = iota((32, 128), 1)
            scale = jnp.sum(jnp.where(lane < 2, extra, 0.0), axis=1, keepdims=True)
            count = jnp.sum(jnp.where(lane == 2, extra, 0.0), axis=1, keepdims=True)
            share = jnp.where(iota((32, 1), 0).astype(F32) < count, 1.0, 0.0) / count
            grad = scaled_grad[d : d + 1]
            along = jnp.mean(grad * norm, axis=-1, keepdims=True)
            sum_grad[at] = (
                (grad - grad_mean[d : d + 1] - norm * along) * (share * scale)
            ).astype(BF16)
        if k == 0:
            first.wait()
        if k % 2 == 0:
            slope_copies[k // 2].wait()
        at = pl.ds(k * 256, 256)
        back = lax.dot_general(
            sum_grad[at], w_out[...].reshape(512, 1024), LAST, preferred_element_type=F32
        )
        act_grad[at] = (back * slope_buf[at]).astype(BF16)
    hid_copy.wait()
    for i in range(2):
        part = jnp.dot(
            hid_buf[i * 256 : i * 256 + 256], sum_grad[...], preferred_element_type=F32
        )
        at = pl.ds(i * 8, 8)
        result[at, :32] = part.astype(BF16).reshape(8, 32, 1024)
        sent.append(pltpu.make_async_copy(result.at[at, 0:32], out.at[at, 0:32], sems.at[9 + i]))
        sent[-1].start()
    tok_copy.wait()
    for i in range(4):
        part = jnp.dot(
            tok_buf[i * 256 : i * 256 + 256], act_grad[...], preferred_element_type=F32
        ).astype(BF16).reshape(4, 2, 32, 512)
        at = pl.ds(i * 4, 4)
        result[at, 32:, :512] = part[:, 0]
        result[at, 32:, 512:] = part[:, 1]
        sent.append(pltpu.make_async_copy(result.at[at, 32:64], out.at[at, 32:64], sems.at[11 + i]))
        sent[-1].start()
    for copy in sent:
        copy.wait()


def backward(grads, gain, rows, toks, hiddens, slopes, weights):
    return pl.pallas_call(
        backward_kernel,
        out_shape=shape((16, 64, 1024), BF16),
        in_specs=[WHOLE] * 5 + [ANYWHERE] * 9,
        out_specs=ANYWHERE,
        scratch_shapes=[
            pltpu.VMEM((1024, 1152), BF16),
            pltpu.VMEM((1024, 1024), BF16),
            pltpu.VMEM((512, 1024), BF16),
            pltpu.VMEM((1024, 512), F32),
            pltpu.VMEM((16, 32, 1024), BF16),
            pltpu.VMEM((1024, 1024), BF16),
            pltpu.VMEM((1024, 512), BF16),
            pltpu.VMEM((16, 64, 1024), BF16),
            pltpu.SemaphoreType.DMA((15,)),
        ],
        compiler_params=MOST,
        cost_estimate=cost(3 * 2**30, 10 * 2**20),
    )(*grads, gain, *rows, toks, hiddens, *slopes, weights)


def total_kernel(meta, got, out, keep, give):
    total = got[0].astype(F32)
    for i in range(1, 16):
        total = total + got[i].astype(F32)
    total = total.astype(BF16)
    core, step = meta[0], pl.program_id(0)

    @pl.when(step < 2)
    def _():
        out[...] = total

    @pl.when(step >= 2)
    def _():
        keep[...] = jnp.where(core == 0, total[:, :512], total[:, 512:])
        give[...] = jnp.where(core == 0, total[:, 512:], total[:, :512])


def place_kernel(meta, own, near, wrap, far, grad_in, grad_out):
    core, role = meta[0], meta[1]
    mine = own[:32].astype(F32) + wrap[:32].astype(F32)
    theirs = near[:32].astype(F32) + far[:32].astype(F32)
    grad_out[:32] = jnp.where(role == 0, mine, theirs)
    grad_out[32:] = jnp.where(role == 0, theirs, mine)
    row, lane = iota((1024, 512), 0), iota((1024, 512), 1)
    piece, at = row // 128, row % 128
    swapped, flipped = piece % 2, piece // 4
    part = (core + swapped - 2 * core * swapped) * 2 + (role + flipped - 2 * role * flipped)
    spread = (lane == at // 32 * 128 + part * 32 + at % 32).astype(BF16)
    blocks = [
        jnp.concatenate(
            [
                a[32:, k * 512 + i * 128 : k * 512 + i * 128 + 128]
                for a in (own, wrap, near, far)
                for k in range(2)
            ],
            axis=1,
        )
        for i in range(4)
    ]
    placed = jnp.dot(jnp.concatenate(blocks, axis=0), spread, preferred_element_type=F32)
    for i in range(4):
        grad_in[:, i * 512 : i * 512 + 512] = placed[i * 32 : i * 32 + 32]


def on_device(
    states,
    lengths,
    w_in,
    w_out,
    norm_gain,
    label_tiles,
    tile_mean,
    tile_var,
    shortlist,
    positives,
    owner_map,
):
    docs, length, width = states.shape
    core = lax.axis_index("c")
    high, low = lax.axis_index("h"), lax.axis_index("l")
    role = high + low - 2 * high * low
    chip = lax.axis_index("x") * 4 + lax.axis_index("z")
    meta = jnp.stack([core, role, chip]).astype(jnp.int32)
    gain = norm_gain.reshape(1, width)
    own_tok = states.reshape(docs * length, width)

    mine, theirs = pl.pallas_call(
        pick_kernel,
        out_shape=(shape((32, 512), BF16),) * 2,
        in_specs=[WHOLE],
        out_specs=(WHOLE, WHOLE),
        compiler_params=LIMIT,
        cost_estimate=cost(2**25, 2**18),
    )(w_in)
    block = pl.pallas_call(
        lay_kernel,
        out_shape=shape((16, 64, width), BF16),
        in_specs=[WHOLE, WHOLE, WHOLE],
        out_specs=ANYWHERE,
        scratch_shapes=[pltpu.VMEM((64, width), BF16), pltpu.SemaphoreType.DMA((16,))],
        compiler_params=LIMIT,
        cost_estimate=cost(0, 2**21),
    )(mine, swap_core(theirs), w_out)
    block, own_tok, label_tiles, shortlist, positives, owner_map = lax.optimization_barrier(
        (block, own_tok, label_tiles, shortlist, positives, owner_map)
    )
    weights = gather_chips(block)

    core_tok, near_tok, diag_tok = swap_core(own_tok), swap_near(own_tok), swap_diag(own_tok)

    oth_tiles = swap_core(label_tiles)
    slots = jnp.concatenate(
        [(chip * 2 + core) * 64 + jnp.arange(64), (chip * 2 + 1 - core) * 64 + jnp.arange(64)]
    ).astype(jnp.int32)
    all_clusters = jnp.arange(owner_map.shape[0], dtype=jnp.int32)
    owner_match = owner_map[:, None] == slots[None, :]
    cluster_ids = jnp.sum(jnp.where(owner_match, all_clusters[:, None], 0), axis=0)
    pick = lambda a: lax.dynamic_index_in_dim(a.reshape(16, 2, 8, -1), core, 1, False).reshape(128, -1)
    short, posit = pick(shortlist), pick(positives)
    cluster_live = jnp.max(
        (short[:, :, None] == cluster_ids[None, None, :]).astype(F32), axis=1
    ).astype(BF16)
    tiles = jnp.concatenate([label_tiles, oth_tiles], axis=0)
    tiles_top = round_bf16(tiles)
    tiles_hi, tiles_lo = tiles_top.astype(BF16), (tiles - tiles_top).astype(BF16)
    cluster_hit = (posit[:, :, None] // LPC == cluster_ids[None, None, :]).astype(F32)
    offset_hit = (
        posit[:, :, None] % LPC == jnp.arange(LPC, dtype=jnp.int32)[None, None, :]
    ).astype(F32)
    hits = jnp.sum(cluster_hit[:, :, :, None] * offset_hit[:, :, None, :], axis=1).reshape(128, 512)
    share_hit = hits / POS
    hit = share_hit.astype(BF16)
    pos_part = jnp.dot(hit, tiles_hi, preferred_element_type=F32) + jnp.dot(
        hit, tiles_lo, preferred_element_type=F32
    )
    pos_part = (pos_part * POS_SCALE).astype(jnp.float16)
    turned_tok = turn(diag_tok, near_tok, core_tok, own_tok)
    weights, cluster_live, share_hit, pos_part, tiles_hi, tiles_lo, turned_tok = (
        lax.optimization_barrier(
            (weights, cluster_live, share_hit, pos_part, tiles_hi, tiles_lo, turned_tok)
        )
    )

    near_a, near_b, near_hidden, near_slope = forward(diag_tok, near_tok, weights, 2**30)
    near_a, core_tok = lax.optimization_barrier((near_a, core_tok))
    own_a, own_b, own_hidden, own_slope = forward(core_tok, own_tok, weights, 2**30)
    near_a, own_a, own_b = lax.optimization_barrier((swap_core(near_a), own_a, own_b))
    near_sum = (near_b + near_a.astype(F32)).astype(BF16)
    near_sum, pos_part = lax.optimization_barrier((near_sum, pos_part))
    from_near = swap_near(near_sum)
    pos_got = gather_chips(pos_part.reshape(16, docs, width))
    from_near, pos_got = lax.optimization_barrier((from_near, pos_got))
    pos_mean = jnp.sum(pos_got.astype(F32), axis=0) * (1.0 / POS_SCALE)
    own_rows, emb = pl.pallas_call(
        norm_kernel,
        out_shape=(shape((256, 1152), BF16), shape((128, width), BF16)),
        in_specs=[SCALARS] + [WHOLE] * 5,
        out_specs=(WHOLE, ANYWHERE),
        scratch_shapes=[pltpu.VMEM((128, width), BF16), pltpu.SemaphoreType.DMA],
        compiler_params=LIMIT,
        cost_estimate=cost(2**22, 4 * 2**20),
    )(lengths, own_tok, own_b, swap_core(own_a), from_near, gain)

    plane_emb = gather_chips(emb.reshape(16, docs, width)).reshape(128, width)
    turned_hidden = turn(near_hidden, own_hidden)
    plane_emb, turned_hidden = lax.optimization_barrier((plane_emb, turned_hidden))
    near_rows = swap_near(own_rows)
    packed, weighted = pl.pallas_call(
        score_kernel,
        out_shape=(shape((128, 1280), BF16), shape((128, 512), F32)),
        in_specs=[ANYWHERE] + [WHOLE] * 3,
        out_specs=(ANYWHERE, WHOLE),
        scratch_shapes=[
            pltpu.VMEM((128, width), BF16),
            pltpu.VMEM((128, 1280), BF16),
            pltpu.SemaphoreType.DMA,
        ],
        compiler_params=LIMIT,
        cost_estimate=cost(2**29, 3 * 2**20, 2**16),
    )(plane_emb, tiles_hi, tiles_lo, cluster_live)
    packed, near_rows = lax.optimization_barrier((packed, near_rows))
    core_rows, diag_rows = swap_core(own_rows), swap_core(near_rows)
    got = lax.all_to_all(packed.reshape(16, docs, 1280), CHIPS, 0, 0, tiled=True)
    emb_grad, loss, sums = pl.pallas_call(
        settle_kernel,
        out_shape=(shape((docs, width), F32), shape((docs, 128), F32), shape((docs, 128), F32)),
        in_specs=[SCALARS, ANYWHERE, WHOLE, WHOLE],
        out_specs=(WHOLE,) * 3,
        scratch_shapes=[
            pltpu.VMEM((16, docs, 1280), BF16),
            pltpu.SemaphoreType.DMA,
        ],
        compiler_params=LIMIT,
        cost_estimate=cost(2**20, 2**20),
    )(meta, got, pos_mean, emb)
    loss = loss[:, 0]

    grads = (swap_diag(emb_grad), swap_near(emb_grad), swap_core(emb_grad), emb_grad)
    send = backward(
        grads,
        gain,
        (diag_rows, near_rows, core_rows, own_rows),
        turned_tok,
        turned_hidden,
        (near_slope, own_slope),
        weights,
    )
    got = lax.all_to_all(send, CHIPS, 0, 0, tiled=True)
    part, keep, give = pl.pallas_call(
        total_kernel,
        out_shape=(shape((32, width), BF16), shape((32, 512), BF16), shape((32, 512), BF16)),
        grid=(4,),
        in_specs=[SCALARS, pl.BlockSpec((16, 16, width), lambda i: (0, i, 0))],
        out_specs=(
            pl.BlockSpec((16, width), lambda i: (jnp.minimum(i, 1), 0)),
            pl.BlockSpec((16, 512), lambda i: (jnp.maximum(i - 2, 0), 0)),
            pl.BlockSpec((16, 512), lambda i: (jnp.maximum(i - 2, 0), 0)),
        ),
        compiler_params=LIMIT,
        cost_estimate=cost(2**20, 2**21),
    )(meta, got)
    both = jnp.concatenate([part, jnp.concatenate([keep, swap_core(give)], axis=1)], axis=0)
    grad_in, grad_out = pl.pallas_call(
        place_kernel,
        out_shape=(shape((32, 2048), F32), shape((64, width), F32)),
        in_specs=[SCALARS] + [WHOLE] * 4,
        out_specs=(WHOLE, WHOLE),
        compiler_params=LIMIT,
        cost_estimate=cost(2**26, 2**20),
    )(meta, both, swap_near(both), swap_wrap(both), swap_far(both))

    tile_own, tile_other = pl.pallas_call(
        tile_kernel,
        out_shape=(shape((256, width), F32), shape((256, width), BF16)),
        in_specs=[WHOLE] * 4,
        out_specs=(WHOLE, WHOLE),
        compiler_params=LIMIT,
        cost_estimate=cost(2**28, 2**21),
    )(sums, weighted, share_hit, plane_emb)
    tile_chip = (tile_own + swap_core(tile_other).astype(F32)).astype(BF16)

    def add(a, swap):
        return a.astype(F32) + swap(a).astype(F32)

    tile_grad = jnp.concatenate(
        [
            add(add(tile_chip[:128], swap_near).astype(BF16), swap_wrap),
            add(add(tile_chip[128:], swap_wrap).astype(BF16), swap_near),
        ],
        axis=0,
    )
    new_mean = 0.9 * tile_mean + 0.1 * tile_grad
    new_var = 0.999 * tile_var + 0.001 * tile_grad * tile_grad
    new_tiles = label_tiles - 0.001 * (new_mean * CORR_ONE) / (jnp.sqrt(new_var * CORR_TWO) + 1e-08)
    return (loss, new_tiles, new_mean, new_var, grad_in, grad_out)


def solution(mesh):
    grid = Mesh(mesh.devices.reshape(2, 2, 4, 4, 2), ("h", "l", "x", "z", "c"))
    every, plane, group = ("h", "l", "x", "z", "c"), ("x", "z", "c"), ("h", "l")
    return jax.shard_map(
        on_device,
        mesh=grid,
        in_specs=(
            P(every, None, None),
            P(every),
            P(plane, None),
            P(plane, None),
            P(),
            P(plane, None),
            P(plane, None),
            P(plane, None),
            P(group, None),
            P(group, None),
            P(),
        ),
        out_specs=(
            P(every),
            P(plane, None),
            P(plane, None),
            P(plane, None),
            P(plane, None),
            P(plane, None),
        ),
        check_vma=False,
    )
```

```python
import jax
import jax.numpy as jnp
from jax import lax
from jax.experimental import pallas as pl
from jax.experimental.pallas import tpu as pltpu
from jax.sharding import Mesh, PartitionSpec as P

LPC = 4
POS = 4
POS_SCALE = 32768.0

NORM_EPS = 1e-05
INV_ROOT_TWO = 0.7071067811865476
INV_ROOT_TWO_PI = 0.3989422804014327
CORR_ONE = 1.000026562104397
CORR_TWO = 10.50333528

F32 = jnp.float32
BF16 = jnp.bfloat16
CHIPS = ("x", "z")
FIRST = (((0,), (0,)), ((), ()))
LAST = (((1,), (1,)), ((), ()))


def swap_core(a):
    return lax.ppermute(a, "c", [(0, 1), (1, 0)])


def swap_near(a):
    return lax.ppermute(a, "l", [(0, 1), (1, 0)])


def swap_diag(a):
    return lax.ppermute(a, ("l", "c"), [(0, 3), (3, 0), (1, 2), (2, 1)])


def swap_far(a):
    return lax.ppermute(a, "h", [(0, 1), (1, 0)])


def swap_wrap(a):
    return lax.ppermute(a, ("h", "l"), [(0, 3), (3, 0), (1, 2), (2, 1)])


def round_bf16(a):
    return lax.reduce_precision(a, 8, 7)


def gather_chips(a):
    return lax.all_to_all(a, CHIPS, 0, 0, tiled=True)


WHOLE = pl.BlockSpec(memory_space=pltpu.VMEM)
SCALARS = pl.BlockSpec(memory_space=pltpu.SMEM)
ANYWHERE = pl.BlockSpec(memory_space=pl.ANY)
LIMIT = pltpu.CompilerParams(vmem_limit_bytes=20 * 1024 * 1024)
MOST = pltpu.CompilerParams(vmem_limit_bytes=60 * 1024 * 1024)


def shape(dims, dtype):
    return jax.ShapeDtypeStruct(dims, dtype)


def cost(flops, data, special=0):
    return pl.CostEstimate(flops=flops, bytes_accessed=data, transcendentals=special)


def iota(dims, axis):
    return lax.broadcasted_iota(jnp.int32, dims, axis)


def place_of():
    core, high, low = (lax.axis_index(axis) for axis in ("c", "h", "l"))
    return core, high + low - 2 * high * low


def pick_kernel(w_in, w_out, mine, theirs, top):
    core, role = place_of()
    top[...] = jnp.where(role == 0, w_out[:32], w_out[32:])
    part = jnp.where(iota((512, 256), 1) < 128, core * 2 + role, 2 - core * 2 + role)
    at = iota((512, 256), 1) % 128
    spread = (iota((512, 256), 0) == at // 32 * 128 + part * 32 + at % 32).astype(BF16)
    for i in range(4):
        got = jnp.dot(w_in[:, i * 512 : i * 512 + 512], spread, preferred_element_type=F32).astype(BF16)
        mine[:, i * 128 : i * 128 + 128] = got[:, :128]
        theirs[:, i * 128 : i * 128 + 128] = got[:, 128:]


def lay_kernel(mine, theirs, top, out, block, sems):
    core, role = place_of()
    block[:32] = top[...]
    block[32:, :512] = jnp.where(core == 0, mine[...], theirs[...])
    block[32:, 512:] = jnp.where(core == 0, theirs[...], mine[...])
    copies = [pltpu.make_async_copy(block, out.at[i], sems.at[i]) for i in range(16)]
    for copy in copies:
        copy.start()
    for copy in copies:
        copy.wait()


def forward_kernel(tok_a, tok_b, weights, part_a, part_b, hidden, slope, w_in, w_out, sems):
    copies = [
        pltpu.make_async_copy(
            weights.at[:, 32:64, k * 512 : k * 512 + 512], w_in.at[:, k * 32 : k * 32 + 32], sems.at[k]
        )
        for k in range(2)
    ]
    copies.append(pltpu.make_async_copy(weights.at[:, 0:32], w_out, sems.at[2]))
    for copy in copies:
        copy.start()
    copies[0].wait()
    copies[1].wait()
    for k, (tok, part) in enumerate(((tok_a, part_a), (tok_b, part_b))):
        pre_act = jnp.dot(tok[...], w_in[...].reshape(1024, 512), preferred_element_type=F32)
        normal_cdf = 0.5 * (1.0 + lax.erf(pre_act * INV_ROOT_TWO))
        act = (pre_act * normal_cdf).astype(BF16)
        hidden[k * 256 : k * 256 + 256] = act
        slope[k * 256 : k * 256 + 256] = (
            normal_cdf + pre_act * jnp.exp(-0.5 * pre_act * pre_act) * INV_ROOT_TWO_PI
        )
        if k == 0:
            copies[2].wait()
        part[...] = jnp.dot(
            act, w_out[...].reshape(512, 1024), preferred_element_type=F32
        ).astype(part.dtype)


def forward(tok_a, tok_b, weights, flops):
    return pl.pallas_call(
        forward_kernel,
        out_shape=(
            shape((256, 1024), BF16),
            shape((256, 1024), F32),
            shape((512, 512), BF16),
            shape((512, 512), F32),
        ),
        in_specs=[WHOLE, WHOLE, ANYWHERE],
        out_specs=(WHOLE,) * 4,
        scratch_shapes=[
            pltpu.VMEM((16, 64, 512), BF16),
            pltpu.VMEM((16, 32, 1024), BF16),
            pltpu.SemaphoreType.DMA((3,)),
        ],
        compiler_params=LIMIT,
        cost_estimate=cost(flops, 6 * 2**20, 2**19),
    )(tok_a, tok_b, weights)


def norm_kernel(lengths, tok, part, from_core, from_near, gain, rows, emb_hbm, emb, sem):
    embs = []
    for d in range(8):
        at = pl.ds(d * 32, 32)
        summed = tok[at].astype(F32) + (
            part[at] + from_core[at].astype(F32) + from_near[at].astype(F32)
        )
        centred = summed - jnp.mean(summed, axis=-1, keepdims=True)
        inv = lax.rsqrt(jnp.mean(centred * centred, axis=-1, keepdims=True) + NORM_EPS)
        normed = centred * inv
        count = jnp.full((32, 1), lengths[d], jnp.int32).astype(F32)
        share = jnp.where(iota((32, 1), 0).astype(F32) < count, 1.0, 0.0) / count
        embs.append(jnp.sum(normed * gain[...] * share, axis=0, keepdims=True))
        high = inv.astype(BF16).astype(F32)
        lane = iota((32, 128), 1)
        extra = jnp.where(lane == 0, high, jnp.where(lane == 1, inv - high, jnp.where(lane == 2, count, 0.0)))
        rows[at, :1024] = normed.astype(BF16)
        rows[at, 1024:] = extra.astype(BF16)
    docs = jnp.concatenate(embs, axis=0)
    emb[...] = jnp.concatenate([docs] * 16, axis=0).astype(BF16)
    copy = pltpu.make_async_copy(emb, emb_hbm, sem)
    copy.start()
    copy.wait()


def score_kernel(emb, tiles_hi, tiles_lo, live, packed_hbm, weighted, emb_buf, packed, sem):
    copy = pltpu.make_async_copy(emb, emb_buf, sem)
    copy.start()
    grow = (iota((128, 512), 0) == iota((128, 512), 1) // LPC).astype(BF16)
    mask = jnp.dot(live[...], grow, preferred_element_type=F32)
    copy.wait()
    docs = emb_buf[...]
    scores = lax.dot_general(docs, tiles_hi[...], LAST, preferred_element_type=F32)
    scores = scores + lax.dot_general(docs, tiles_lo[...], LAST, preferred_element_type=F32)
    value = mask * jnp.exp(scores)
    weighted[...] = value
    value_hi = value.astype(BF16)
    value_lo = (value - value_hi.astype(F32)).astype(BF16)
    part_emb = jnp.dot(value_hi, tiles_hi[...], preferred_element_type=F32)
    part_emb = part_emb + jnp.dot(value_hi, tiles_lo[...], preferred_element_type=F32)
    part_emb = part_emb + jnp.dot(value_lo, tiles_hi[...], preferred_element_type=F32)
    sums = jnp.sum(value, axis=1, keepdims=True) * 0.5
    high = sums.astype(BF16).astype(F32)
    row, lane = iota((128, 128), 0), iota((128, 128), 1)
    chosen = row // 8 == lane
    same = (row % 8 == lane % 8).astype(BF16)
    for k, part in enumerate((high, sums - high)):
        table = jnp.where(chosen, part, 0.0).astype(BF16)
        packed[:, 1024 + k * 128 : 1152 + k * 128] = jnp.dot(
            same, table, preferred_element_type=F32
        ).astype(BF16)
    packed[:, :1024] = part_emb.astype(BF16)
    copy = pltpu.make_async_copy(packed, packed_hbm, sem)
    copy.start()
    copy.wait()


def settle_kernel(meta, got_hbm, pos, emb, grad, loss, sums, got, sem):
    copy = pltpu.make_async_copy(got_hbm, got, sem)
    copy.start()
    copy.wait()
    total = got[0].astype(F32)
    for i in range(1, 16):
        total = total + got[i].astype(F32)
    every = (total[:, 1024:1152] + total[:, 1152:1280]) * 2.0
    sums[...] = every
    expsum = jnp.sum(jnp.where(iota((8, 128), 1) == meta[2], every, 0.0), axis=1, keepdims=True)
    pos_mean = pos[...]
    grad[...] = total[:, :1024] / expsum - pos_mean
    picked = jnp.sum(emb[...].astype(F32)[:8] * pos_mean, axis=1, keepdims=True)
    loss[...] = jnp.broadcast_to(jnp.log(expsum) - picked, (8, 128))


def backward_kernel(*refs):
    grads, gain, sums = refs[:4], refs[4], refs[5]
    rows, toks = refs[6:10], refs[10:14]
    hiddens, slopes, weights = refs[14:16], refs[16:18], refs[18]
    tile_in, out, tile_out = refs[19:22], refs[22], refs[23:25]
    row_buf, tok_buf, hid_buf, slope_buf, w_out, sum_grad, act_grad, result = refs[25:33]
    tile_bufs, tile_results, sems = refs[33:36], refs[36:38], refs[38]
    sent = []
    first = pltpu.make_async_copy(weights.at[:, 0:32], w_out, sems.at[0])
    tile_copies = [
        pltpu.make_async_copy(part, buf, sems.at[21 + k])
        for k, (part, buf) in enumerate(zip(tile_in, tile_bufs))
    ]
    for copy in tile_copies:
        copy.start()
    first.start()
    row_copies, tok_copies, hid_copies, slope_copies = [], [], [], []
    for k in range(4):
        at = pl.ds(k * 256, 256)
        row_copies.append(pltpu.make_async_copy(rows[k], row_buf.at[at], sems.at[1 + k]))
        row_copies[k].start()
    for k in range(2):
        at = pl.ds(k * 512, 512)
        slope_copies.append(pltpu.make_async_copy(slopes[k], slope_buf.at[at], sems.at[5 + k]))
        slope_copies[k].start()
    for k in range(2):
        at = pl.ds(k * 512, 512)
        hid_copies.append(pltpu.make_async_copy(hiddens[k], hid_buf.at[at], sems.at[7 + k]))
        hid_copies[k].start()
    for k in range(4):
        at = pl.ds(k * 256, 256)
        tok_copies.append(pltpu.make_async_copy(toks[k], tok_buf.at[at], sems.at[9 + k]))
        tok_copies[k].start()
    for copy in tile_copies:
        copy.wait()
    weighted, share_hit, emb = tile_bufs
    chosen = iota((128, 128), 0) // 8 == iota((128, 128), 1)
    column = jnp.where(chosen, jnp.concatenate([sums[...]] * 16, axis=0), 0.0)
    logit = weighted[...] / jnp.sum(column, axis=1, keepdims=True) - share_hit[...]
    logit_hi = logit.astype(BF16)
    logit_lo = (logit - logit_hi.astype(F32)).astype(BF16)
    for k, part in enumerate(tile_results):
        at = slice(k * 256, k * 256 + 256)
        value = lax.dot_general(logit_hi[:, at], emb[...], FIRST, preferred_element_type=F32)
        value = value + lax.dot_general(logit_lo[:, at], emb[...], FIRST, preferred_element_type=F32)
        part[...] = value.astype(part.dtype)
        sent.append(pltpu.make_async_copy(part, tile_out[k], sems.at[24 + k]))
        sent[-1].start()
    for k in range(4):
        row_copies[k].wait()
        scaled_grad = grads[k][...] * gain[...]
        grad_mean = jnp.mean(scaled_grad, axis=-1, keepdims=True)
        for d in range(8):
            at = pl.ds(k * 256 + d * 32, 32)
            norm = row_buf[at, :1024].astype(F32)
            extra = row_buf[at, 1024:].astype(F32)
            lane = iota((32, 128), 1)
            scale = jnp.sum(jnp.where(lane < 2, extra, 0.0), axis=1, keepdims=True)
            count = jnp.sum(jnp.where(lane == 2, extra, 0.0), axis=1, keepdims=True)
            share = jnp.where(iota((32, 1), 0).astype(F32) < count, 1.0, 0.0) / count
            grad = scaled_grad[d : d + 1]
            along = jnp.mean(grad * norm, axis=-1, keepdims=True)
            sum_grad[at] = (
                (grad - grad_mean[d : d + 1] - norm * along) * (share * scale)
            ).astype(BF16)
        if k == 0:
            first.wait()
        if k % 2 == 0:
            slope_copies[k // 2].wait()
        at = pl.ds(k * 256, 256)
        back = lax.dot_general(
            sum_grad[at], w_out[...].reshape(512, 1024), LAST, preferred_element_type=F32
        )
        act_grad[at] = (back * slope_buf[at]).astype(BF16)
    for copy in hid_copies:
        copy.wait()
    for i in range(2):
        part = lax.dot_general(
            hid_buf[:, i * 256 : i * 256 + 256], sum_grad[...], FIRST, preferred_element_type=F32
        )
        at = pl.ds(i * 8, 8)
        result[at, :32] = part.astype(BF16).reshape(8, 32, 1024)
        sent.append(pltpu.make_async_copy(result.at[at, 0:32], out.at[at, 0:32], sems.at[13 + i]))
        sent[-1].start()
    for copy in tok_copies:
        copy.wait()
    for i in range(4):
        part = lax.dot_general(
            tok_buf[:, i * 256 : i * 256 + 256], act_grad[...], FIRST, preferred_element_type=F32
        ).astype(BF16).reshape(4, 2, 32, 512)
        at = pl.ds(i * 4, 4)
        result[at, 32:, :512] = part[:, 0]
        result[at, 32:, 512:] = part[:, 1]
        sent.append(pltpu.make_async_copy(result.at[at, 32:64], out.at[at, 32:64], sems.at[17 + i]))
        sent[-1].start()
    for copy in sent:
        copy.wait()


def backward(grads, gain, sums, rows, toks, hiddens, slopes, weights, tile_in):
    return pl.pallas_call(
        backward_kernel,
        out_shape=(
            shape((16, 64, 1024), BF16),
            shape((256, 1024), F32),
            shape((256, 1024), BF16),
        ),
        in_specs=[WHOLE] * 6 + [ANYWHERE] * 16,
        out_specs=(ANYWHERE,) * 3,
        scratch_shapes=[
            pltpu.VMEM((1024, 1152), BF16),
            pltpu.VMEM((1024, 1024), BF16),
            pltpu.VMEM((1024, 512), BF16),
            pltpu.VMEM((1024, 512), F32),
            pltpu.VMEM((16, 32, 1024), BF16),
            pltpu.VMEM((1024, 1024), BF16),
            pltpu.VMEM((1024, 512), BF16),
            pltpu.VMEM((16, 64, 1024), BF16),
            pltpu.VMEM((128, 512), F32),
            pltpu.VMEM((128, 512), F32),
            pltpu.VMEM((128, 1024), BF16),
            pltpu.VMEM((256, 1024), F32),
            pltpu.VMEM((256, 1024), BF16),
            pltpu.SemaphoreType.DMA((26,)),
        ],
        compiler_params=MOST,
        cost_estimate=cost(3 * 2**30, 10 * 2**20),
    )(*grads, gain, sums, *rows, *toks, *hiddens, *slopes, weights, *tile_in)


def total_kernel(meta, got, out, keep, give):
    total = got[0].astype(F32)
    for i in range(1, 16):
        total = total + got[i].astype(F32)
    total = total.astype(BF16)
    core, step = meta[0], pl.program_id(0)

    @pl.when(step < 2)
    def _():
        out[...] = total

    @pl.when(step >= 2)
    def _():
        keep[...] = jnp.where(core == 0, total[:, :512], total[:, 512:])
        give[...] = jnp.where(core == 0, total[:, 512:], total[:, :512])


def place_kernel(meta, own, near, wrap, far, grad_in, grad_out):
    core, role = meta[0], meta[1]
    mine = own[:32].astype(F32) + wrap[:32].astype(F32)
    theirs = near[:32].astype(F32) + far[:32].astype(F32)
    grad_out[:32] = jnp.where(role == 0, mine, theirs)
    grad_out[32:] = jnp.where(role == 0, theirs, mine)
    row, lane = iota((1024, 512), 0), iota((1024, 512), 1)
    piece, at = row // 128, row % 128
    swapped, flipped = piece % 2, piece // 4
    part = (core + swapped - 2 * core * swapped) * 2 + (role + flipped - 2 * role * flipped)
    spread = (lane == at // 32 * 128 + part * 32 + at % 32).astype(BF16)
    blocks = [
        jnp.concatenate(
            [
                a[32:, k * 512 + i * 128 : k * 512 + i * 128 + 128]
                for a in (own, wrap, near, far)
                for k in range(2)
            ],
            axis=1,
        )
        for i in range(4)
    ]
    placed = jnp.dot(jnp.concatenate(blocks, axis=0), spread, preferred_element_type=F32)
    for i in range(4):
        grad_in[:, i * 512 : i * 512 + 512] = placed[i * 32 : i * 32 + 32]


def on_device(
    states,
    lengths,
    w_in,
    w_out,
    norm_gain,
    label_tiles,
    tile_mean,
    tile_var,
    shortlist,
    positives,
    owner_map,
):
    docs, length, width = states.shape
    core = lax.axis_index("c")
    high, low = lax.axis_index("h"), lax.axis_index("l")
    role = high + low - 2 * high * low
    chip = lax.axis_index("x") * 4 + lax.axis_index("z")
    meta = jnp.stack([core, role, chip]).astype(jnp.int32)
    gain = norm_gain.reshape(1, width)
    own_tok = states.reshape(docs * length, width)

    mine, theirs, top = pl.pallas_call(
        pick_kernel,
        out_shape=(shape((32, 512), BF16),) * 2 + (shape((32, width), BF16),),
        in_specs=[WHOLE, WHOLE],
        out_specs=(WHOLE,) * 3,
        compiler_params=LIMIT,
        cost_estimate=cost(2**25, 2**18),
    )(w_in, w_out)
    block = pl.pallas_call(
        lay_kernel,
        out_shape=shape((16, 64, width), BF16),
        in_specs=[WHOLE, WHOLE, WHOLE],
        out_specs=ANYWHERE,
        scratch_shapes=[pltpu.VMEM((64, width), BF16), pltpu.SemaphoreType.DMA((16,))],
        compiler_params=LIMIT,
        cost_estimate=cost(0, 2**21),
    )(mine, swap_core(theirs), top)
    block, own_tok, label_tiles, shortlist, positives, owner_map = lax.optimization_barrier(
        (block, own_tok, label_tiles, shortlist, positives, owner_map)
    )
    weights = gather_chips(block)

    core_tok, near_tok, diag_tok = swap_core(own_tok), swap_near(own_tok), swap_diag(own_tok)

    oth_tiles = swap_core(label_tiles)
    slots = jnp.concatenate(
        [(chip * 2 + core) * 64 + jnp.arange(64), (chip * 2 + 1 - core) * 64 + jnp.arange(64)]
    ).astype(jnp.int32)
    all_clusters = jnp.arange(owner_map.shape[0], dtype=jnp.int32)
    owner_match = owner_map[:, None] == slots[None, :]
    cluster_ids = jnp.sum(jnp.where(owner_match, all_clusters[:, None], 0), axis=0)
    pick = lambda a: lax.dynamic_index_in_dim(a.reshape(16, 2, 8, -1), core, 1, False).reshape(128, -1)
    short, posit = pick(shortlist), pick(positives)
    cluster_live = jnp.max(
        (short[:, :, None] == cluster_ids[None, None, :]).astype(F32), axis=1
    ).astype(BF16)
    tiles = jnp.concatenate([label_tiles, oth_tiles], axis=0)
    tiles_top = round_bf16(tiles)
    tiles_hi, tiles_lo = tiles_top.astype(BF16), (tiles - tiles_top).astype(BF16)
    cluster_hit = (posit[:, :, None] // LPC == cluster_ids[None, None, :]).astype(F32)
    offset_hit = (
        posit[:, :, None] % LPC == jnp.arange(LPC, dtype=jnp.int32)[None, None, :]
    ).astype(F32)
    hits = jnp.sum(cluster_hit[:, :, :, None] * offset_hit[:, :, None, :], axis=1).reshape(128, 512)
    share_hit = hits / POS
    hit = share_hit.astype(BF16)
    pos_part = jnp.dot(hit, tiles_hi, preferred_element_type=F32) + jnp.dot(
        hit, tiles_lo, preferred_element_type=F32
    )
    pos_part = (pos_part * POS_SCALE).astype(jnp.float16)
    weights, cluster_live, share_hit, pos_part, tiles_hi, tiles_lo = lax.optimization_barrier(
        (weights, cluster_live, share_hit, pos_part, tiles_hi, tiles_lo)
    )

    near_a, near_b, near_hidden, near_slope = forward(diag_tok, near_tok, weights, 2**30)
    near_a, core_tok = lax.optimization_barrier((near_a, core_tok))
    own_a, own_b, own_hidden, own_slope = forward(core_tok, own_tok, weights, 2**30)
    near_a, own_a, own_b = lax.optimization_barrier((swap_core(near_a), own_a, own_b))
    near_sum = (near_b + near_a.astype(F32)).astype(BF16)
    near_sum, pos_part = lax.optimization_barrier((near_sum, pos_part))
    from_near = swap_near(near_sum)
    pos_got = gather_chips(pos_part.reshape(16, docs, width))
    from_near, pos_got = lax.optimization_barrier((from_near, pos_got))
    pos_mean = jnp.sum(pos_got.astype(F32), axis=0) * (1.0 / POS_SCALE)
    own_rows, emb = pl.pallas_call(
        norm_kernel,
        out_shape=(shape((256, 1152), BF16), shape((128, width), BF16)),
        in_specs=[SCALARS] + [WHOLE] * 5,
        out_specs=(WHOLE, ANYWHERE),
        scratch_shapes=[pltpu.VMEM((128, width), BF16), pltpu.SemaphoreType.DMA],
        compiler_params=LIMIT,
        cost_estimate=cost(2**22, 4 * 2**20),
    )(lengths, own_tok, own_b, swap_core(own_a), from_near, gain)

    plane_emb = gather_chips(emb.reshape(16, docs, width)).reshape(128, width)
    near_rows = swap_near(own_rows)
    packed, weighted = pl.pallas_call(
        score_kernel,
        out_shape=(shape((128, 1280), BF16), shape((128, 512), F32)),
        in_specs=[ANYWHERE] + [WHOLE] * 3,
        out_specs=(ANYWHERE, WHOLE),
        scratch_shapes=[
            pltpu.VMEM((128, width), BF16),
            pltpu.VMEM((128, 1280), BF16),
            pltpu.SemaphoreType.DMA,
        ],
        compiler_params=LIMIT,
        cost_estimate=cost(2**29, 3 * 2**20, 2**16),
    )(plane_emb, tiles_hi, tiles_lo, cluster_live)
    packed, near_rows = lax.optimization_barrier((packed, near_rows))
    core_rows, diag_rows = swap_core(own_rows), swap_core(near_rows)
    got = lax.all_to_all(packed.reshape(16, docs, 1280), CHIPS, 0, 0, tiled=True)
    emb_grad, loss, sums = pl.pallas_call(
        settle_kernel,
        out_shape=(shape((docs, width), F32), shape((docs, 128), F32), shape((docs, 128), F32)),
        in_specs=[SCALARS, ANYWHERE, WHOLE, WHOLE],
        out_specs=(WHOLE,) * 3,
        scratch_shapes=[
            pltpu.VMEM((16, docs, 1280), BF16),
            pltpu.SemaphoreType.DMA,
        ],
        compiler_params=LIMIT,
        cost_estimate=cost(2**20, 2**20),
    )(meta, got, pos_mean, emb)
    loss = loss[:, 0]

    grads = (swap_diag(emb_grad), swap_near(emb_grad), swap_core(emb_grad), emb_grad)
    send, tile_own, tile_other = backward(
        grads,
        gain,
        sums,
        (diag_rows, near_rows, core_rows, own_rows),
        (diag_tok, near_tok, core_tok, own_tok),
        (near_hidden, own_hidden),
        (near_slope, own_slope),
        weights,
        (weighted, share_hit, plane_emb),
    )
    got = lax.all_to_all(send, CHIPS, 0, 0, tiled=True)
    part, keep, give = pl.pallas_call(
        total_kernel,
        out_shape=(shape((32, width), BF16), shape((32, 512), BF16), shape((32, 512), BF16)),
        grid=(4,),
        in_specs=[SCALARS, pl.BlockSpec((16, 16, width), lambda i: (0, i, 0))],
        out_specs=(
            pl.BlockSpec((16, width), lambda i: (jnp.minimum(i, 1), 0)),
            pl.BlockSpec((16, 512), lambda i: (jnp.maximum(i - 2, 0), 0)),
            pl.BlockSpec((16, 512), lambda i: (jnp.maximum(i - 2, 0), 0)),
        ),
        compiler_params=LIMIT,
        cost_estimate=cost(2**20, 2**21),
    )(meta, got)
    both = jnp.concatenate([part, jnp.concatenate([keep, swap_core(give)], axis=1)], axis=0)
    grad_in, grad_out = pl.pallas_call(
        place_kernel,
        out_shape=(shape((32, 2048), F32), shape((64, width), F32)),
        in_specs=[SCALARS] + [WHOLE] * 4,
        out_specs=(WHOLE, WHOLE),
        compiler_params=LIMIT,
        cost_estimate=cost(2**26, 2**20),
    )(meta, both, swap_near(both), swap_wrap(both), swap_far(both))

    tile_chip = (tile_own + swap_core(tile_other).astype(F32)).astype(BF16)

    def add(a, swap):
        return a.astype(F32) + swap(a).astype(F32)

    tile_grad = jnp.concatenate(
        [
            add(add(tile_chip[:128], swap_near).astype(BF16), swap_wrap),
            add(add(tile_chip[128:], swap_wrap).astype(BF16), swap_near),
        ],
        axis=0,
    )
    new_mean = 0.9 * tile_mean + 0.1 * tile_grad
    new_var = 0.999 * tile_var + 0.001 * tile_grad * tile_grad
    new_tiles = label_tiles - 0.001 * (new_mean * CORR_ONE) / (jnp.sqrt(new_var * CORR_TWO) + 1e-08)
    return (loss, new_tiles, new_mean, new_var, grad_in, grad_out)


def solution(mesh):
    grid = Mesh(mesh.devices.reshape(2, 2, 4, 4, 2), ("h", "l", "x", "z", "c"))
    every, plane, group = ("h", "l", "x", "z", "c"), ("x", "z", "c"), ("h", "l")
    return jax.shard_map(
        on_device,
        mesh=grid,
        in_specs=(
            P(every, None, None),
            P(every),
            P(plane, None),
            P(plane, None),
            P(),
            P(plane, None),
            P(plane, None),
            P(plane, None),
            P(group, None),
            P(group, None),
            P(),
        ),
        out_specs=(
            P(every),
            P(plane, None),
            P(plane, None),
            P(plane, None),
            P(plane, None),
            P(plane, None),
        ),
        check_vma=False,
    )
```

```python
import jax
import jax.numpy as jnp
from jax import lax
from jax.experimental import pallas as pl
from jax.experimental.pallas import tpu as pltpu
from jax.sharding import Mesh, PartitionSpec as P

LPC = 4
POS = 4
POS_SCALE = 32768.0

NORM_EPS = 1e-05
INV_ROOT_TWO = 0.7071067811865476
INV_ROOT_TWO_PI = 0.3989422804014327
CORR_ONE = 1.000026562104397
CORR_TWO = 10.50333528

F32 = jnp.float32
BF16 = jnp.bfloat16
CHIPS = ("x", "z")
FIRST = (((0,), (0,)), ((), ()))
LAST = (((1,), (1,)), ((), ()))


def swap_core(a):
    return lax.ppermute(a, "c", [(0, 1), (1, 0)])


def swap_near(a):
    return lax.ppermute(a, "l", [(0, 1), (1, 0)])


def swap_diag(a):
    return lax.ppermute(a, ("l", "c"), [(0, 3), (3, 0), (1, 2), (2, 1)])


def swap_far(a):
    return lax.ppermute(a, "h", [(0, 1), (1, 0)])


def swap_wrap(a):
    return lax.ppermute(a, ("h", "l"), [(0, 3), (3, 0), (1, 2), (2, 1)])


def round_bf16(a):
    return lax.reduce_precision(a, 8, 7)


def gather_chips(a):
    return lax.all_to_all(a, CHIPS, 0, 0, tiled=True)


WHOLE = pl.BlockSpec(memory_space=pltpu.VMEM)
SCALARS = pl.BlockSpec(memory_space=pltpu.SMEM)
ANYWHERE = pl.BlockSpec(memory_space=pl.ANY)
LIMIT = pltpu.CompilerParams(vmem_limit_bytes=20 * 1024 * 1024)
MOST = pltpu.CompilerParams(vmem_limit_bytes=60 * 1024 * 1024)


def shape(dims, dtype):
    return jax.ShapeDtypeStruct(dims, dtype)


def cost(flops, data, special=0):
    return pl.CostEstimate(flops=flops, bytes_accessed=data, transcendentals=special)


def iota(dims, axis):
    return lax.broadcasted_iota(jnp.int32, dims, axis)


def place_of():
    core, high, low = (lax.axis_index(axis) for axis in ("c", "h", "l"))
    return core, high + low - 2 * high * low


def pick_kernel(w_in, mine, theirs):
    core, role = place_of()
    part = jnp.where(iota((512, 256), 1) < 128, core * 2 + role, 2 - core * 2 + role)
    at = iota((512, 256), 1) % 128
    spread = (iota((512, 256), 0) == at // 32 * 128 + part * 32 + at % 32).astype(BF16)
    for i in range(4):
        got = jnp.dot(w_in[:, i * 512 : i * 512 + 512], spread, preferred_element_type=F32).astype(BF16)
        mine[:, i * 128 : i * 128 + 128] = got[:, :128]
        theirs[:, i * 128 : i * 128 + 128] = got[:, 128:]


def lay_kernel(mine, theirs, w_out, out, block, sems):
    core, role = place_of()
    top = w_out.at[pl.ds(pl.multiple_of(role * 32, 32), 32)]
    copies = [pltpu.make_async_copy(top, out.at[i, 0:32], sems.at[i]) for i in range(16)]
    for copy in copies:
        copy.start()
    block[:, :512] = jnp.where(core == 0, mine[...], theirs[...])
    block[:, 512:] = jnp.where(core == 0, theirs[...], mine[...])
    for i in range(16):
        copies.append(pltpu.make_async_copy(block, out.at[i, 32:64], sems.at[16 + i]))
        copies[-1].start()
    for copy in copies:
        copy.wait()


def forward_kernel(tok_a, tok_b, weights, part_a, part_b, hidden, slope, w_in, w_out, sems):
    copies = [
        pltpu.make_async_copy(
            weights.at[:, 32:64, k * 512 : k * 512 + 512], w_in.at[:, k * 32 : k * 32 + 32], sems.at[k]
        )
        for k in range(2)
    ]
    copies.append(pltpu.make_async_copy(weights.at[:, 0:32], w_out, sems.at[2]))
    for copy in copies:
        copy.start()
    copies[0].wait()
    copies[1].wait()
    for k, (tok, part) in enumerate(((tok_a, part_a), (tok_b, part_b))):
        pre_act = jnp.dot(tok[...], w_in[...].reshape(1024, 512), preferred_element_type=F32)
        normal_cdf = 0.5 * (1.0 + lax.erf(pre_act * INV_ROOT_TWO))
        act = (pre_act * normal_cdf).astype(BF16)
        hidden[k * 256 : k * 256 + 256] = act
        slope[k * 256 : k * 256 + 256] = (
            normal_cdf + pre_act * jnp.exp(-0.5 * pre_act * pre_act) * INV_ROOT_TWO_PI
        )
        if k == 0:
            copies[2].wait()
        part[...] = jnp.dot(
            act, w_out[...].reshape(512, 1024), preferred_element_type=F32
        ).astype(part.dtype)


def forward(tok_a, tok_b, weights, flops):
    return pl.pallas_call(
        forward_kernel,
        out_shape=(
            shape((256, 1024), BF16),
            shape((256, 1024), F32),
            shape((512, 512), BF16),
            shape((512, 512), F32),
        ),
        in_specs=[WHOLE, WHOLE, ANYWHERE],
        out_specs=(WHOLE,) * 4,
        scratch_shapes=[
            pltpu.VMEM((16, 64, 512), BF16),
            pltpu.VMEM((16, 32, 1024), BF16),
            pltpu.SemaphoreType.DMA((3,)),
        ],
        compiler_params=LIMIT,
        cost_estimate=cost(flops, 6 * 2**20, 2**19),
    )(tok_a, tok_b, weights)


def hit_kernel(positives, labels, share):
    total = jnp.zeros(share.shape, F32)
    for p in range(POS):
        total = total + (positives[:, p : p + 1] == labels[...]).astype(F32)
    share[...] = total * (1.0 / POS)


def norm_kernel(lengths, tok, part, from_core, from_near, gain, rows, emb_hbm, emb, sem):
    embs = []
    for d in range(8):
        at = pl.ds(d * 32, 32)
        summed = tok[at].astype(F32) + (
            part[at] + from_core[at].astype(F32) + from_near[at].astype(F32)
        )
        centred = summed - jnp.mean(summed, axis=-1, keepdims=True)
        inv = lax.rsqrt(jnp.mean(centred * centred, axis=-1, keepdims=True) + NORM_EPS)
        normed = centred * inv
        count = jnp.full((32, 1), lengths[d], jnp.int32).astype(F32)
        share = jnp.where(iota((32, 1), 0).astype(F32) < count, 1.0, 0.0) / count
        embs.append(jnp.sum(normed * gain[...] * share, axis=0, keepdims=True))
        high = inv.astype(BF16).astype(F32)
        lane = iota((32, 128), 1)
        extra = jnp.where(lane == 0, high, jnp.where(lane == 1, inv - high, jnp.where(lane == 2, count, 0.0)))
        rows[at, :1024] = normed.astype(BF16)
        rows[at, 1024:] = extra.astype(BF16)
    docs = jnp.concatenate(embs, axis=0)
    emb[...] = jnp.concatenate([docs] * 16, axis=0).astype(BF16)
    copy = pltpu.make_async_copy(emb, emb_hbm, sem)
    copy.start()
    copy.wait()


def score_kernel(emb, tiles_hi, tiles_lo, live, packed_hbm, weighted, emb_buf, packed, sem):
    copy = pltpu.make_async_copy(emb, emb_buf, sem)
    copy.start()
    grow = (iota((128, 512), 0) == iota((128, 512), 1) // LPC).astype(BF16)
    mask = jnp.dot(live[...], grow, preferred_element_type=F32)
    copy.wait()
    docs = emb_buf[...]
    scores = lax.dot_general(docs, tiles_hi[...], LAST, preferred_element_type=F32)
    scores = scores + lax.dot_general(docs, tiles_lo[...], LAST, preferred_element_type=F32)
    value = mask * jnp.exp(scores)
    weighted[...] = value
    value_hi = value.astype(BF16)
    value_lo = (value - value_hi.astype(F32)).astype(BF16)
    part_emb = jnp.dot(value_hi, tiles_hi[...], preferred_element_type=F32)
    part_emb = part_emb + jnp.dot(value_hi, tiles_lo[...], preferred_element_type=F32)
    part_emb = part_emb + jnp.dot(value_lo, tiles_hi[...], preferred_element_type=F32)
    sums = jnp.sum(value, axis=1, keepdims=True) * 0.5
    high = sums.astype(BF16).astype(F32)
    row, lane = iota((128, 128), 0), iota((128, 128), 1)
    chosen = row // 8 == lane
    same = (row % 8 == lane % 8).astype(BF16)
    for k, part in enumerate((high, sums - high)):
        table = jnp.where(chosen, part, 0.0).astype(BF16)
        packed[:, 1024 + k * 128 : 1152 + k * 128] = jnp.dot(
            same, table, preferred_element_type=F32
        ).astype(BF16)
    packed[:, :1024] = part_emb.astype(BF16)
    copy = pltpu.make_async_copy(packed, packed_hbm, sem)
    copy.start()
    copy.wait()


def settle_kernel(meta, got_hbm, pos, emb, grad, loss, sums, got, sem):
    copy = pltpu.make_async_copy(got_hbm, got, sem)
    copy.start()
    copy.wait()
    total = got[0].astype(F32)
    for i in range(1, 16):
        total = total + got[i].astype(F32)
    every = (total[:, 1024:1152] + total[:, 1152:1280]) * 2.0
    sums[...] = every
    expsum = jnp.sum(jnp.where(iota((8, 128), 1) == meta[2], every, 0.0), axis=1, keepdims=True)
    pos_mean = pos[...]
    grad[...] = total[:, :1024] / expsum - pos_mean
    picked = jnp.sum(emb[...].astype(F32)[:8] * pos_mean, axis=1, keepdims=True)
    loss[...] = jnp.broadcast_to(jnp.log(expsum) - picked, (8, 128))


def backward_kernel(*refs):
    grads, gain, sums = refs[:4], refs[4], refs[5]
    rows, toks = refs[6:10], refs[10:14]
    hiddens, slopes, weights = refs[14:16], refs[16:18], refs[18]
    tile_in, out, tile_out = refs[19:22], refs[22], refs[23:25]
    row_buf, tok_buf, hid_buf, slope_buf, w_out, sum_grad, act_grad, result = refs[25:33]
    tile_bufs, tile_results, sems = refs[33:36], refs[36:38], refs[38]
    sent = []
    first = pltpu.make_async_copy(weights.at[:, 0:32], w_out, sems.at[0])
    tile_copies = [
        pltpu.make_async_copy(part, buf, sems.at[21 + k])
        for k, (part, buf) in enumerate(zip(tile_in, tile_bufs))
    ]
    for copy in tile_copies:
        copy.start()
    first.start()
    row_copies, tok_copies, hid_copies, slope_copies = [], [], [], []
    for k in range(4):
        at = pl.ds(k * 256, 256)
        row_copies.append(pltpu.make_async_copy(rows[k], row_buf.at[at], sems.at[1 + k]))
        row_copies[k].start()
    for k in range(2):
        at = pl.ds(k * 512, 512)
        slope_copies.append(pltpu.make_async_copy(slopes[k], slope_buf.at[at], sems.at[5 + k]))
        slope_copies[k].start()
    for k in range(2):
        at = pl.ds(k * 512, 512)
        hid_copies.append(pltpu.make_async_copy(hiddens[k], hid_buf.at[at], sems.at[7 + k]))
        hid_copies[k].start()
    for k in range(4):
        at = pl.ds(k * 256, 256)
        tok_copies.append(pltpu.make_async_copy(toks[k], tok_buf.at[at], sems.at[9 + k]))
        tok_copies[k].start()
    for copy in tile_copies:
        copy.wait()
    weighted, share_hit, emb = tile_bufs
    chosen = iota((128, 128), 0) // 8 == iota((128, 128), 1)
    column = jnp.where(chosen, jnp.concatenate([sums[...]] * 16, axis=0), 0.0)
    logit = weighted[...] / jnp.sum(column, axis=1, keepdims=True) - share_hit[...]
    logit_hi = logit.astype(BF16)
    logit_lo = (logit - logit_hi.astype(F32)).astype(BF16)
    for k, part in enumerate(tile_results):
        at = slice(k * 256, k * 256 + 256)
        value = lax.dot_general(logit_hi[:, at], emb[...], FIRST, preferred_element_type=F32)
        value = value + lax.dot_general(logit_lo[:, at], emb[...], FIRST, preferred_element_type=F32)
        part[...] = value.astype(part.dtype)
        sent.append(pltpu.make_async_copy(part, tile_out[k], sems.at[24 + k]))
        sent[-1].start()
    for k in range(4):
        row_copies[k].wait()
        scaled_grad = grads[k][...] * gain[...]
        grad_mean = jnp.mean(scaled_grad, axis=-1, keepdims=True)
        for d in range(8):
            at = pl.ds(k * 256 + d * 32, 32)
            norm = row_buf[at, :1024].astype(F32)
            extra = row_buf[at, 1024:].astype(F32)
            lane = iota((32, 128), 1)
            scale = jnp.sum(jnp.where(lane < 2, extra, 0.0), axis=1, keepdims=True)
            count = jnp.sum(jnp.where(lane == 2, extra, 0.0), axis=1, keepdims=True)
            share = jnp.where(iota((32, 1), 0).astype(F32) < count, 1.0, 0.0) / count
            grad = scaled_grad[d : d + 1]
            along = jnp.mean(grad * norm, axis=-1, keepdims=True)
            sum_grad[at] = (
                (grad - grad_mean[d : d + 1] - norm * along) * (share * scale)
            ).astype(BF16)
        if k == 0:
            first.wait()
        if k % 2 == 0:
            slope_copies[k // 2].wait()
        at = pl.ds(k * 256, 256)
        back = lax.dot_general(
            sum_grad[at], w_out[...].reshape(512, 1024), LAST, preferred_element_type=F32
        )
        act_grad[at] = (back * slope_buf[at]).astype(BF16)
    for copy in hid_copies:
        copy.wait()
    for i in range(2):
        part = lax.dot_general(
            hid_buf[:, i * 256 : i * 256 + 256], sum_grad[...], FIRST, preferred_element_type=F32
        )
        at = pl.ds(i * 8, 8)
        result[at, :32] = part.astype(BF16).reshape(8, 32, 1024)
        sent.append(pltpu.make_async_copy(result.at[at, 0:32], out.at[at, 0:32], sems.at[13 + i]))
        sent[-1].start()
    for copy in tok_copies:
        copy.wait()
    for i in range(4):
        part = lax.dot_general(
            tok_buf[:, i * 256 : i * 256 + 256], act_grad[...], FIRST, preferred_element_type=F32
        ).astype(BF16).reshape(4, 2, 32, 512)
        at = pl.ds(i * 4, 4)
        result[at, 32:, :512] = part[:, 0]
        result[at, 32:, 512:] = part[:, 1]
        sent.append(pltpu.make_async_copy(result.at[at, 32:64], out.at[at, 32:64], sems.at[17 + i]))
        sent[-1].start()
    for copy in sent:
        copy.wait()


def backward(grads, gain, sums, rows, toks, hiddens, slopes, weights, tile_in):
    return pl.pallas_call(
        backward_kernel,
        out_shape=(
            shape((16, 64, 1024), BF16),
            shape((256, 1024), F32),
            shape((256, 1024), BF16),
        ),
        in_specs=[WHOLE] * 6 + [ANYWHERE] * 16,
        out_specs=(ANYWHERE,) * 3,
        scratch_shapes=[
            pltpu.VMEM((1024, 1152), BF16),
            pltpu.VMEM((1024, 1024), BF16),
            pltpu.VMEM((1024, 512), BF16),
            pltpu.VMEM((1024, 512), F32),
            pltpu.VMEM((16, 32, 1024), BF16),
            pltpu.VMEM((1024, 1024), BF16),
            pltpu.VMEM((1024, 512), BF16),
            pltpu.VMEM((16, 64, 1024), BF16),
            pltpu.VMEM((128, 512), F32),
            pltpu.VMEM((128, 512), F32),
            pltpu.VMEM((128, 1024), BF16),
            pltpu.VMEM((256, 1024), F32),
            pltpu.VMEM((256, 1024), BF16),
            pltpu.SemaphoreType.DMA((26,)),
        ],
        compiler_params=MOST,
        cost_estimate=cost(3 * 2**30, 10 * 2**20),
    )(*grads, gain, sums, *rows, *toks, *hiddens, *slopes, weights, *tile_in)


def total_kernel(meta, got, out, keep, give):
    total = got[0].astype(F32)
    for i in range(1, 16):
        total = total + got[i].astype(F32)
    total = total.astype(BF16)
    core, step = meta[0], pl.program_id(0)

    @pl.when(step < 2)
    def _():
        out[...] = total

    @pl.when(step >= 2)
    def _():
        keep[...] = jnp.where(core == 0, total[:, :512], total[:, 512:])
        give[...] = jnp.where(core == 0, total[:, 512:], total[:, :512])


def place_kernel(meta, own, near, wrap, far, grad_in, grad_out):
    core, role = meta[0], meta[1]
    mine = own[:32].astype(F32) + wrap[:32].astype(F32)
    theirs = near[:32].astype(F32) + far[:32].astype(F32)
    grad_out[:32] = jnp.where(role == 0, mine, theirs)
    grad_out[32:] = jnp.where(role == 0, theirs, mine)
    row, lane = iota((1024, 512), 0), iota((1024, 512), 1)
    piece, at = row // 128, row % 128
    swapped, flipped = piece % 2, piece // 4
    part = (core + swapped - 2 * core * swapped) * 2 + (role + flipped - 2 * role * flipped)
    spread = (lane == at // 32 * 128 + part * 32 + at % 32).astype(BF16)
    blocks = [
        jnp.concatenate(
            [
                a[32:, k * 512 + i * 128 : k * 512 + i * 128 + 128]
                for a in (own, wrap, near, far)
                for k in range(2)
            ],
            axis=1,
        )
        for i in range(4)
    ]
    placed = jnp.dot(jnp.concatenate(blocks, axis=0), spread, preferred_element_type=F32)
    for i in range(4):
        grad_in[:, i * 512 : i * 512 + 512] = placed[i * 32 : i * 32 + 32]


def on_device(
    states,
    lengths,
    w_in,
    w_out,
    norm_gain,
    label_tiles,
    tile_mean,
    tile_var,
    shortlist,
    positives,
    owner_map,
):
    docs, length, width = states.shape
    core = lax.axis_index("c")
    high, low = lax.axis_index("h"), lax.axis_index("l")
    role = high + low - 2 * high * low
    chip = lax.axis_index("x") * 4 + lax.axis_index("z")
    meta = jnp.stack([core, role, chip]).astype(jnp.int32)
    gain = norm_gain.reshape(1, width)
    own_tok = states.reshape(docs * length, width)

    mine, theirs = pl.pallas_call(
        pick_kernel,
        out_shape=(shape((32, 512), BF16),) * 2,
        in_specs=[WHOLE],
        out_specs=(WHOLE,) * 2,
        compiler_params=LIMIT,
        cost_estimate=cost(2**25, 2**18),
    )(w_in)
    block = pl.pallas_call(
        lay_kernel,
        out_shape=shape((16, 64, width), BF16),
        in_specs=[WHOLE, WHOLE, ANYWHERE],
        out_specs=ANYWHERE,
        scratch_shapes=[pltpu.VMEM((32, width), BF16), pltpu.SemaphoreType.DMA((32,))],
        compiler_params=LIMIT,
        cost_estimate=cost(0, 2**21),
    )(mine, swap_core(theirs), w_out)
    block, own_tok, label_tiles, shortlist, positives, owner_map = lax.optimization_barrier(
        (block, own_tok, label_tiles, shortlist, positives, owner_map)
    )
    weights = gather_chips(block)

    core_tok, near_tok, diag_tok = swap_core(own_tok), swap_near(own_tok), swap_diag(own_tok)

    oth_tiles = swap_core(label_tiles)
    slots = jnp.concatenate(
        [(chip * 2 + core) * 64 + jnp.arange(64), (chip * 2 + 1 - core) * 64 + jnp.arange(64)]
    ).astype(jnp.int32)
    all_clusters = jnp.arange(owner_map.shape[0], dtype=jnp.int32)
    owner_match = owner_map[:, None] == slots[None, :]
    cluster_ids = jnp.sum(jnp.where(owner_match, all_clusters[:, None], 0), axis=0)
    pick = lambda a: lax.dynamic_index_in_dim(a.reshape(16, 2, 8, -1), core, 1, False).reshape(128, -1)
    short, posit = pick(shortlist), pick(positives)
    cluster_live = jnp.max(
        (short[:, :, None] == cluster_ids[None, None, :]).astype(F32), axis=1
    ).astype(BF16)
    tiles = jnp.concatenate([label_tiles, oth_tiles], axis=0)
    tiles_top = round_bf16(tiles)
    tiles_hi, tiles_lo = tiles_top.astype(BF16), (tiles - tiles_top).astype(BF16)
    label_ids = (jnp.repeat(cluster_ids, LPC) * LPC + jnp.arange(512) % LPC).astype(jnp.int32)
    share_hit = pl.pallas_call(
        hit_kernel,
        out_shape=shape((128, 512), F32),
        in_specs=[WHOLE, WHOLE],
        out_specs=WHOLE,
        compiler_params=LIMIT,
        cost_estimate=cost(2**18, 2**18),
    )(posit, label_ids[None, :])
    hit = share_hit.astype(BF16)
    pos_part = jnp.dot(hit, tiles_hi, preferred_element_type=F32) + jnp.dot(
        hit, tiles_lo, preferred_element_type=F32
    )
    pos_part = (pos_part * POS_SCALE).astype(jnp.float16)
    weights, cluster_live, share_hit, pos_part, tiles_hi, tiles_lo = lax.optimization_barrier(
        (weights, cluster_live, share_hit, pos_part, tiles_hi, tiles_lo)
    )

    near_a, near_b, near_hidden, near_slope = forward(diag_tok, near_tok, weights, 2**30)
    near_sum = (near_b + swap_core(near_a).astype(F32)).astype(BF16)
    near_sum, pos_part = lax.optimization_barrier((near_sum, pos_part))
    from_near = swap_near(near_sum)
    pos_got = gather_chips(pos_part.reshape(16, docs, width))
    own_a, own_b, own_hidden, own_slope = forward(core_tok, own_tok, weights, 2**36)
    from_near, pos_got = lax.optimization_barrier((from_near, pos_got))
    pos_mean = jnp.sum(pos_got.astype(F32), axis=0) * (1.0 / POS_SCALE)
    own_rows, emb = pl.pallas_call(
        norm_kernel,
        out_shape=(shape((256, 1152), BF16), shape((128, width), BF16)),
        in_specs=[SCALARS] + [WHOLE] * 5,
        out_specs=(WHOLE, ANYWHERE),
        scratch_shapes=[pltpu.VMEM((128, width), BF16), pltpu.SemaphoreType.DMA],
        compiler_params=LIMIT,
        cost_estimate=cost(2**22, 4 * 2**20),
    )(lengths, own_tok, own_b, swap_core(own_a), from_near, gain)

    plane_emb = gather_chips(emb.reshape(16, docs, width)).reshape(128, width)
    near_rows = swap_near(own_rows)
    packed, weighted = pl.pallas_call(
        score_kernel,
        out_shape=(shape((128, 1280), BF16), shape((128, 512), F32)),
        in_specs=[ANYWHERE] + [WHOLE] * 3,
        out_specs=(ANYWHERE, WHOLE),
        scratch_shapes=[
            pltpu.VMEM((128, width), BF16),
            pltpu.VMEM((128, 1280), BF16),
            pltpu.SemaphoreType.DMA,
        ],
        compiler_params=LIMIT,
        cost_estimate=cost(2**29, 3 * 2**20, 2**16),
    )(plane_emb, tiles_hi, tiles_lo, cluster_live)
    packed, near_rows = lax.optimization_barrier((packed, near_rows))
    core_rows, diag_rows = swap_core(own_rows), swap_core(near_rows)
    got = lax.all_to_all(packed.reshape(16, docs, 1280), CHIPS, 0, 0, tiled=True)
    emb_grad, loss, sums = pl.pallas_call(
        settle_kernel,
        out_shape=(shape((docs, width), F32), shape((docs, 128), F32), shape((docs, 128), F32)),
        in_specs=[SCALARS, ANYWHERE, WHOLE, WHOLE],
        out_specs=(WHOLE,) * 3,
        scratch_shapes=[
            pltpu.VMEM((16, docs, 1280), BF16),
            pltpu.SemaphoreType.DMA,
        ],
        compiler_params=LIMIT,
        cost_estimate=cost(2**20, 2**20),
    )(meta, got, pos_mean, emb)
    loss = loss[:, 0]

    grads = (swap_diag(emb_grad), swap_near(emb_grad), swap_core(emb_grad), emb_grad)
    send, tile_own, tile_other = backward(
        grads,
        gain,
        sums,
        (diag_rows, near_rows, core_rows, own_rows),
        (diag_tok, near_tok, core_tok, own_tok),
        (near_hidden, own_hidden),
        (near_slope, own_slope),
        weights,
        (weighted, share_hit, plane_emb),
    )
    got = lax.all_to_all(send, CHIPS, 0, 0, tiled=True)
    part, keep, give = pl.pallas_call(
        total_kernel,
        out_shape=(shape((32, width), BF16), shape((32, 512), BF16), shape((32, 512), BF16)),
        grid=(4,),
        in_specs=[SCALARS, pl.BlockSpec((16, 16, width), lambda i: (0, i, 0))],
        out_specs=(
            pl.BlockSpec((16, width), lambda i: (jnp.minimum(i, 1), 0)),
            pl.BlockSpec((16, 512), lambda i: (jnp.maximum(i - 2, 0), 0)),
            pl.BlockSpec((16, 512), lambda i: (jnp.maximum(i - 2, 0), 0)),
        ),
        compiler_params=LIMIT,
        cost_estimate=cost(2**20, 2**21),
    )(meta, got)
    both = jnp.concatenate([part, jnp.concatenate([keep, swap_core(give)], axis=1)], axis=0)
    grad_in, grad_out = pl.pallas_call(
        place_kernel,
        out_shape=(shape((32, 2048), F32), shape((64, width), F32)),
        in_specs=[SCALARS] + [WHOLE] * 4,
        out_specs=(WHOLE, WHOLE),
        compiler_params=LIMIT,
        cost_estimate=cost(2**26, 2**20),
    )(meta, both, swap_near(both), swap_wrap(both), swap_far(both))

    tile_chip = (tile_own + swap_core(tile_other).astype(F32)).astype(BF16)

    def add(a, swap):
        return a.astype(F32) + swap(a).astype(F32)

    tile_grad = jnp.concatenate(
        [
            add(add(tile_chip[:128], swap_near).astype(BF16), swap_wrap),
            add(add(tile_chip[128:], swap_wrap).astype(BF16), swap_near),
        ],
        axis=0,
    )
    new_mean = 0.9 * tile_mean + 0.1 * tile_grad
    new_var = 0.999 * tile_var + 0.001 * tile_grad * tile_grad
    new_tiles = label_tiles - 0.001 * (new_mean * CORR_ONE) / (jnp.sqrt(new_var * CORR_TWO) + 1e-08)
    return (loss, new_tiles, new_mean, new_var, grad_in, grad_out)


def solution(mesh):
    grid = Mesh(mesh.devices.reshape(2, 2, 4, 4, 2), ("h", "l", "x", "z", "c"))
    every, plane, group = ("h", "l", "x", "z", "c"), ("x", "z", "c"), ("h", "l")
    return jax.shard_map(
        on_device,
        mesh=grid,
        in_specs=(
            P(every, None, None),
            P(every),
            P(plane, None),
            P(plane, None),
            P(),
            P(plane, None),
            P(plane, None),
            P(plane, None),
            P(group, None),
            P(group, None),
            P(),
        ),
        out_specs=(
            P(every),
            P(plane, None),
            P(plane, None),
            P(plane, None),
            P(plane, None),
            P(plane, None),
        ),
        check_vma=False,
    )
```

```python
import jax
import jax.numpy as jnp
from jax import lax
from jax.experimental import pallas as pl
from jax.experimental.pallas import tpu as pltpu
from jax.sharding import Mesh, PartitionSpec as P

LPC = 4
POS = 4
POS_SCALE = 32768.0

NORM_EPS = 1e-05
INV_ROOT_TWO = 0.7071067811865476
INV_ROOT_TWO_PI = 0.3989422804014327
CORR_ONE = 1.000026562104397
CORR_TWO = 10.50333528

F32 = jnp.float32
BF16 = jnp.bfloat16
CHIPS = ("x", "z")
FIRST = (((0,), (0,)), ((), ()))
LAST = (((1,), (1,)), ((), ()))


def swap_core(a):
    return lax.ppermute(a, "c", [(0, 1), (1, 0)])


def swap_near(a):
    return lax.ppermute(a, "l", [(0, 1), (1, 0)])


def swap_diag(a):
    return lax.ppermute(a, ("l", "c"), [(0, 3), (3, 0), (1, 2), (2, 1)])


def swap_far(a):
    return lax.ppermute(a, "h", [(0, 1), (1, 0)])


def swap_wrap(a):
    return lax.ppermute(a, ("h", "l"), [(0, 3), (3, 0), (1, 2), (2, 1)])


def round_bf16(a):
    return lax.reduce_precision(a, 8, 7)


def gather_chips(a):
    return lax.all_to_all(a, CHIPS, 0, 0, tiled=True)


WHOLE = pl.BlockSpec(memory_space=pltpu.VMEM)
SCALARS = pl.BlockSpec(memory_space=pltpu.SMEM)
ANYWHERE = pl.BlockSpec(memory_space=pl.ANY)
LIMIT = pltpu.CompilerParams(vmem_limit_bytes=20 * 1024 * 1024)
MOST = pltpu.CompilerParams(vmem_limit_bytes=60 * 1024 * 1024)


def shape(dims, dtype):
    return jax.ShapeDtypeStruct(dims, dtype)


def cost(flops, data, special=0):
    return pl.CostEstimate(flops=flops, bytes_accessed=data, transcendentals=special)


def iota(dims, axis):
    return lax.broadcasted_iota(jnp.int32, dims, axis)


def place_of():
    core, high, low = (lax.axis_index(axis) for axis in ("c", "h", "l"))
    return core, high + low - 2 * high * low


def pick_kernel(w_in, mine, theirs):
    core, role = place_of()
    part = jnp.where(iota((512, 256), 1) < 128, core * 2 + role, 2 - core * 2 + role)
    at = iota((512, 256), 1) % 128
    spread = (iota((512, 256), 0) == at // 32 * 128 + part * 32 + at % 32).astype(BF16)
    for i in range(4):
        got = jnp.dot(w_in[:, i * 512 : i * 512 + 512], spread, preferred_element_type=F32).astype(BF16)
        mine[:, i * 128 : i * 128 + 128] = got[:, :128]
        theirs[:, i * 128 : i * 128 + 128] = got[:, 128:]


def lay_kernel(mine, theirs, top, out, block, sems):
    core, role = place_of()
    copies = [pltpu.make_async_copy(top, out.at[i, 0:32], sems.at[i]) for i in range(16)]
    for copy in copies:
        copy.start()
    block[:, :512] = jnp.where(core == 0, mine[...], theirs[...])
    block[:, 512:] = jnp.where(core == 0, theirs[...], mine[...])
    for i in range(16):
        copies.append(pltpu.make_async_copy(block, out.at[i, 32:64], sems.at[16 + i]))
        copies[-1].start()
    for copy in copies:
        copy.wait()


def forward_kernel(tok_a, tok_b, weights, part_a, part_b, hidden, slope, w_in, w_out, sems):
    copies = [
        pltpu.make_async_copy(
            weights.at[:, 32:64, k * 512 : k * 512 + 512], w_in.at[:, k * 32 : k * 32 + 32], sems.at[k]
        )
        for k in range(2)
    ]
    copies.append(pltpu.make_async_copy(weights.at[:, 0:32], w_out, sems.at[2]))
    for copy in copies:
        copy.start()
    copies[0].wait()
    copies[1].wait()
    for k, (tok, part) in enumerate(((tok_a, part_a), (tok_b, part_b))):
        pre_act = jnp.dot(tok[...], w_in[...].reshape(1024, 512), preferred_element_type=F32)
        normal_cdf = 0.5 * (1.0 + lax.erf(pre_act * INV_ROOT_TWO))
        act = (pre_act * normal_cdf).astype(BF16)
        hidden[k * 256 : k * 256 + 256] = act
        slope[k * 256 : k * 256 + 256] = (
            normal_cdf + pre_act * jnp.exp(-0.5 * pre_act * pre_act) * INV_ROOT_TWO_PI
        )
        if k == 0:
            copies[2].wait()
        part[...] = jnp.dot(
            act, w_out[...].reshape(512, 1024), preferred_element_type=F32
        ).astype(part.dtype)


def forward(tok_a, tok_b, weights, flops):
    return pl.pallas_call(
        forward_kernel,
        out_shape=(
            shape((256, 1024), BF16),
            shape((256, 1024), F32),
            shape((512, 512), BF16),
            shape((512, 512), F32),
        ),
        in_specs=[WHOLE, WHOLE, ANYWHERE],
        out_specs=(WHOLE,) * 4,
        scratch_shapes=[
            pltpu.VMEM((16, 64, 512), BF16),
            pltpu.VMEM((16, 32, 1024), BF16),
            pltpu.SemaphoreType.DMA((3,)),
        ],
        compiler_params=LIMIT,
        cost_estimate=cost(flops, 6 * 2**20, 2**19),
    )(tok_a, tok_b, weights)


def hit_kernel(positives, labels, share):
    total = jnp.zeros(share.shape, F32)
    for p in range(POS):
        total = total + (positives[:, p : p + 1] == labels[...]).astype(F32)
    share[...] = total * (1.0 / POS)


def norm_kernel(lengths, tok, part, from_core, from_near, gain, rows, emb_hbm, emb, sem):
    embs = []
    for d in range(8):
        at = pl.ds(d * 32, 32)
        summed = tok[at].astype(F32) + (
            part[at] + from_core[at].astype(F32) + from_near[at].astype(F32)
        )
        centred = summed - jnp.mean(summed, axis=-1, keepdims=True)
        inv = lax.rsqrt(jnp.mean(centred * centred, axis=-1, keepdims=True) + NORM_EPS)
        normed = centred * inv
        count = jnp.full((32, 1), lengths[d], jnp.int32).astype(F32)
        share = jnp.where(iota((32, 1), 0).astype(F32) < count, 1.0, 0.0) / count
        embs.append(jnp.sum(normed * gain[...] * share, axis=0, keepdims=True))
        high = inv.astype(BF16).astype(F32)
        lane = iota((32, 128), 1)
        extra = jnp.where(lane == 0, high, jnp.where(lane == 1, inv - high, jnp.where(lane == 2, count, 0.0)))
        rows[at, :1024] = normed.astype(BF16)
        rows[at, 1024:] = extra.astype(BF16)
    docs = jnp.concatenate(embs, axis=0)
    emb[...] = jnp.concatenate([docs] * 16, axis=0).astype(BF16)
    copy = pltpu.make_async_copy(emb, emb_hbm, sem)
    copy.start()
    copy.wait()


def score_kernel(emb, tiles_hi, tiles_lo, live, packed_hbm, weighted, emb_buf, packed, sem):
    copy = pltpu.make_async_copy(emb, emb_buf, sem)
    copy.start()
    grow = (iota((128, 512), 0) == iota((128, 512), 1) // LPC).astype(BF16)
    mask = jnp.dot(live[...], grow, preferred_element_type=F32)
    copy.wait()
    docs = emb_buf[...]
    scores = lax.dot_general(docs, tiles_hi[...], LAST, preferred_element_type=F32)
    scores = scores + lax.dot_general(docs, tiles_lo[...], LAST, preferred_element_type=F32)
    value = mask * jnp.exp(scores)
    weighted[...] = value
    value_hi = value.astype(BF16)
    value_lo = (value - value_hi.astype(F32)).astype(BF16)
    part_emb = jnp.dot(value_hi, tiles_hi[...], preferred_element_type=F32)
    part_emb = part_emb + jnp.dot(value_hi, tiles_lo[...], preferred_element_type=F32)
    part_emb = part_emb + jnp.dot(value_lo, tiles_hi[...], preferred_element_type=F32)
    sums = jnp.sum(value, axis=1, keepdims=True) * 0.5
    high = sums.astype(BF16).astype(F32)
    row, lane = iota((128, 128), 0), iota((128, 128), 1)
    chosen = row // 8 == lane
    same = (row % 8 == lane % 8).astype(BF16)
    for k, part in enumerate((high, sums - high)):
        table = jnp.where(chosen, part, 0.0).astype(BF16)
        packed[:, 1024 + k * 128 : 1152 + k * 128] = jnp.dot(
            same, table, preferred_element_type=F32
        ).astype(BF16)
    packed[:, :1024] = part_emb.astype(BF16)
    copy = pltpu.make_async_copy(packed, packed_hbm, sem)
    copy.start()
    copy.wait()


def settle_kernel(meta, got_hbm, pos, emb, grad, loss, sums, got, sem):
    copy = pltpu.make_async_copy(got_hbm, got, sem)
    copy.start()
    copy.wait()
    total = got[0].astype(F32)
    for i in range(1, 16):
        total = total + got[i].astype(F32)
    every = (total[:, 1024:1152] + total[:, 1152:1280]) * 2.0
    sums[...] = every
    expsum = jnp.sum(jnp.where(iota((8, 128), 1) == meta[2], every, 0.0), axis=1, keepdims=True)
    pos_mean = pos[...]
    grad[...] = total[:, :1024] / expsum - pos_mean
    picked = jnp.sum(emb[...].astype(F32)[:8] * pos_mean, axis=1, keepdims=True)
    loss[...] = jnp.broadcast_to(jnp.log(expsum) - picked, (8, 128))


def backward_kernel(*refs):
    grads, gain, sums = refs[:4], refs[4], refs[5]
    rows, toks = refs[6:10], refs[10:14]
    hiddens, slopes, weights = refs[14:16], refs[16:18], refs[18]
    tile_in, out, tile_out = refs[19:22], refs[22], refs[23:25]
    row_buf, tok_buf, hid_buf, slope_buf, w_out, sum_grad, act_grad, result = refs[25:33]
    tile_bufs, tile_results, sems = refs[33:36], refs[36:38], refs[38]
    sent = []
    first = pltpu.make_async_copy(weights.at[:, 0:32], w_out, sems.at[0])
    tile_copies = [
        pltpu.make_async_copy(part, buf, sems.at[21 + k])
        for k, (part, buf) in enumerate(zip(tile_in, tile_bufs))
    ]
    for copy in tile_copies:
        copy.start()
    row_copies, tok_copies, hid_copies, slope_copies = [], [], [], []
    for k in range(4):
        at = pl.ds(k * 256, 256)
        row_copies.append(pltpu.make_async_copy(rows[k], row_buf.at[at], sems.at[1 + k]))
        row_copies[k].start()
        if k == 0:
            first.start()
    for k in range(2):
        at = pl.ds(k * 512, 512)
        slope_copies.append(pltpu.make_async_copy(slopes[k], slope_buf.at[at], sems.at[5 + k]))
        slope_copies[k].start()
    for k in range(2):
        at = pl.ds(k * 512, 512)
        hid_copies.append(pltpu.make_async_copy(hiddens[k], hid_buf.at[at], sems.at[7 + k]))
        hid_copies[k].start()
    for k in range(4):
        at = pl.ds(k * 256, 256)
        tok_copies.append(pltpu.make_async_copy(toks[k], tok_buf.at[at], sems.at[9 + k]))
        tok_copies[k].start()
    for copy in tile_copies:
        copy.wait()
    weighted, share_hit, emb = tile_bufs
    chosen = iota((128, 128), 0) // 8 == iota((128, 128), 1)
    column = jnp.where(chosen, jnp.concatenate([sums[...]] * 16, axis=0), 0.0)
    logit = weighted[...] / jnp.sum(column, axis=1, keepdims=True) - share_hit[...]
    logit_hi = logit.astype(BF16)
    logit_lo = (logit - logit_hi.astype(F32)).astype(BF16)
    for k, part in enumerate(tile_results):
        at = slice(k * 256, k * 256 + 256)
        value = lax.dot_general(logit_hi[:, at], emb[...], FIRST, preferred_element_type=F32)
        value = value + lax.dot_general(logit_lo[:, at], emb[...], FIRST, preferred_element_type=F32)
        part[...] = value.astype(part.dtype)
        sent.append(pltpu.make_async_copy(part, tile_out[k], sems.at[24 + k]))
        sent[-1].start()
    for k in range(4):
        row_copies[k].wait()
        scaled_grad = grads[k][...] * gain[...]
        grad_mean = jnp.mean(scaled_grad, axis=-1, keepdims=True)
        for d in range(8):
            at = pl.ds(k * 256 + d * 32, 32)
            norm = row_buf[at, :1024].astype(F32)
            extra = row_buf[at, 1024:].astype(F32)
            lane = iota((32, 128), 1)
            scale = jnp.sum(jnp.where(lane < 2, extra, 0.0), axis=1, keepdims=True)
            count = jnp.sum(jnp.where(lane == 2, extra, 0.0), axis=1, keepdims=True)
            share = jnp.where(iota((32, 1), 0).astype(F32) < count, 1.0, 0.0) / count
            grad = scaled_grad[d : d + 1]
            along = jnp.mean(grad * norm, axis=-1, keepdims=True)
            sum_grad[at] = (
                (grad - grad_mean[d : d + 1] - norm * along) * (share * scale)
            ).astype(BF16)
        if k == 0:
            first.wait()
        if k % 2 == 0:
            slope_copies[k // 2].wait()
        at = pl.ds(k * 256, 256)
        back = lax.dot_general(
            sum_grad[at], w_out[...].reshape(512, 1024), LAST, preferred_element_type=F32
        )
        act_grad[at] = (back * slope_buf[at]).astype(BF16)
    for copy in hid_copies:
        copy.wait()
    for i in range(2):
        part = lax.dot_general(
            hid_buf[:, i * 256 : i * 256 + 256], sum_grad[...], FIRST, preferred_element_type=F32
        )
        at = pl.ds(i * 8, 8)
        result[at, :32] = part.astype(BF16).reshape(8, 32, 1024)
        sent.append(pltpu.make_async_copy(result.at[at, 0:32], out.at[at, 0:32], sems.at[13 + i]))
        sent[-1].start()
    for copy in tok_copies:
        copy.wait()
    for i in range(4):
        part = lax.dot_general(
            tok_buf[:, i * 256 : i * 256 + 256], act_grad[...], FIRST, preferred_element_type=F32
        ).astype(BF16).reshape(4, 2, 32, 512)
        at = pl.ds(i * 4, 4)
        result[at, 32:, :512] = part[:, 0]
        result[at, 32:, 512:] = part[:, 1]
        sent.append(pltpu.make_async_copy(result.at[at, 32:64], out.at[at, 32:64], sems.at[17 + i]))
        sent[-1].start()
    for copy in sent:
        copy.wait()


def backward(grads, gain, sums, rows, toks, hiddens, slopes, weights, tile_in):
    return pl.pallas_call(
        backward_kernel,
        out_shape=(
            shape((16, 64, 1024), BF16),
            shape((256, 1024), F32),
            shape((256, 1024), BF16),
        ),
        in_specs=[WHOLE] * 6 + [ANYWHERE] * 16,
        out_specs=(ANYWHERE,) * 3,
        scratch_shapes=[
            pltpu.VMEM((1024, 1152), BF16),
            pltpu.VMEM((1024, 1024), BF16),
            pltpu.VMEM((1024, 512), BF16),
            pltpu.VMEM((1024, 512), F32),
            pltpu.VMEM((16, 32, 1024), BF16),
            pltpu.VMEM((1024, 1024), BF16),
            pltpu.VMEM((1024, 512), BF16),
            pltpu.VMEM((16, 64, 1024), BF16),
            pltpu.VMEM((128, 512), F32),
            pltpu.VMEM((128, 512), F32),
            pltpu.VMEM((128, 1024), BF16),
            pltpu.VMEM((256, 1024), F32),
            pltpu.VMEM((256, 1024), BF16),
            pltpu.SemaphoreType.DMA((26,)),
        ],
        compiler_params=MOST,
        cost_estimate=cost(3 * 2**30, 10 * 2**20),
    )(*grads, gain, sums, *rows, *toks, *hiddens, *slopes, weights, *tile_in)


def total_kernel(meta, got, out, keep, give):
    total = got[0].astype(F32)
    for i in range(1, 16):
        total = total + got[i].astype(F32)
    total = total.astype(BF16)
    core, step = meta[0], pl.program_id(0)

    @pl.when(step < 2)
    def _():
        out[...] = total

    @pl.when(step >= 2)
    def _():
        keep[...] = jnp.where(core == 0, total[:, :512], total[:, 512:])
        give[...] = jnp.where(core == 0, total[:, 512:], total[:, :512])


def place_kernel(meta, own, near, wrap, far, grad_in, grad_out):
    core, role = meta[0], meta[1]
    mine = own[:32].astype(F32) + wrap[:32].astype(F32)
    theirs = near[:32].astype(F32) + far[:32].astype(F32)
    grad_out[:32] = jnp.where(role == 0, mine, theirs)
    grad_out[32:] = jnp.where(role == 0, theirs, mine)
    row, lane = iota((1024, 512), 0), iota((1024, 512), 1)
    piece, at = row // 128, row % 128
    swapped, flipped = piece % 2, piece // 4
    part = (core + swapped - 2 * core * swapped) * 2 + (role + flipped - 2 * role * flipped)
    spread = (lane == at // 32 * 128 + part * 32 + at % 32).astype(BF16)
    blocks = [
        jnp.concatenate(
            [
                a[32:, k * 512 + i * 128 : k * 512 + i * 128 + 128]
                for a in (own, wrap, near, far)
                for k in range(2)
            ],
            axis=1,
        )
        for i in range(4)
    ]
    placed = jnp.dot(jnp.concatenate(blocks, axis=0), spread, preferred_element_type=F32)
    for i in range(4):
        grad_in[:, i * 512 : i * 512 + 512] = placed[i * 32 : i * 32 + 32]


def on_device(
    states,
    lengths,
    w_in,
    w_out,
    norm_gain,
    label_tiles,
    tile_mean,
    tile_var,
    shortlist,
    positives,
    owner_map,
):
    docs, length, width = states.shape
    core = lax.axis_index("c")
    high, low = lax.axis_index("h"), lax.axis_index("l")
    role = high + low - 2 * high * low
    chip = lax.axis_index("x") * 4 + lax.axis_index("z")
    meta = jnp.stack([core, role, chip]).astype(jnp.int32)
    gain = norm_gain.reshape(1, width)
    own_tok = states.reshape(docs * length, width)

    mine, theirs = pl.pallas_call(
        pick_kernel,
        out_shape=(shape((32, 512), BF16),) * 2,
        in_specs=[WHOLE],
        out_specs=(WHOLE,) * 2,
        compiler_params=LIMIT,
        cost_estimate=cost(2**25, 2**18),
    )(w_in)
    block = pl.pallas_call(
        lay_kernel,
        out_shape=shape((16, 64, width), BF16),
        in_specs=[WHOLE, WHOLE, WHOLE],
        out_specs=ANYWHERE,
        scratch_shapes=[pltpu.VMEM((32, width), BF16), pltpu.SemaphoreType.DMA((32,))],
        compiler_params=LIMIT,
        cost_estimate=cost(0, 2**21),
    )(mine, swap_core(theirs), lax.dynamic_slice_in_dim(w_out, role * 32, 32, 0))
    block, own_tok, label_tiles, shortlist, positives, owner_map = lax.optimization_barrier(
        (block, own_tok, label_tiles, shortlist, positives, owner_map)
    )
    weights = gather_chips(block)

    core_tok, near_tok, diag_tok = swap_core(own_tok), swap_near(own_tok), swap_diag(own_tok)

    oth_tiles = swap_core(label_tiles)
    slots = jnp.concatenate(
        [(chip * 2 + core) * 64 + jnp.arange(64), (chip * 2 + 1 - core) * 64 + jnp.arange(64)]
    ).astype(jnp.int32)
    all_clusters = jnp.arange(owner_map.shape[0], dtype=jnp.int32)
    owner_match = owner_map[:, None] == slots[None, :]
    cluster_ids = jnp.sum(jnp.where(owner_match, all_clusters[:, None], 0), axis=0)
    pick = lambda a: lax.dynamic_index_in_dim(a.reshape(16, 2, 8, -1), core, 1, False).reshape(128, -1)
    short, posit = pick(shortlist), pick(positives)
    cluster_live = jnp.max(
        (short[:, :, None] == cluster_ids[None, None, :]).astype(F32), axis=1
    ).astype(BF16)
    tiles = jnp.concatenate([label_tiles, oth_tiles], axis=0)
    tiles_top = round_bf16(tiles)
    tiles_hi, tiles_lo = tiles_top.astype(BF16), (tiles - tiles_top).astype(BF16)
    label_ids = (jnp.repeat(cluster_ids, LPC) * LPC + jnp.arange(512) % LPC).astype(jnp.int32)
    share_hit = pl.pallas_call(
        hit_kernel,
        out_shape=shape((128, 512), F32),
        in_specs=[WHOLE, WHOLE],
        out_specs=WHOLE,
        compiler_params=LIMIT,
        cost_estimate=cost(2**18, 2**18),
    )(posit, label_ids[None, :])
    hit = share_hit.astype(BF16)
    pos_part = jnp.dot(hit, tiles_hi, preferred_element_type=F32) + jnp.dot(
        hit, tiles_lo, preferred_element_type=F32
    )
    pos_part = (pos_part * POS_SCALE).astype(jnp.float16)
    weights, cluster_live, share_hit, pos_part, tiles_hi, tiles_lo = lax.optimization_barrier(
        (weights, cluster_live, share_hit, pos_part, tiles_hi, tiles_lo)
    )

    near_a, near_b, near_hidden, near_slope = forward(diag_tok, near_tok, weights, 2**30)
    near_sum = (near_b + swap_core(near_a).astype(F32)).astype(BF16)
    near_sum, pos_part = lax.optimization_barrier((near_sum, pos_part))
    from_near = swap_near(near_sum)
    pos_got = gather_chips(pos_part.reshape(16, docs, width))
    own_a, own_b, own_hidden, own_slope = forward(core_tok, own_tok, weights, 2**36)
    from_near, pos_got = lax.optimization_barrier((from_near, pos_got))
    pos_mean = jnp.sum(pos_got.astype(F32), axis=0) * (1.0 / POS_SCALE)
    own_rows, emb = pl.pallas_call(
        norm_kernel,
        out_shape=(shape((256, 1152), BF16), shape((128, width), BF16)),
        in_specs=[SCALARS] + [WHOLE] * 5,
        out_specs=(WHOLE, ANYWHERE),
        scratch_shapes=[pltpu.VMEM((128, width), BF16), pltpu.SemaphoreType.DMA],
        compiler_params=LIMIT,
        cost_estimate=cost(2**22, 4 * 2**20),
    )(lengths, own_tok, own_b, swap_core(own_a), from_near, gain)

    plane_emb = gather_chips(emb.reshape(16, docs, width)).reshape(128, width)
    near_rows = swap_near(own_rows)
    packed, weighted = pl.pallas_call(
        score_kernel,
        out_shape=(shape((128, 1280), BF16), shape((128, 512), F32)),
        in_specs=[ANYWHERE] + [WHOLE] * 3,
        out_specs=(ANYWHERE, WHOLE),
        scratch_shapes=[
            pltpu.VMEM((128, width), BF16),
            pltpu.VMEM((128, 1280), BF16),
            pltpu.SemaphoreType.DMA,
        ],
        compiler_params=LIMIT,
        cost_estimate=cost(2**29, 3 * 2**20, 2**16),
    )(plane_emb, tiles_hi, tiles_lo, cluster_live)
    packed, near_rows = lax.optimization_barrier((packed, near_rows))
    core_rows, diag_rows = swap_core(own_rows), swap_core(near_rows)
    got = lax.all_to_all(packed.reshape(16, docs, 1280), CHIPS, 0, 0, tiled=True)
    emb_grad, loss, sums = pl.pallas_call(
        settle_kernel,
        out_shape=(shape((docs, width), F32), shape((docs, 128), F32), shape((docs, 128), F32)),
        in_specs=[SCALARS, ANYWHERE, WHOLE, WHOLE],
        out_specs=(WHOLE,) * 3,
        scratch_shapes=[
            pltpu.VMEM((16, docs, 1280), BF16),
            pltpu.SemaphoreType.DMA,
        ],
        compiler_params=LIMIT,
        cost_estimate=cost(2**20, 2**20),
    )(meta, got, pos_mean, emb)
    loss = loss[:, 0]

    grads = (swap_diag(emb_grad), swap_near(emb_grad), swap_core(emb_grad), emb_grad)
    send, tile_own, tile_other = backward(
        grads,
        gain,
        sums,
        (diag_rows, near_rows, core_rows, own_rows),
        (diag_tok, near_tok, core_tok, own_tok),
        (near_hidden, own_hidden),
        (near_slope, own_slope),
        weights,
        (weighted, share_hit, plane_emb),
    )
    got = lax.all_to_all(send, CHIPS, 0, 0, tiled=True)
    part, keep, give = pl.pallas_call(
        total_kernel,
        out_shape=(shape((32, width), BF16), shape((32, 512), BF16), shape((32, 512), BF16)),
        grid=(4,),
        in_specs=[SCALARS, pl.BlockSpec((16, 16, width), lambda i: (0, i, 0))],
        out_specs=(
            pl.BlockSpec((16, width), lambda i: (jnp.minimum(i, 1), 0)),
            pl.BlockSpec((16, 512), lambda i: (jnp.maximum(i - 2, 0), 0)),
            pl.BlockSpec((16, 512), lambda i: (jnp.maximum(i - 2, 0), 0)),
        ),
        compiler_params=LIMIT,
        cost_estimate=cost(2**20, 2**21),
    )(meta, got)
    both = jnp.concatenate([part, jnp.concatenate([keep, swap_core(give)], axis=1)], axis=0)
    grad_in, grad_out = pl.pallas_call(
        place_kernel,
        out_shape=(shape((32, 2048), F32), shape((64, width), F32)),
        in_specs=[SCALARS] + [WHOLE] * 4,
        out_specs=(WHOLE, WHOLE),
        compiler_params=LIMIT,
        cost_estimate=cost(2**26, 2**20),
    )(meta, both, swap_near(both), swap_wrap(both), swap_far(both))

    tile_chip = (tile_own + swap_core(tile_other).astype(F32)).astype(BF16)

    def add(a, swap):
        return a.astype(F32) + swap(a).astype(F32)

    tile_grad = jnp.concatenate(
        [
            add(add(tile_chip[:128], swap_near).astype(BF16), swap_wrap),
            add(add(tile_chip[128:], swap_wrap).astype(BF16), swap_near),
        ],
        axis=0,
    )
    new_mean = 0.9 * tile_mean + 0.1 * tile_grad
    new_var = 0.999 * tile_var + 0.001 * tile_grad * tile_grad
    new_tiles = label_tiles - 0.001 * (new_mean * CORR_ONE) / (jnp.sqrt(new_var * CORR_TWO) + 1e-08)
    return (loss, new_tiles, new_mean, new_var, grad_in, grad_out)


def solution(mesh):
    grid = Mesh(mesh.devices.reshape(2, 2, 4, 4, 2), ("h", "l", "x", "z", "c"))
    every, plane, group = ("h", "l", "x", "z", "c"), ("x", "z", "c"), ("h", "l")
    return jax.shard_map(
        on_device,
        mesh=grid,
        in_specs=(
            P(every, None, None),
            P(every),
            P(plane, None),
            P(plane, None),
            P(),
            P(plane, None),
            P(plane, None),
            P(plane, None),
            P(group, None),
            P(group, None),
            P(),
        ),
        out_specs=(
            P(every),
            P(plane, None),
            P(plane, None),
            P(plane, None),
            P(plane, None),
            P(plane, None),
        ),
        check_vma=False,
    )
```

```python
import jax
import jax.numpy as jnp
from jax import lax
from jax.experimental import pallas as pl
from jax.experimental.pallas import tpu as pltpu
from jax.sharding import Mesh, PartitionSpec as P

LPC = 4
POS = 4
POS_SCALE = 32768.0

NORM_EPS = 1e-05
INV_ROOT_TWO = 0.7071067811865476
INV_ROOT_TWO_PI = 0.3989422804014327
CORR_ONE = 1.000026562104397
CORR_TWO = 10.50333528

F32 = jnp.float32
BF16 = jnp.bfloat16
CHIPS = ("x", "z")
FIRST = (((0,), (0,)), ((), ()))
LAST = (((1,), (1,)), ((), ()))


def swap_core(a):
    return lax.ppermute(a, "c", [(0, 1), (1, 0)])


def swap_near(a):
    return lax.ppermute(a, "l", [(0, 1), (1, 0)])


def swap_diag(a):
    return lax.ppermute(a, ("l", "c"), [(0, 3), (3, 0), (1, 2), (2, 1)])


def swap_far(a):
    return lax.ppermute(a, "h", [(0, 1), (1, 0)])


def swap_wrap(a):
    return lax.ppermute(a, ("h", "l"), [(0, 3), (3, 0), (1, 2), (2, 1)])


def round_bf16(a):
    return lax.reduce_precision(a, 8, 7)


def gather_chips(a):
    return lax.all_to_all(a, CHIPS, 0, 0, tiled=True)


WHOLE = pl.BlockSpec(memory_space=pltpu.VMEM)
SCALARS = pl.BlockSpec(memory_space=pltpu.SMEM)
ANYWHERE = pl.BlockSpec(memory_space=pl.ANY)
LIMIT = pltpu.CompilerParams(vmem_limit_bytes=20 * 1024 * 1024)
MOST = pltpu.CompilerParams(vmem_limit_bytes=56 * 1024 * 1024)


def shape(dims, dtype):
    return jax.ShapeDtypeStruct(dims, dtype)


def cost(flops, data, special=0):
    return pl.CostEstimate(flops=flops, bytes_accessed=data, transcendentals=special)


def iota(dims, axis):
    return lax.broadcasted_iota(jnp.int32, dims, axis)


def place_of():
    core, high, low = (lax.axis_index(axis) for axis in ("c", "h", "l"))
    return core, high + low - 2 * high * low


def pick_kernel(w_in, mine, theirs):
    core, role = place_of()
    part = jnp.where(iota((512, 256), 1) < 128, core * 2 + role, 2 - core * 2 + role)
    at = iota((512, 256), 1) % 128
    spread = (iota((512, 256), 0) == at // 32 * 128 + part * 32 + at % 32).astype(BF16)
    for i in range(4):
        got = jnp.dot(w_in[:, i * 512 : i * 512 + 512], spread, preferred_element_type=F32).astype(BF16)
        mine[:, i * 128 : i * 128 + 128] = got[:, :128]
        theirs[:, i * 128 : i * 128 + 128] = got[:, 128:]


def lay_kernel(mine, theirs, top, out, block, sems):
    core, role = place_of()
    copies = [pltpu.make_async_copy(top, out.at[i, 0:32], sems.at[i]) for i in range(16)]
    for copy in copies:
        copy.start()
    block[:, :512] = jnp.where(core == 0, mine[...], theirs[...])
    block[:, 512:] = jnp.where(core == 0, theirs[...], mine[...])
    for i in range(16):
        copies.append(pltpu.make_async_copy(block, out.at[i, 32:64], sems.at[16 + i]))
        copies[-1].start()
    for copy in copies:
        copy.wait()


def forward_kernel(tok_a, tok_b, weights, part_a, part_b, hidden, slope, w_in, w_out, sems):
    copies = [
        pltpu.make_async_copy(
            weights.at[:, 32:64, k * 512 : k * 512 + 512], w_in.at[:, k * 32 : k * 32 + 32], sems.at[k]
        )
        for k in range(2)
    ]
    copies.append(pltpu.make_async_copy(weights.at[:, 0:32], w_out, sems.at[2]))
    for copy in copies:
        copy.start()
    copies[0].wait()
    copies[1].wait()
    for k, (tok, part) in enumerate(((tok_a, part_a), (tok_b, part_b))):
        pre_act = jnp.dot(tok[...], w_in[...].reshape(1024, 512), preferred_element_type=F32)
        normal_cdf = 0.5 * (1.0 + lax.erf(pre_act * INV_ROOT_TWO))
        act = (pre_act * normal_cdf).astype(BF16)
        hidden[k * 256 : k * 256 + 256] = act
        slope[k * 256 : k * 256 + 256] = (
            normal_cdf + pre_act * jnp.exp(-0.5 * pre_act * pre_act) * INV_ROOT_TWO_PI
        )
        if k == 0:
            copies[2].wait()
        part[...] = jnp.dot(
            act, w_out[...].reshape(512, 1024), preferred_element_type=F32
        ).astype(part.dtype)


def forward(tok_a, tok_b, weights, flops):
    return pl.pallas_call(
        forward_kernel,
        out_shape=(
            shape((256, 1024), BF16),
            shape((256, 1024), F32),
            shape((512, 512), BF16),
            shape((512, 512), F32),
        ),
        in_specs=[WHOLE, WHOLE, ANYWHERE],
        out_specs=(WHOLE,) * 4,
        scratch_shapes=[
            pltpu.VMEM((16, 64, 512), BF16),
            pltpu.VMEM((16, 32, 1024), BF16),
            pltpu.SemaphoreType.DMA((3,)),
        ],
        compiler_params=LIMIT,
        cost_estimate=cost(flops, 6 * 2**20, 2**19),
    )(tok_a, tok_b, weights)


def hit_kernel(positives, labels, share):
    total = jnp.zeros(share.shape, F32)
    for p in range(POS):
        total = total + (positives[:, p : p + 1] == labels[...]).astype(F32)
    share[...] = total * (1.0 / POS)


def norm_kernel(lengths, tok, part, from_core, from_near, gain, rows, emb_hbm, emb, sem):
    embs = []
    for d in range(8):
        at = pl.ds(d * 32, 32)
        summed = tok[at].astype(F32) + (
            part[at] + from_core[at].astype(F32) + from_near[at].astype(F32)
        )
        centred = summed - jnp.mean(summed, axis=-1, keepdims=True)
        inv = lax.rsqrt(jnp.mean(centred * centred, axis=-1, keepdims=True) + NORM_EPS)
        normed = centred * inv
        count = jnp.full((32, 1), lengths[d], jnp.int32).astype(F32)
        share = jnp.where(iota((32, 1), 0).astype(F32) < count, 1.0, 0.0) / count
        embs.append(jnp.sum(normed * gain[...] * share, axis=0, keepdims=True))
        high = inv.astype(BF16).astype(F32)
        lane = iota((32, 128), 1)
        extra = jnp.where(lane == 0, high, jnp.where(lane == 1, inv - high, jnp.where(lane == 2, count, 0.0)))
        rows[at, :1024] = normed.astype(BF16)
        rows[at, 1024:] = extra.astype(BF16)
    docs = jnp.concatenate(embs, axis=0)
    emb[...] = jnp.concatenate([docs] * 16, axis=0).astype(BF16)
    copy = pltpu.make_async_copy(emb, emb_hbm, sem)
    copy.start()
    copy.wait()


def score_kernel(emb, tiles_hi, tiles_lo, live, packed_hbm, weighted, emb_buf, packed, sem):
    copy = pltpu.make_async_copy(emb, emb_buf, sem)
    copy.start()
    grow = (iota((128, 512), 0) == iota((128, 512), 1) // LPC).astype(BF16)
    mask = jnp.dot(live[...], grow, preferred_element_type=F32)
    copy.wait()
    docs = emb_buf[...]
    scores = lax.dot_general(docs, tiles_hi[...], LAST, preferred_element_type=F32)
    scores = scores + lax.dot_general(docs, tiles_lo[...], LAST, preferred_element_type=F32)
    value = mask * jnp.exp(scores)
    weighted[...] = value
    value_hi = value.astype(BF16)
    value_lo = (value - value_hi.astype(F32)).astype(BF16)
    part_emb = jnp.dot(value_hi, tiles_hi[...], preferred_element_type=F32)
    part_emb = part_emb + jnp.dot(value_hi, tiles_lo[...], preferred_element_type=F32)
    part_emb = part_emb + jnp.dot(value_lo, tiles_hi[...], preferred_element_type=F32)
    sums = jnp.sum(value, axis=1, keepdims=True) * 0.5
    high = sums.astype(BF16).astype(F32)
    row, lane = iota((128, 128), 0), iota((128, 128), 1)
    chosen = row // 8 == lane
    same = (row % 8 == lane % 8).astype(BF16)
    for k, part in enumerate((high, sums - high)):
        table = jnp.where(chosen, part, 0.0).astype(BF16)
        packed[:, 1024 + k * 128 : 1152 + k * 128] = jnp.dot(
            same, table, preferred_element_type=F32
        ).astype(BF16)
    packed[:, :1024] = part_emb.astype(BF16)
    copy = pltpu.make_async_copy(packed, packed_hbm, sem)
    copy.start()
    copy.wait()


def settle_kernel(meta, got_hbm, pos, emb, grad, loss, sums, got, sem):
    copy = pltpu.make_async_copy(got_hbm, got, sem)
    copy.start()
    copy.wait()
    total = got[0].astype(F32)
    for i in range(1, 16):
        total = total + got[i].astype(F32)
    every = (total[:, 1024:1152] + total[:, 1152:1280]) * 2.0
    sums[...] = every
    expsum = jnp.sum(jnp.where(iota((8, 128), 1) == meta[2], every, 0.0), axis=1, keepdims=True)
    pos_mean = pos[...]
    grad[...] = total[:, :1024] / expsum - pos_mean
    picked = jnp.sum(emb[...].astype(F32)[:8] * pos_mean, axis=1, keepdims=True)
    loss[...] = jnp.broadcast_to(jnp.log(expsum) - picked, (8, 128))


def backward_kernel(*refs):
    grads, gain, sums = refs[:4], refs[4], refs[5]
    rows, toks = refs[6:10], refs[10:14]
    hiddens, slopes, weights = refs[14:16], refs[16:18], refs[18]
    tile_in, out, tile_out = refs[19:22], refs[22], refs[23:25]
    row_buf, tok_buf, hid_buf, slope_buf, w_out, sum_grad, act_grad, result = refs[25:33]
    tile_bufs, tile_results, sems = refs[33:36], refs[36:38], refs[38]
    sent = []
    first = pltpu.make_async_copy(weights.at[:, 0:32], w_out, sems.at[0])
    tile_copies = [
        pltpu.make_async_copy(part, buf, sems.at[21 + k])
        for k, (part, buf) in enumerate(zip(tile_in, tile_bufs))
    ]
    for copy in tile_copies:
        copy.start()
    row_copies, tok_copies, hid_copies, slope_copies = [], [], [], []
    for k in range(4):
        at = pl.ds(k * 256, 256)
        row_copies.append(pltpu.make_async_copy(rows[k], row_buf.at[at], sems.at[1 + k]))
        row_copies[k].start()
        if k == 0:
            first.start()
    for k in range(2):
        at = pl.ds(k * 512, 512)
        slope_copies.append(pltpu.make_async_copy(slopes[k], slope_buf.at[at], sems.at[5 + k]))
        slope_copies[k].start()
    for k in range(2):
        at = pl.ds(k * 512, 512)
        hid_copies.append(pltpu.make_async_copy(hiddens[k], hid_buf.at[at], sems.at[7 + k]))
        hid_copies[k].start()
    for k in range(4):
        at = pl.ds(k * 256, 256)
        tok_copies.append(pltpu.make_async_copy(toks[k], tok_buf.at[at], sems.at[9 + k]))
        tok_copies[k].start()
    for copy in tile_copies:
        copy.wait()
    weighted, share_hit, emb = tile_bufs
    chosen = iota((128, 128), 0) // 8 == iota((128, 128), 1)
    column = jnp.where(chosen, jnp.concatenate([sums[...]] * 16, axis=0), 0.0)
    logit = weighted[...] / jnp.sum(column, axis=1, keepdims=True) - share_hit[...]
    logit_hi = logit.astype(BF16)
    logit_lo = (logit - logit_hi.astype(F32)).astype(BF16)
    for k, part in enumerate(tile_results):
        at = slice(k * 256, k * 256 + 256)
        value = lax.dot_general(logit_hi[:, at], emb[...], FIRST, preferred_element_type=F32)
        value = value + lax.dot_general(logit_lo[:, at], emb[...], FIRST, preferred_element_type=F32)
        part[...] = value.astype(part.dtype)
        sent.append(pltpu.make_async_copy(part, tile_out[k], sems.at[24 + k]))
        sent[-1].start()
    for k in range(4):
        row_copies[k].wait()
        scaled_grad = grads[k][...] * gain[...]
        grad_mean = jnp.mean(scaled_grad, axis=-1, keepdims=True)
        for d in range(8):
            at = pl.ds(k * 256 + d * 32, 32)
            norm = row_buf[at, :1024].astype(F32)
            extra = row_buf[at, 1024:].astype(F32)
            lane = iota((32, 128), 1)
            scale = jnp.sum(jnp.where(lane < 2, extra, 0.0), axis=1, keepdims=True)
            count = jnp.sum(jnp.where(lane == 2, extra, 0.0), axis=1, keepdims=True)
            share = jnp.where(iota((32, 1), 0).astype(F32) < count, 1.0, 0.0) / count
            grad = scaled_grad[d : d + 1]
            along = jnp.mean(grad * norm, axis=-1, keepdims=True)
            sum_grad[at] = (
                (grad - grad_mean[d : d + 1] - norm * along) * (share * scale)
            ).astype(BF16)
        if k == 0:
            first.wait()
        if k % 2 == 0:
            slope_copies[k // 2].wait()
        at = pl.ds(k * 256, 256)
        back = lax.dot_general(
            sum_grad[at], w_out[...].reshape(512, 1024), LAST, preferred_element_type=F32
        )
        act_grad[at] = (back * slope_buf[at]).astype(BF16)
    for copy in hid_copies:
        copy.wait()
    for i in range(2):
        part = lax.dot_general(
            hid_buf[:, i * 256 : i * 256 + 256], sum_grad[...], FIRST, preferred_element_type=F32
        )
        at = pl.ds(i * 8, 8)
        result[at, :32] = part.astype(BF16).reshape(8, 32, 1024)
        sent.append(pltpu.make_async_copy(result.at[at, 0:32], out.at[at, 0:32], sems.at[13 + i]))
        sent[-1].start()
    for copy in tok_copies:
        copy.wait()
    for i in range(4):
        part = lax.dot_general(
            tok_buf[:, i * 256 : i * 256 + 256], act_grad[...], FIRST, preferred_element_type=F32
        ).astype(BF16).reshape(4, 2, 32, 512)
        at = pl.ds(i * 4, 4)
        result[at, 32:, :512] = part[:, 0]
        result[at, 32:, 512:] = part[:, 1]
        sent.append(pltpu.make_async_copy(result.at[at, 32:64], out.at[at, 32:64], sems.at[17 + i]))
        sent[-1].start()
    for copy in sent:
        copy.wait()


def backward(grads, gain, sums, rows, toks, hiddens, slopes, weights, tile_in):
    return pl.pallas_call(
        backward_kernel,
        out_shape=(
            shape((16, 64, 1024), BF16),
            shape((256, 1024), F32),
            shape((256, 1024), BF16),
        ),
        in_specs=[WHOLE] * 6 + [ANYWHERE] * 16,
        out_specs=(ANYWHERE,) * 3,
        scratch_shapes=[
            pltpu.VMEM((1024, 1152), BF16),
            pltpu.VMEM((1024, 1024), BF16),
            pltpu.VMEM((1024, 512), BF16),
            pltpu.VMEM((1024, 512), F32),
            pltpu.VMEM((16, 32, 1024), BF16),
            pltpu.VMEM((1024, 1024), BF16),
            pltpu.VMEM((1024, 512), BF16),
            pltpu.VMEM((16, 64, 1024), BF16),
            pltpu.VMEM((128, 512), F32),
            pltpu.VMEM((128, 512), F32),
            pltpu.VMEM((128, 1024), BF16),
            pltpu.VMEM((256, 1024), F32),
            pltpu.VMEM((256, 1024), BF16),
            pltpu.SemaphoreType.DMA((26,)),
        ],
        compiler_params=MOST,
        cost_estimate=cost(3 * 2**30, 10 * 2**20),
    )(*grads, gain, sums, *rows, *toks, *hiddens, *slopes, weights, *tile_in)


def total_kernel(meta, got, out, keep, give):
    total = got[0].astype(F32)
    for i in range(1, 16):
        total = total + got[i].astype(F32)
    total = total.astype(BF16)
    core, step = meta[0], pl.program_id(0)

    @pl.when(step < 2)
    def _():
        out[...] = total

    @pl.when(step >= 2)
    def _():
        keep[...] = jnp.where(core == 0, total[:, :512], total[:, 512:])
        give[...] = jnp.where(core == 0, total[:, 512:], total[:, :512])


def place_kernel(meta, own, near, wrap, far, grad_in, grad_out):
    core, role = meta[0], meta[1]
    mine = own[:32].astype(F32) + wrap[:32].astype(F32)
    theirs = near[:32].astype(F32) + far[:32].astype(F32)
    grad_out[:32] = jnp.where(role == 0, mine, theirs)
    grad_out[32:] = jnp.where(role == 0, theirs, mine)
    row, lane = iota((1024, 512), 0), iota((1024, 512), 1)
    piece, at = row // 128, row % 128
    swapped, flipped = piece % 2, piece // 4
    part = (core + swapped - 2 * core * swapped) * 2 + (role + flipped - 2 * role * flipped)
    spread = (lane == at // 32 * 128 + part * 32 + at % 32).astype(BF16)
    blocks = [
        jnp.concatenate(
            [
                a[32:, k * 512 + i * 128 : k * 512 + i * 128 + 128]
                for a in (own, wrap, near, far)
                for k in range(2)
            ],
            axis=1,
        )
        for i in range(4)
    ]
    placed = jnp.dot(jnp.concatenate(blocks, axis=0), spread, preferred_element_type=F32)
    for i in range(4):
        grad_in[:, i * 512 : i * 512 + 512] = placed[i * 32 : i * 32 + 32]


def on_device(
    states,
    lengths,
    w_in,
    w_out,
    norm_gain,
    label_tiles,
    tile_mean,
    tile_var,
    shortlist,
    positives,
    owner_map,
):
    docs, length, width = states.shape
    core = lax.axis_index("c")
    high, low = lax.axis_index("h"), lax.axis_index("l")
    role = high + low - 2 * high * low
    chip = lax.axis_index("x") * 4 + lax.axis_index("z")
    meta = jnp.stack([core, role, chip]).astype(jnp.int32)
    gain = norm_gain.reshape(1, width)
    own_tok = states.reshape(docs * length, width)

    mine, theirs = pl.pallas_call(
        pick_kernel,
        out_shape=(shape((32, 512), BF16),) * 2,
        in_specs=[WHOLE],
        out_specs=(WHOLE,) * 2,
        compiler_params=LIMIT,
        cost_estimate=cost(2**25, 2**18),
    )(w_in)
    block = pl.pallas_call(
        lay_kernel,
        out_shape=shape((16, 64, width), BF16),
        in_specs=[WHOLE, WHOLE, WHOLE],
        out_specs=ANYWHERE,
        scratch_shapes=[pltpu.VMEM((32, width), BF16), pltpu.SemaphoreType.DMA((32,))],
        compiler_params=LIMIT,
        cost_estimate=cost(0, 2**21),
    )(mine, swap_core(theirs), lax.dynamic_slice_in_dim(w_out, role * 32, 32, 0))
    block, own_tok, label_tiles, shortlist, positives, owner_map = lax.optimization_barrier(
        (block, own_tok, label_tiles, shortlist, positives, owner_map)
    )
    weights = gather_chips(block)

    core_tok, near_tok, diag_tok = swap_core(own_tok), swap_near(own_tok), swap_diag(own_tok)

    oth_tiles = swap_core(label_tiles)
    slots = jnp.concatenate(
        [(chip * 2 + core) * 64 + jnp.arange(64), (chip * 2 + 1 - core) * 64 + jnp.arange(64)]
    ).astype(jnp.int32)
    all_clusters = jnp.arange(owner_map.shape[0], dtype=jnp.int32)
    owner_match = owner_map[:, None] == slots[None, :]
    cluster_ids = jnp.sum(jnp.where(owner_match, all_clusters[:, None], 0), axis=0)
    pick = lambda a: lax.dynamic_index_in_dim(a.reshape(16, 2, 8, -1), core, 1, False).reshape(128, -1)
    short, posit = pick(shortlist), pick(positives)
    cluster_live = jnp.max(
        (short[:, :, None] == cluster_ids[None, None, :]).astype(F32), axis=1
    ).astype(BF16)
    tiles = jnp.concatenate([label_tiles, oth_tiles], axis=0)
    tiles_top = round_bf16(tiles)
    tiles_hi, tiles_lo = tiles_top.astype(BF16), (tiles - tiles_top).astype(BF16)
    label_ids = (jnp.repeat(cluster_ids, LPC) * LPC + jnp.arange(512) % LPC).astype(jnp.int32)
    share_hit = pl.pallas_call(
        hit_kernel,
        out_shape=shape((128, 512), F32),
        in_specs=[WHOLE, WHOLE],
        out_specs=WHOLE,
        compiler_params=LIMIT,
        cost_estimate=cost(2**18, 2**18),
    )(posit, label_ids[None, :])
    hit = share_hit.astype(BF16)
    pos_part = jnp.dot(hit, tiles_hi, preferred_element_type=F32) + jnp.dot(
        hit, tiles_lo, preferred_element_type=F32
    )
    pos_part = (pos_part * POS_SCALE).astype(jnp.float16)
    weights, cluster_live, share_hit, pos_part, tiles_hi, tiles_lo = lax.optimization_barrier(
        (weights, cluster_live, share_hit, pos_part, tiles_hi, tiles_lo)
    )

    near_a, near_b, near_hidden, near_slope = forward(diag_tok, near_tok, weights, 2**30)
    near_sum = (near_b + swap_core(near_a).astype(F32)).astype(BF16)
    near_sum, pos_part = lax.optimization_barrier((near_sum, pos_part))
    from_near = swap_near(near_sum)
    pos_got = gather_chips(pos_part.reshape(16, docs, width))
    own_a, own_b, own_hidden, own_slope = forward(core_tok, own_tok, weights, 2**36)
    from_near, pos_got = lax.optimization_barrier((from_near, pos_got))
    pos_mean = jnp.sum(pos_got.astype(F32), axis=0) * (1.0 / POS_SCALE)
    own_rows, emb = pl.pallas_call(
        norm_kernel,
        out_shape=(shape((256, 1152), BF16), shape((128, width), BF16)),
        in_specs=[SCALARS] + [WHOLE] * 5,
        out_specs=(WHOLE, ANYWHERE),
        scratch_shapes=[pltpu.VMEM((128, width), BF16), pltpu.SemaphoreType.DMA],
        compiler_params=LIMIT,
        cost_estimate=cost(2**22, 4 * 2**20),
    )(lengths, own_tok, own_b, swap_core(own_a), from_near, gain)

    plane_emb = gather_chips(emb.reshape(16, docs, width)).reshape(128, width)
    near_rows = swap_near(own_rows)
    packed, weighted = pl.pallas_call(
        score_kernel,
        out_shape=(shape((128, 1280), BF16), shape((128, 512), F32)),
        in_specs=[ANYWHERE] + [WHOLE] * 3,
        out_specs=(ANYWHERE, WHOLE),
        scratch_shapes=[
            pltpu.VMEM((128, width), BF16),
            pltpu.VMEM((128, 1280), BF16),
            pltpu.SemaphoreType.DMA,
        ],
        compiler_params=LIMIT,
        cost_estimate=cost(2**29, 3 * 2**20, 2**16),
    )(plane_emb, tiles_hi, tiles_lo, cluster_live)
    packed, near_rows = lax.optimization_barrier((packed, near_rows))
    core_rows, diag_rows = swap_core(own_rows), swap_core(near_rows)
    got = lax.all_to_all(packed.reshape(16, docs, 1280), CHIPS, 0, 0, tiled=True)
    emb_grad, loss, sums = pl.pallas_call(
        settle_kernel,
        out_shape=(shape((docs, width), F32), shape((docs, 128), F32), shape((docs, 128), F32)),
        in_specs=[SCALARS, ANYWHERE, WHOLE, WHOLE],
        out_specs=(WHOLE,) * 3,
        scratch_shapes=[
            pltpu.VMEM((16, docs, 1280), BF16),
            pltpu.SemaphoreType.DMA,
        ],
        compiler_params=LIMIT,
        cost_estimate=cost(2**20, 2**20),
    )(meta, got, pos_mean, emb)
    loss = loss[:, 0]

    grads = (swap_diag(emb_grad), swap_near(emb_grad), swap_core(emb_grad), emb_grad)
    send, tile_own, tile_other = backward(
        grads,
        gain,
        sums,
        (diag_rows, near_rows, core_rows, own_rows),
        (diag_tok, near_tok, core_tok, own_tok),
        (near_hidden, own_hidden),
        (near_slope, own_slope),
        weights,
        (weighted, share_hit, plane_emb),
    )
    got = lax.all_to_all(send, CHIPS, 0, 0, tiled=True)
    part, keep, give = pl.pallas_call(
        total_kernel,
        out_shape=(shape((32, width), BF16), shape((32, 512), BF16), shape((32, 512), BF16)),
        grid=(4,),
        in_specs=[SCALARS, pl.BlockSpec((16, 16, width), lambda i: (0, i, 0))],
        out_specs=(
            pl.BlockSpec((16, width), lambda i: (jnp.minimum(i, 1), 0)),
            pl.BlockSpec((16, 512), lambda i: (jnp.maximum(i - 2, 0), 0)),
            pl.BlockSpec((16, 512), lambda i: (jnp.maximum(i - 2, 0), 0)),
        ),
        compiler_params=LIMIT,
        cost_estimate=cost(2**20, 2**21),
    )(meta, got)
    both = jnp.concatenate([part, jnp.concatenate([keep, swap_core(give)], axis=1)], axis=0)
    grad_in, grad_out = pl.pallas_call(
        place_kernel,
        out_shape=(shape((32, 2048), F32), shape((64, width), F32)),
        in_specs=[SCALARS] + [WHOLE] * 4,
        out_specs=(WHOLE, WHOLE),
        compiler_params=LIMIT,
        cost_estimate=cost(2**26, 2**20),
    )(meta, both, swap_near(both), swap_wrap(both), swap_far(both))

    tile_chip = (tile_own + swap_core(tile_other).astype(F32)).astype(BF16)

    def add(a, swap):
        return a.astype(F32) + swap(a).astype(F32)

    tile_grad = jnp.concatenate(
        [
            add(add(tile_chip[:128], swap_near).astype(BF16), swap_wrap),
            add(add(tile_chip[128:], swap_wrap).astype(BF16), swap_near),
        ],
        axis=0,
    )
    new_mean = 0.9 * tile_mean + 0.1 * tile_grad
    new_var = 0.999 * tile_var + 0.001 * tile_grad * tile_grad
    new_tiles = label_tiles - 0.001 * (new_mean * CORR_ONE) / (jnp.sqrt(new_var * CORR_TWO) + 1e-08)
    return (loss, new_tiles, new_mean, new_var, grad_in, grad_out)


def solution(mesh):
    grid = Mesh(mesh.devices.reshape(2, 2, 4, 4, 2), ("h", "l", "x", "z", "c"))
    every, plane, group = ("h", "l", "x", "z", "c"), ("x", "z", "c"), ("h", "l")
    return jax.shard_map(
        on_device,
        mesh=grid,
        in_specs=(
            P(every, None, None),
            P(every),
            P(plane, None),
            P(plane, None),
            P(),
            P(plane, None),
            P(plane, None),
            P(plane, None),
            P(group, None),
            P(group, None),
            P(),
        ),
        out_specs=(
            P(every),
            P(plane, None),
            P(plane, None),
            P(plane, None),
            P(plane, None),
            P(plane, None),
        ),
        check_vma=False,
    )
```
